32 devices in a mesh: grp: 2 (over y), view: 4 (over z), slab: 2 (over x), chan: 2 (over core).
Axes of the slice: x: 2, y: 2, z: 4, core: 2. Of those that a mesh axis runs over, the one named last changes fastest.
Arguments:
- volume: bfloat16 [32, 8, 1024], P('grp', ('view', 'slab')), parts along dimension 0, may hold values from -6 to 6
- dual_state: bfloat16 [8, 16, 512], P(('grp', 'view'), 'chan', 'slab'), parts along dimension 0, may hold values from -6 to 6
- measured: bfloat16 [8, 16, 512], P(('grp', 'view'), 'chan', 'slab'), parts along dimension 0, may hold values from -6 to 6
- cotangent: bfloat16 [32, 8, 1024], P('grp', ('view', 'slab')), parts along dimension 0, may hold values from -0.125 to 0.125
- conv_first: bfloat16 [16, 2, 3, 3, 3], P('chan'), may hold values from -0.875 to 0.875
- conv_middle: bfloat16 [16, 16, 3, 3, 3], P('chan'), may hold values from -0.3125 to 0.3125
- conv_last: bfloat16 [1, 16, 3, 3, 3], P(None, 'chan'), may hold values from -0.3125 to 0.3125
- dual_mixing: float32 [16, 3], replicated, may hold values from -3.5 to 3.5
- dual_readout: float32 [16], replicated, may hold values from -1.5 to 1.5
- footprints: bfloat16 [64, 128, 128], replicated, may hold values from -0.1875 to 0.1875
- tile_rows: int32 [4, 4, 8, 1], replicated, may hold values from 0 to 7
- tile_blocks: int32 [4, 4, 8, 1], replicated, may hold values from 0 to 63
Outputs:
- new_volume: float32 [32, 8, 1024], P('grp', ('view', 'slab')), parts along dimension 0
- new_dual: float32 [8, 16, 512], P(('grp', 'view'), 'chan', 'slab'), parts along dimension 0
- grad_first: float32 [32, 2, 3, 3, 3], P(('grp', 'chan')), parts along dimension 0
- grad_middle: float32 [32, 16, 3, 3, 3], P(('grp', 'chan')), parts along dimension 0
- grad_last: float32 [2, 16, 3, 3, 3], P('grp', 'chan'), parts along dimension 0
- grad_mixing: float32 [32, 3], P('grp'), parts along dimension 0
- grad_readout: float32 [32], P('grp'), parts along dimension 0
The draws below stay inside these ranges and needn't reach their ends.
There are 2 independent parts, one for each index of `grp`. The reference program is written for one: setup_inputs(seed, part) draws one part's arguments, and reference() takes and returns one part's arrays. A program takes and returns all parts, laid end to end along the dimension named above; an argument that names none is the same for every part. Nothing has to cross between parts.
All inputs are finite; a program needn't handle non-finite values.
Results may differ from the reference program's by a relative error of at most 0.0098.
Values may be sent and summed in bfloat16 or wider, within the bound.
No kernel may reach another device: no remote copies, remote signals or barrier semaphores. Data moves between devices by JAX's collectives and lax.ppermute only.
A program may use at most 64 MiB of HBM per device.

```python
import jax
import jax.numpy as jnp
from jax import lax

NZ = 16
YD = 1
TILE = 128
XT = 8
KO = 1
NB = 64
HID = 16
NX = 1024
VIEWS = 4
DTILES = 4
OWNERS = 8
NY = 8
DCOLS = 512


def plant(entries, rng, low, high):
    place = [jax.random.randint(jax.random.fold_in(rng, axis), (), 0, length) for axis, length in enumerate(entries.shape)]
    main_axis = entries.shape.index(max(entries.shape))
    next_to = place[:main_axis] + [(place[main_axis] + 1) % entries.shape[main_axis]] + place[main_axis + 1:]
    return entries.at[tuple(place)].set(low).at[tuple(next_to)].set(high)


def block_levels(rng, shape, shards, smallest, top_value):
    def one(position, blocks):
        steps = jax.random.uniform(jax.random.fold_in(jax.random.fold_in(rng, 6), position), (blocks,), jnp.float32, smallest / len(shards), top_value / len(shards))
        return jnp.repeat(jnp.exp(steps), shape[position] // blocks).reshape((-1,) + (1,) * (len(shape) - position - 1))

    factor_of = one(*shards[0])
    for cut in shards[1:]:
        factor_of = factor_of * one(*cut)
    return factor_of


def noise(stream_key, extent, deviation, limit, split=(), kind=jnp.bfloat16):
    values = jax.random.normal(stream_key, extent, jnp.float32) * deviation
    if len(split) > 0:
        values = block_levels(stream_key, extent, split, -0.22, 0.18) * values
    return jnp.clip(values, min=-limit, max=limit).astype(kind)


def setup_inputs(seed: int = 0, part: int = 0) -> dict:
    splits = jax.random.split(jax.random.key(seed), 13)
    own_keys = jax.random.split(jax.random.fold_in(splits[12], part), 13)
    return {
        "volume": noise(own_keys[0], (NZ, NY, NX), 1.0, 6.0, ((1, 8),)),
        "dual_state": noise(own_keys[1], (VIEWS, NZ, DCOLS), 1.0, 6.0, ((0, 4), (1, 2), (2, 2))),
        "measured": noise(own_keys[2], (VIEWS, NZ, DCOLS), 1.0, 6.0, ((0, 4), (1, 2), (2, 2))),
        "cotangent": noise(own_keys[3], (NZ, NY, NX), (8.0 / (NZ * NY * NX) ** 0.5), 0.125, ((1, 8),)),
        "conv_first": noise(splits[4], (HID, 2, 3, 3, 3), 54 ** -0.5, 0.875, ((0, 2),)),
        "conv_middle": noise(splits[5], (HID, HID, 3, 3, 3), (27 * HID) ** -0.5, 0.3125, ((0, 2),)),
        "conv_last": noise(splits[6], (1, HID, 3, 3, 3), (27 * HID) ** -0.5, 0.3125, ((1, 2),)),
        "dual_mixing": noise(splits[7], (HID, 3), 3 ** -0.5, 3.5, (), jnp.float32),
        "dual_readout": noise(splits[8], (HID,), HID ** -0.5, 1.5, (), jnp.float32),
        "footprints": noise(splits[9], (NB, TILE, TILE), (TILE * KO * OWNERS) ** -0.5, 0.1875),
        "tile_rows": plant(jax.random.randint(splits[10], (VIEWS, DTILES, OWNERS, KO), 0, YD * XT), jax.random.fold_in(splits[10], 1), 0, (YD * XT) - 1).astype(jnp.int32),
        "tile_blocks": plant(jax.random.randint(splits[11], (VIEWS, DTILES, OWNERS, KO), 0, NB), jax.random.fold_in(splits[11], 1), 0, NB - 1).astype(jnp.int32),
    }


HIGHEST = lax.Precision.HIGHEST

def silu_slope(pre_value):
    sigmoid_of = jax.nn.sigmoid(pre_value)
    return sigmoid_of * (1.0 + pre_value * (1.0 - sigmoid_of))

def conv_same(weight, field):
    result = lax.conv_general_dilated(field.astype(jnp.float32)[None], weight.astype(jnp.float32), (1, 1, 1), ((1, 1), (1, 1), (1, 1)), dimension_numbers=('NCDHW', 'OIDHW', 'NCDHW'), precision=HIGHEST)
    return result[0]

def conv_adjoint(weight, cotangent):
    flipped = jnp.flip(weight, axis=(2, 3, 4)).transpose(1, 0, 2, 3, 4)
    return conv_same(flipped, cotangent)

def weight_grad(cotangent, field):
    padded = jnp.pad(field.astype(jnp.float32), ((0, 0), (1, 1), (1, 1), (1, 1)))
    cot_float = cotangent.astype(jnp.float32)
    slices, height, breadth = cot_float.shape[1:]
    term_list = []
    for shift_depth in range(3):
        for shift_row in range(3):
            for shift_col in range(3):
                window = padded[:, shift_depth:shift_depth + slices, shift_row:shift_row + height, shift_col:shift_col + breadth]
                term_list.append(jnp.einsum('ozyx,izyx->oi', cot_float, window, precision=HIGHEST))
    stacked = jnp.stack(term_list, axis=-1)
    return stacked.reshape(stacked.shape[0], stacked.shape[1], 3, 3, 3)

def global_rows(tile_rows):
    offsets = (jnp.arange(OWNERS, dtype=jnp.int32) * (YD * XT))[:, None]
    return (tile_rows + offsets).astype(jnp.int32).reshape(VIEWS * DTILES, OWNERS * KO)

def project(field, tile_rows, tile_blocks, footprints):
    row_tiles = jnp.transpose(field.reshape(NZ, NY * XT, TILE), (1, 0, 2))
    row_index = global_rows(tile_rows)
    block_index = tile_blocks.reshape(VIEWS * DTILES, OWNERS * KO)
    float_blocks = footprints.astype(jnp.float32)

    def one_tile(pair):
        picked = jnp.take(row_tiles, pair[0], axis=0).astype(jnp.float32)
        matrices = jnp.take(float_blocks, pair[1], axis=0)
        return jnp.einsum('ezx,exc->zc', picked, matrices, precision=HIGHEST)
    result = lax.map(one_tile, (row_index, block_index))
    result = result.reshape(VIEWS, DTILES, NZ, TILE)
    return jnp.transpose(result, (0, 2, 1, 3)).reshape(VIEWS, NZ, DTILES * TILE)

def backproject(sinogram, tile_rows, tile_blocks, footprints):
    tiles_all = jnp.transpose(sinogram.reshape(VIEWS, NZ, DTILES, TILE), (0, 2, 1, 3)).reshape(VIEWS * DTILES, NZ, TILE)
    row_index = global_rows(tile_rows)
    block_index = tile_blocks.reshape(VIEWS * DTILES, OWNERS * KO)
    float_blocks = footprints.astype(jnp.float32)

    def add_tile(running, triple):
        matrices = jnp.take(float_blocks, triple[2], axis=0)
        products = jnp.einsum('zc,exc->ezx', triple[0].astype(jnp.float32), matrices, precision=HIGHEST)
        return (running.at[triple[1]].add(products), None)
    initial = jnp.zeros((NY * XT, NZ, TILE), jnp.float32)
    running, unused = lax.scan(add_tile, initial, (tiles_all, row_index, block_index))
    return jnp.transpose(running, (1, 0, 2)).reshape(NZ, NY, NX)

def reference(volume, dual_state, measured, cotangent, conv_first, conv_middle, conv_last, dual_mixing, dual_readout, footprints, tile_rows, tile_blocks):
    projected = project(volume, tile_rows, tile_blocks, footprints)
    stacked_in = jnp.stack([dual_state.astype(jnp.float32), projected, measured.astype(jnp.float32)])
    mixed_pre = jnp.einsum('mc,cvzx->mvzx', dual_mixing, stacked_in, precision=HIGHEST)
    active = jax.nn.silu(mixed_pre)
    new_dual = dual_state.astype(jnp.float32) + jnp.einsum('m,mvzx->vzx', dual_readout, active, precision=HIGHEST)
    dual_half = lax.optimization_barrier(new_dual.astype(jnp.bfloat16))
    back_full = lax.optimization_barrier(backproject(dual_half, tile_rows, tile_blocks, footprints).astype(jnp.bfloat16))
    conv_inputs = jnp.stack([volume, back_full])
    first_pre = conv_same(conv_first, conv_inputs)
    first_act = lax.optimization_barrier(jax.nn.silu(first_pre).astype(jnp.bfloat16))
    middle_pre = conv_same(conv_middle, first_act)
    middle_act = lax.optimization_barrier(jax.nn.silu(middle_pre).astype(jnp.bfloat16))
    new_volume = volume.astype(jnp.float32) + conv_same(conv_last, middle_act)[0]
    seed_grad = cotangent[None]
    grad_last = weight_grad(seed_grad, middle_act)
    middle_grad = lax.optimization_barrier((conv_adjoint(conv_last, seed_grad) * silu_slope(middle_pre)).astype(jnp.bfloat16))
    grad_middle = weight_grad(middle_grad, first_act)
    first_grad = lax.optimization_barrier((conv_adjoint(conv_middle, middle_grad) * silu_slope(first_pre)).astype(jnp.bfloat16))
    grad_first = weight_grad(first_grad, conv_inputs)
    back_grad = lax.optimization_barrier(conv_adjoint(conv_first[:, 1:2], first_grad)[0].astype(jnp.bfloat16))
    dual_grad = project(back_grad, tile_rows, tile_blocks, footprints)
    grad_readout = jnp.einsum('vzx,mvzx->m', dual_grad, active, precision=HIGHEST)
    mixed_grad = dual_grad[None] * dual_readout[:, None, None, None] * silu_slope(mixed_pre)
    grad_mixing = jnp.einsum('mvzx,cvzx->mc', mixed_grad, stacked_in, precision=HIGHEST)
    return (new_volume, new_dual, grad_first, grad_middle, grad_last, grad_mixing, grad_readout)
```

```python
import functools

import jax
import jax.numpy as jnp
from jax import lax
from jax.experimental import pallas as pl
from jax.experimental.pallas import tpu as pltpu
from jax.sharding import PartitionSpec as P

F32 = jnp.float32
BF16 = jnp.bfloat16
ALL_AXES = ("view", "slab", "chan")
ROW_AXES = ("view", "slab")
HID = 16
TILE = 128
REACH = 4
TAPS = 9
NN = (((1,), (0,)), ((), ()))
NT = (((1,), (1,)), ((), ()))
TN = (((0,), (0,)), ((), ()))
VMEM_LIMIT = 56 * 1024 * 1024


def dot(left, right, dims=NN, precision=None):
    return lax.dot_general(left, right, dims, precision=precision, preferred_element_type=F32)


def iota(shape, dim):
    return lax.broadcasted_iota(jnp.int32, shape, dim)


def repeat(count, step, limit=16):
    if count <= limit:
        for index in range(count):
            step(index)
    else:

        @pl.loop(0, count)
        def unused(index):
            step(index)


def weights_kernel(base, middle, first, last):
    wide = HID * HID
    spread = ((iota((HID, wide), 1) & (HID - 1)) == iota((HID, wide), 0)).astype(BF16)
    values = dot(base[...], spread)
    lane_z = iota((HID, wide), 1) >> 4
    row_z = iota((HID, wide), 0)

    def part(depth, tap, start, count):
        begin = (depth * TAPS + tap) * 2 * HID + start
        return values[begin : begin + count]

    for z in range(HID):
        below, level, above = (lane_z == z + 1, lane_z == z, lane_z == z - 1)
        for tap in range(TAPS):
            block = jnp.where(
                below,
                part(0, tap, 0, HID),
                jnp.where(
                    level,
                    part(1, tap, 0, HID),
                    jnp.where(above, part(2, tap, 0, HID), 0.0),
                ),
            )
            begin = (tap % 3) * wide + z * HID
            middle[tap // 3, begin : begin + HID, :] = block.astype(BF16)

    def banded(tap, row, step):
        out = jnp.zeros((HID, wide), F32)
        for depth in range(3):
            line = jnp.broadcast_to(part(depth, tap, row, 1), (HID, wide))
            out = jnp.where(row_z - lane_z == step * (depth - 1), line, out)
        return out.astype(BF16)

    for tap in range(TAPS):
        for channel in range(2):
            begin = (channel * TAPS + tap) * HID
            first[begin : begin + HID, :] = banded(tap, HID + channel, 1)
        last[tap * HID : (tap + 1) * HID, :] = banded(tap, HID + 2, -1)


def build_weights(conv_first, conv_middle, conv_last):
    own = jnp.concatenate(
        [
            conv_middle.reshape(conv_middle.shape[0], HID, 27),
            conv_first.reshape(conv_first.shape[0], 2, 27),
            jnp.swapaxes(conv_last.reshape(1, -1, 27), 0, 1),
        ],
        axis=1,
    )
    other = lax.ppermute(own, "chan", [(0, 1), (1, 0)])
    is_low = lax.axis_index("chan") == 0
    full = jnp.concatenate([jnp.where(is_low, own, other), jnp.where(is_low, other, own)], axis=0)
    base = jnp.pad(full.transpose(2, 1, 0), ((0, 0), (0, 2 * HID - 19), (0, 0)))
    wide = HID * HID
    return pl.pallas_call(
        weights_kernel,
        out_shape=(
            jax.ShapeDtypeStruct((3, 3 * wide, wide), BF16),
            jax.ShapeDtypeStruct((2 * TAPS * HID, wide), BF16),
            jax.ShapeDtypeStruct((TAPS * HID, wide), BF16),
        ),
        cost_estimate=pl.CostEstimate(flops=10**8, bytes_accessed=2 * 10**6, transcendentals=0),
        name="band_weights",
    )(base.reshape(27 * 2 * HID, HID))


def sigmoid(value):
    return jax.nn.sigmoid(value)


def projector(sizes, table, footprints):
    rows_count, detectors = (sizes[0], sizes[2])
    entries = rows_count
    groups = rows_count // 8

    def tile_of(tile, owner):
        return table[tile * entries + owner]

    def block_of(tile, owner):
        return footprints[table[(detectors + tile) * entries + owner]]

    def project(tile, pick):
        def one(group):
            owners = [group * 8 + o for o in range(8)]
            left = jnp.concatenate([pick(tile, o) for o in owners], axis=1)
            right = jnp.concatenate([block_of(tile, o) for o in owners], axis=0)
            return dot(left, right)

        if groups == 1:
            return one(0)
        return lax.fori_loop(0, groups, lambda g, a: a + one(g), jnp.zeros((16, TILE), F32))

    return tile_of, block_of, project


def dual_reader(scalars, proj, dual, meas):
    batch = 4

    def mixed_of(m, parts):
        return scalars[3 * m] * parts[0] + scalars[3 * m + 1] * parts[1] + scalars[3 * m + 2] * parts[2]

    def stack_of(chunk):
        span = pl.ds(chunk * batch, batch)
        return span, (dual[span], proj[span], meas[span])

    return batch, mixed_of, stack_of


def dual_gradients(sizes, table, scalars, footprints, proj, dual, meas, grad_tiles, grad, sums):
    rows_count, chans, detectors, tiles, width = sizes[:5]
    low = (table[2 * detectors * rows_count] * chans + table[2 * detectors * rows_count + 1]) * width
    tile_of, _, project = projector(sizes, table, footprints)
    batch, mixed_of, stack_of = dual_reader(scalars, proj, dual, meas)

    def project_grad(tile):
        def pick(t, o):
            return grad_tiles[o, (tile_of(t, o) == lax.div(low, TILE)).astype(jnp.int32)]

        grad[tile] = project(tile, pick)

    repeat(detectors, project_grad)
    sums[...] = jnp.zeros_like(sums)

    def dual_sums(chunk):
        span, parts = stack_of(chunk)
        pulled_in = grad[span]
        for m in range(HID):
            mixed = mixed_of(m, parts)
            gate = sigmoid(mixed)
            slope = gate * (1.0 + mixed * (1.0 - gate))
            pulled = pulled_in * slope * scalars[3 * HID + m]
            terms = [pulled_in * (mixed * gate)] + [pulled * part for part in parts]
            for k, term in enumerate(terms):
                sums[k, m] += jnp.sum(term.reshape(batch * 2, 8, TILE), axis=0)

    repeat(detectors // batch, dual_sums)
    lane_out = iota((HID, TILE), 1)
    small = jnp.zeros((HID, TILE), F32)
    for k in range(4):
        column = jnp.sum(jnp.sum(sums[k], axis=1), axis=1, keepdims=True)
        small = jnp.where(lane_out == k, column, small)
    return small


def dual_gradients_kernel(sizes, table, scalars, footprints, proj, dual, meas, grad_tiles, out,
                          grad, sums):
    out[...] = dual_gradients(
        sizes, table, scalars, footprints, proj, dual, meas, grad_tiles, grad, sums
    )


def main_kernel(sizes, whole, table, scalars, payload, footprints, middle, first, last,
                keep, send, dual_out, proj, dual, meas, grad_tiles,
                vol, cot, dual_half, dual_new, back, field, col_in, col_cot,
                act_wide, grad_wide, slope_first, slope_middle, row_tiles, sums):
    rows_count, chans, detectors, tiles, width, stride, cells, piece_slot, update_row = sizes
    near = tiles // chans
    entries = rows_count
    row = table[2 * detectors * entries]
    chan = table[2 * detectors * entries + 1]
    low = (row * chans + chan) * width
    count = rows_count * stride
    lanes = count + TILE

    def place(device):
        owner, part = (device // chans, device % chans)
        slot = piece_slot(owner, part, row, chan)
        for k in range(near):
            vol[owner * tiles + part * near + k] = payload[slot, k]
            cot[owner * tiles + part * near + k] = payload[slot, near + k]
        for k, target in ((2 * near, dual), (2 * near + 1, meas)):
            piece = payload[slot, k].astype(F32)
            for t in range(2):
                target[owner * 2 + t, pl.ds(pl.multiple_of(part * 8, 8), 8), :] = piece[
                    t * 8 : (t + 1) * 8
                ]

    repeat(rows_count * chans, place)

    tile_of, block_of, project = projector(sizes, table, footprints)

    def project_volume(tile):
        proj[tile] = project(tile, lambda t, o: vol[o * tiles + tile_of(t, o)])

    repeat(detectors, project_volume)

    batch, mixed_of, stack_of = dual_reader(scalars, proj, dual, meas)

    def dual_block(chunk):
        span, parts = stack_of(chunk)
        total = parts[0]
        for m in range(HID):
            mixed = mixed_of(m, parts)
            total = total + scalars[3 * HID + m] * (mixed * sigmoid(mixed))
        dual_new[span] = total
        dual_half[span] = total.astype(BF16)

    repeat(detectors // batch, dual_block)
    for t in range(2):
        dual_out[:, t * TILE : (t + 1) * TILE] = dual_new[
            row * 2 + t, pl.ds(pl.multiple_of(chan * 8, 8), 8), :
        ]

    window = width + 2 * REACH
    tile_low = lax.div(low - REACH + TILE, TILE) - 1
    offset = low - REACH - tile_low * TILE

    def backproject(group):
        owners = [group * 8 + o for o in range(8)]

        def add(tile, totals):
            right = jnp.concatenate([block_of(tile, o) for o in owners], axis=0)
            products = dot(dual_half[tile], right, NT)
            out = []
            for o in range(8):
                place_of = tile_of(tile, owners[o]) - tile_low
                product = products[:, o * TILE : (o + 1) * TILE]
                for side in range(2):
                    out.append(totals[2 * o + side] + jnp.where(place_of == side, product, 0.0))
            return tuple(out)

        totals = tuple(jnp.zeros((16, TILE), F32) for _ in range(16))
        if detectors <= 16:
            for tile in range(detectors):
                totals = add(tile, totals)
        else:
            totals = lax.fori_loop(0, detectors, add, totals)
        for o in range(8):
            for side in range(2):
                back[owners[o], side] = totals[2 * o + side]

    repeat(rows_count // 8, backproject)

    lane = iota((3 * 16, TILE), 1)
    clip_low = jnp.clip(tile_low, 0, tiles - 1)
    clip_high = jnp.clip(tile_low + 1, 0, tiles - 1)
    pieces = [None] * (lanes // TILE)
    for y in range(rows_count):
        sides = []
        for side, clipped in ((0, clip_low), (1, clip_high)):
            sides.append(
                jnp.concatenate(
                    [
                        vol[y * tiles + clipped].astype(F32),
                        back[y, side].astype(BF16).astype(F32),
                        cot[y * tiles + clipped].astype(F32),
                    ],
                    axis=0,
                )
            )
        merged = jnp.where(lane >= offset, sides[0], sides[1])
        shift = lax.rem(y * stride - offset + TILE * (count // TILE + 1), TILE)
        merged = pltpu.roll(merged, shift, 1)
        for t in range(y * stride // TILE, (y * stride + window - 1) // TILE + 1):
            column = lane + (t * TILE - y * stride)
            cell = column + (low - REACH)
            inside = (column >= 0) & (column < window) & (cell >= 0) & (cell < cells)
            taken = jnp.where(inside, merged, 0.0)
            pieces[t] = taken if pieces[t] is None else pieces[t] + taken
    for t in range(lanes // TILE):
        field[:, t * TILE : (t + 1) * TILE] = (
            jnp.zeros((3 * 16, TILE), F32) if pieces[t] is None else pieces[t]
        )

    def shift_of(tap):
        return stride * (tap // 3 - 1) + (tap % 3 - 1)

    def rolled(value, amount):
        amount = amount % lanes
        return value if amount == 0 else pltpu.roll(value, amount, 1)

    for tap in range(TAPS):
        for channel in range(2):
            begin = (channel * TAPS + tap) * HID
            part = rolled(field[channel * 16 : (channel + 1) * 16, :], -shift_of(tap))
            col_in[begin : begin + HID, :] = part[:, :count].astype(BF16)
        part = rolled(field[32:48, :], shift_of(tap))
        col_cot[tap * HID : (tap + 1) * HID, :] = part[:, :count].astype(BF16)

    wide = HID * HID
    place_x = iota((stride, wide), 0)
    cell_x = place_x + (low - REACH)
    valid = (cell_x >= 0) & (cell_x < cells)
    own = (place_x >= REACH) & (place_x < REACH + width)

    def masked(mask, value):
        shaped = value.reshape(rows_count, stride, wide)
        return jnp.where(mask[None], shaped, 0.0).reshape(count, wide)

    def widen(target, value, step):
        zero = jnp.zeros((stride, 3 * wide), BF16)
        target[0:stride, :] = zero
        target[stride + count :, :] = zero
        for k, amount in ((0, step), (1, 0), (2, -step)):
            moved = value if amount == 0 else pltpu.roll(value, amount % count, 0)
            target[stride : stride + count, k * wide : (k + 1) * wide] = moved.astype(BF16)

    first_pre = dot(col_in[...], first[...], TN)
    gate = sigmoid(first_pre)
    slope_first[...] = gate * (1.0 + first_pre * (1.0 - gate))
    widen(act_wide, masked(valid, first_pre * gate), 1)
    middle_pre = None
    for dy in range(3):
        part = dot(act_wide[stride * dy : stride * dy + count, :], middle[dy])
        middle_pre = part if middle_pre is None else middle_pre + part
    gate = sigmoid(middle_pre)
    slope_middle[...] = gate * (1.0 + middle_pre * (1.0 - gate))
    middle_act = masked(valid, middle_pre * gate)
    middle_half = middle_act.astype(BF16)

    def gather_taps(products, sign):
        padded = jnp.concatenate([products, jnp.zeros((TAPS * HID, TILE), F32)], axis=1)
        total = None
        for tap in range(TAPS):
            part = rolled(padded[tap * HID : (tap + 1) * HID], sign * shift_of(tap))
            total = part if total is None else total + part
        return total

    def rows_to_tiles(value, target):
        lane_one = iota((16, TILE), 1)
        for y in range(rows_count):
            begin = y * stride + REACH
            merged = None
            for t in range(begin // TILE, (begin + width - 1) // TILE + 1):
                column = lane_one + t * TILE
                inside = (column >= begin) & (column < begin + width)
                part = jnp.where(inside, value[:, t * TILE : (t + 1) * TILE], 0.0)
                merged = part if merged is None else merged + part
            shift = lax.rem(low - begin + TILE * (count // TILE + 1), TILE)
            target(y, pltpu.roll(merged, shift, 1))

    update = gather_taps(dot(last[...], middle_half, NT), -1) + field[0:16, :]

    def put_row(y, tile):
        row_tiles[y] = tile

    rows_to_tiles(update, put_row)

    middle_grad = masked(valid, dot(col_cot[...], last[...], TN) * slope_middle[...])
    grad_last = dot(col_cot[...], masked(own, middle_act).astype(BF16))
    widen(grad_wide, middle_grad, -1)
    turned = jnp.transpose(masked(own, middle_grad)).astype(BF16)
    grads_middle = [
        dot(turned, act_wide[stride * dy : stride * dy + count, :]) for dy in range(3)
    ]
    first_sum = None
    for dy in range(3):
        for dx in range(3):
            part = dot(
                grad_wide[stride * (2 - dy) : stride * (2 - dy) + count, dx * wide : (dx + 1) * wide],
                middle[dy, dx * wide : (dx + 1) * wide, :],
                NT,
            )
            first_sum = part if first_sum is None else first_sum + part
    first_grad = masked(valid, first_sum * slope_first[...])
    first_half = first_grad.astype(BF16)
    turned = jnp.transpose(masked(own, first_grad)).astype(BF16)
    grad_first = dot(turned, col_in[...], NT)
    back_grad = gather_taps(dot(first[TAPS * HID :, :], first_half, NT), 1)

    def put_grad(y, tile):
        grad_tiles[y, 0] = jnp.zeros((16, TILE), BF16)
        grad_tiles[y, 1] = tile.astype(BF16)

    rows_to_tiles(back_grad, put_grad)

    lane_z = iota((HID, wide), 1) >> 4
    lane_group = iota((HID, TILE), 1) >> 4
    out_tiles = [jnp.zeros((HID, TILE), F32) for _ in range(5)]

    def fold_lanes(value):
        value = value[:, :TILE] + value[:, TILE:]
        for amount in (64, 32, 16):
            value = value + pltpu.roll(value, amount, 1)
        return value

    def put(index, value):
        group = index // 8
        out_tiles[group] = jnp.where(lane_group == index % 8, value, out_tiles[group])

    for tap in range(TAPS):
        plane = grads_middle[tap // 3][:, (tap % 3) * wide : (tap % 3 + 1) * wide]
        for depth in range(3):
            total = jnp.zeros((HID, wide), F32)
            for z in range(HID):
                total = total + jnp.where(lane_z == z + depth - 1, plane[z * HID : (z + 1) * HID], 0.0)
            put(depth * TAPS + tap, fold_lanes(total))

    lane_in = iota((HID, 2 * TAPS * HID), 1) & (HID - 1)
    folds = []
    for depth in range(3):
        total = jnp.zeros((HID, 2 * TAPS * HID), F32)
        for z in range(HID):
            total = total + jnp.where(lane_in == z + depth - 1, grad_first[z * HID : (z + 1) * HID], 0.0)
        folds.append(total)
    source = iota((2 * TAPS * HID, TILE), 0) >> 4
    target = iota((2 * TAPS * HID, TILE), 1)
    for depth in range(3):
        fold = (target == 48 + depth * 2 * TAPS + source).astype(F32)
        out_tiles[3] = out_tiles[3] + dot(folds[depth], fold, precision=lax.Precision.HIGHEST)

    row_z = iota((HID, wide), 0)
    lines = []
    for depth in range(3):
        keep_last = lane_z == row_z + depth - 1
        for tap in range(TAPS):
            part = jnp.where(keep_last, grad_last[tap * HID : (tap + 1) * HID], 0.0)
            lines.append(jnp.sum(part, axis=0, keepdims=True))
    lines.append(jnp.zeros((TILE - 27, wide), F32))
    out_tiles[4] = jnp.transpose(fold_lanes(jnp.concatenate(lines, axis=0)))[:HID]

    if whole:
        small = dual_gradients(
            sizes, table, scalars, footprints, proj, dual, meas, grad_tiles, dual_new, sums
        )
    else:
        small = jnp.zeros((HID, TILE), F32)

    for t in range(5):
        slope_first[0:HID, 0:TILE] = out_tiles[t]
        keep[t * 8 : (t + 1) * 8, :] = slope_first[pl.ds(pl.multiple_of(chan * 8, 8), 8), 0:TILE]
        send[t * 8 : (t + 1) * 8, :] = slope_first[
            pl.ds(pl.multiple_of((chans - 1 - chan) * 8, 8), 8), 0:TILE
        ]
    keep[40:56, :] = small
    send[40:56, :] = small

    def put_update(y):
        begin = pl.multiple_of(56 + y * 16, 8)
        tile = row_tiles[update_row(y, row)]
        keep[pl.ds(begin, 16), :] = tile
        send[pl.ds(begin, 16), :] = tile

    repeat(rows_count, put_update)


def finish_kernel(table, own, one, two, three, far, total, *rest):
    volume, grads, slots = rest
    row = table[0]
    grads[...] = total[...] + far[0:56, :]
    for k, (source, begin) in enumerate(
        ((own, 56), (one, 56), (two, 56), (three, 56), (far, 56), (far, 72), (far, 88), (far, 104))
    ):
        slots[k] = source[begin : begin + 16, :]
    for tile in range(8):
        volume[:, tile * TILE : (tile + 1) * TILE] = slots[tile ^ row]


def row_mask_pairs(devices, mask):
    return [(index, index ^ mask) for index in range(devices)]


def body(
    volume,
    dual_state,
    measured,
    cotangent,
    conv_first,
    conv_middle,
    conv_last,
    dual_mixing,
    dual_readout,
    footprints,
    tile_rows,
    tile_blocks,
):
    views, slabs, chans = (lax.axis_size(a) for a in ALL_AXES)
    rows_count = views * slabs
    devices = rows_count * chans
    cells = volume.shape[2]
    tiles = cells // TILE
    width = cells // devices
    stride = -(-(width + 2 * REACH) // 16) * 16
    detectors = tile_rows.shape[0] * tile_rows.shape[1]
    entries = tile_rows.shape[2]
    near = tiles // chans
    chan = lax.axis_index("chan")
    row = lax.axis_index("view") * slabs + lax.axis_index("slab")
    quick = rows_count == 8 and chans == 2

    def chan_half(value):
        shaped = jnp.swapaxes(value.reshape(16, tiles, TILE), 0, 1)
        return lax.dynamic_slice_in_dim(shaped, chan * near, near, 0)

    def dual_piece(value):
        return jnp.swapaxes(value.reshape(8, 2, TILE), 0, 1).reshape(1, 16, TILE)

    payload = jnp.concatenate(
        [chan_half(volume), chan_half(cotangent), dual_piece(dual_state), dual_piece(measured)],
        axis=0,
    )[None]

    def swap(value, mask):
        return lax.ppermute(value, ALL_AXES, row_mask_pairs(devices, mask))

    if quick:
        payload = jnp.concatenate([payload, swap(payload, 8)], axis=0)
        payload = jnp.concatenate([payload] + [swap(payload, k) for k in (2, 4, 6)], axis=0)
        payload = jnp.concatenate([payload, swap(payload, 1)], axis=0)
    else:
        payload = lax.all_gather(payload, ALL_AXES, axis=0, tiled=True)

    def piece_slot(owner, part, row, chan):
        if not quick:
            return owner * chans + part
        mask = owner ^ row
        return (mask & 3) * 2 + (mask >> 2) + rows_count * (part ^ chan)

    def update_row(owner, row):
        return owner ^ row if quick else owner

    middle, first, last = build_weights(conv_first, conv_middle, conv_last)
    table = jnp.concatenate(
        [
            tile_rows.reshape(-1),
            tile_blocks.reshape(-1),
            jnp.stack([row, chan]).astype(jnp.int32),
        ]
    )
    scalars = jnp.concatenate([dual_mixing.reshape(-1), dual_readout])
    count = rows_count * stride
    wide = HID * HID
    moved = 56 + 16 * rows_count
    vmem = pl.BlockSpec(memory_space=pltpu.VMEM)
    smem = pl.BlockSpec(memory_space=pltpu.SMEM)
    sizes = (rows_count, chans, detectors, tiles, width, stride, cells, piece_slot, update_row)
    outs = [
        ((moved, TILE), F32),
        ((moved, TILE), F32),
        ((8, 2 * TILE), F32),
    ]
    shared = [
        ((detectors, 16, TILE), F32),
        ((detectors, 16, TILE), F32),
        ((detectors, 16, TILE), F32),
        ((rows_count, 2, 16, TILE), BF16),
    ]
    scratch = [
        ((rows_count * tiles, 16, TILE), BF16),
        ((rows_count * tiles, 16, TILE), BF16),
        ((detectors, 16, TILE), BF16),
        ((detectors, 16, TILE), F32),
        ((rows_count, 2, 16, TILE), F32),
        ((48, count + TILE), F32),
        ((2 * TAPS * HID, count), BF16),
        ((TAPS * HID, count), BF16),
        ((count + 2 * stride, 3 * wide), BF16),
        ((count + 2 * stride, 3 * wide), BF16),
        ((count, wide), F32),
        ((count, wide), F32),
        ((rows_count, 16, TILE), F32),
        ((4, HID, 8, TILE), F32),
    ]
    if quick:
        scratch = shared + scratch
    else:
        outs = outs + shared
    keep, send, new_dual, *rest = pl.pallas_call(
        functools.partial(main_kernel, sizes, quick),
        out_shape=[jax.ShapeDtypeStruct(*spec) for spec in outs],
        in_specs=[smem, smem] + [vmem] * 5,
        out_specs=[vmem] * len(outs),
        scratch_shapes=[pltpu.VMEM(*spec) for spec in scratch],
        compiler_params=pltpu.CompilerParams(vmem_limit_bytes=VMEM_LIMIT),
        cost_estimate=pl.CostEstimate(
            flops=5 * 10**9, bytes_accessed=5 * 10**6, transcendentals=2 * 10**6
        ),
        name="primal_dual",
    )(table, scalars, payload, footprints, middle, first, last)

    mine = keep + swap(send, 1)
    if quick:

        def piece(value, index):
            return value[56 + 16 * index : 72 + 16 * index]

        parts = [
            swap(jnp.concatenate([mine[:56], piece(mine, k), piece(mine, k ^ 4)], axis=0), 2 * k)
            for k in (1, 2, 3)
        ]
        total = mine[:56] + parts[0][:56] + parts[1][:56] + parts[2][:56]
        far = swap(
            jnp.concatenate([total, piece(mine, 4)] + [piece(part, 1) for part in parts], axis=0), 8
        )
        new_volume, grads = pl.pallas_call(
            finish_kernel,
            out_shape=(
                jax.ShapeDtypeStruct((16, cells), F32),
                jax.ShapeDtypeStruct((56, TILE), F32),
            ),
            in_specs=[smem] + [vmem] * 6,
            out_specs=(vmem, vmem),
            scratch_shapes=[pltpu.VMEM((8, 16, TILE), F32)],
            name="finish",
        )(row.reshape(1).astype(jnp.int32), mine, *parts, far, total)
    else:
        small = pl.pallas_call(
            functools.partial(dual_gradients_kernel, sizes),
            out_shape=jax.ShapeDtypeStruct((HID, TILE), F32),
            in_specs=[smem, smem] + [vmem] * 5,
            out_specs=vmem,
            scratch_shapes=[
                pltpu.VMEM((detectors, 16, TILE), F32),
                pltpu.VMEM((4, HID, 8, TILE), F32),
            ],
            compiler_params=pltpu.CompilerParams(vmem_limit_bytes=VMEM_LIMIT),
            name="dual_gradients",
        )(table, scalars, footprints, *rest)
        grads = lax.psum(mine[:40], ROW_AXES)
        grads = jnp.concatenate([grads, lax.psum(small, ALL_AXES)], axis=0)
        pieces = lax.all_to_all(
            mine[56:].reshape(rows_count, 16, TILE), ROW_AXES, 0, 0, tiled=True
        )
        pieces = pieces.reshape(tiles, rows_count // tiles, 16, TILE).sum(axis=1)
        new_volume = jnp.swapaxes(pieces, 0, 1)

    kernels = jnp.swapaxes(grads[:40].reshape(5, 8, TILE), 0, 1).reshape(8, 5 * TILE)
    grad_middle = jnp.swapaxes(kernels[:, :432].reshape(8, 27, HID), 1, 2)
    grad_first = jnp.swapaxes(kernels[:, 432:486].reshape(8, 3, 2, TAPS), 1, 2)
    grad_last = kernels[:, 512:539]
    small = grads[40:56]
    return (
        new_volume.reshape(volume.shape),
        new_dual.reshape(dual_state.shape),
        grad_first.reshape(8, 2, 3, 3, 3),
        grad_middle.reshape(8, HID, 3, 3, 3),
        grad_last.reshape(1, 8, 3, 3, 3),
        small[:, 1:4],
        small[:, 0],
    )


def solution(mesh):
    placed = (
        P("grp", ("view", "slab"), None),
        P(("grp", "view"), "chan", "slab"),
        P(("grp", "view"), "chan", "slab"),
        P("grp", ("view", "slab"), None),
        P("chan", None, None, None, None),
        P("chan", None, None, None, None),
        P(None, "chan", None, None, None),
        P(),
        P(),
        P(),
        P(),
        P(),
    )
    return jax.shard_map(
        body,
        mesh=mesh,
        in_specs=placed,
        out_specs=(
            P("grp", ("view", "slab"), None),
            P(("grp", "view"), "chan", "slab"),
            P(("grp", "chan"), None, None, None, None),
            P(("grp", "chan"), None, None, None, None),
            P("grp", "chan", None, None, None),
            P("grp", None),
            P("grp"),
        ),
        check_vma=False,
    )
```

```python
import functools

import jax
import jax.numpy as jnp
from jax import lax
from jax.experimental import pallas as pl
from jax.experimental.pallas import tpu as pltpu
from jax.sharding import PartitionSpec as P

F32 = jnp.float32
BF16 = jnp.bfloat16
ALL_AXES = ("view", "slab", "chan")
ROW_AXES = ("view", "slab")
HID = 16
TILE = 128
REACH = 4
TAPS = 9
NN = (((1,), (0,)), ((), ()))
NT = (((1,), (1,)), ((), ()))
TN = (((0,), (0,)), ((), ()))
MIB = 1024 * 1024


def dot(left, right, dims=NN, precision=None):
    return lax.dot_general(left, right, dims, precision=precision, preferred_element_type=F32)


def iota(shape, dim):
    return lax.broadcasted_iota(jnp.int32, shape, dim)


def repeat(count, step, limit=16):
    if count <= limit:
        for index in range(count):
            step(index)
    else:

        @pl.loop(0, count)
        def unused(index):
            step(index)


def weights_kernel(chan_ref, middle_own, first_own, last_own, middle_other, first_other, last_other,
                   middle, first, last):
    wide = HID * HID
    chan = chan_ref[0]
    lane_z = iota((HID, wide), 1) >> 4
    row_z = iota((HID, wide), 0)

    spread = ((iota((HID, wide), 1) & (HID - 1)) == iota((HID, wide), 0)).astype(BF16)

    def spread_middle(source):
        rows = jnp.concatenate([source[k].astype(F32) for k in range(27)], axis=0)
        return dot(rows.astype(BF16), spread)

    mine, theirs = (spread_middle(middle_own), spread_middle(middle_other))
    lower = jnp.where(chan == 0, mine, theirs)
    upper = jnp.where(chan == 0, theirs, mine)
    for tap in range(TAPS):
        parts = []
        for depth in range(3):
            begin = (depth * TAPS + tap) * 8
            parts.append(
                jnp.concatenate([lower[begin : begin + 8], upper[begin : begin + 8]], axis=0)
            )
        for z in range(HID):
            block = jnp.where(
                lane_z == z - 1,
                parts[0],
                jnp.where(lane_z == z, parts[1], jnp.where(lane_z == z + 1, parts[2], 0.0)),
            )
            begin = (tap % 3) * wide + z * HID
            middle[tap // 3, begin : begin + HID, :] = block.astype(BF16)

    channel = iota((8, wide), 1) & (HID - 1)
    spread_own = (channel == iota((8, wide), 0) + 8 * chan).astype(BF16)
    spread_other = (channel == iota((8, wide), 0) + 8 * (1 - chan)).astype(BF16)

    def lines(own, other):
        return dot(own, spread_own) + dot(other, spread_other)

    def banded(rows, step):
        out = jnp.zeros((HID, wide), F32)
        for depth, line in enumerate(rows):
            line = jnp.broadcast_to(line, (HID, wide))
            out = jnp.where(row_z - lane_z == step * (depth - 1), line, out)
        return out.astype(BF16)

    first_lines = [lines(first_own[k], first_other[k]) for k in range(27)]
    last_lines = [lines(last_own[k // 3, k % 3], last_other[k // 3, k % 3]) for k in range(9)]
    for tap in range(TAPS):
        for c in range(2):
            begin = (c * TAPS + tap) * HID
            rows = [first_lines[depth * TAPS + tap][c : c + 1] for depth in range(3)]
            first[begin : begin + HID, :] = banded(rows, 1)
        dy, dx = (tap // 3, tap % 3)
        rows = [last_lines[depth * 3 + dy][dx : dx + 1] for depth in range(3)]
        last[tap * HID : (tap + 1) * HID, :] = banded(rows, -1)


def build_weights(chan, conv_first, conv_middle, conv_last):
    own = (
        conv_middle.transpose(2, 3, 4, 0, 1).reshape(27, 8, HID),
        conv_first.transpose(2, 3, 4, 1, 0).reshape(27, 2, 8),
        conv_last.transpose(0, 2, 3, 4, 1).reshape(3, 3, 3, 8),
    )
    other = tuple(lax.ppermute(value, "chan", [(0, 1), (1, 0)]) for value in own)
    wide = HID * HID
    smem = pl.BlockSpec(memory_space=pltpu.SMEM)
    vmem = pl.BlockSpec(memory_space=pltpu.VMEM)
    return pl.pallas_call(
        weights_kernel,
        out_shape=(
            jax.ShapeDtypeStruct((3, 3 * wide, wide), BF16),
            jax.ShapeDtypeStruct((2 * TAPS * HID, wide), BF16),
            jax.ShapeDtypeStruct((TAPS * HID, wide), BF16),
        ),
        in_specs=[smem] + [vmem] * 6,
        out_specs=(vmem, vmem, vmem),
        compiler_params=pltpu.CompilerParams(vmem_limit_bytes=16 * MIB),
        cost_estimate=pl.CostEstimate(flops=10**8, bytes_accessed=2 * 10**6, transcendentals=0),
        name="band_weights",
    )(chan, *own, *other)


def sigmoid(value):
    return jax.nn.sigmoid(value)


def projector(sizes, table, footprints):
    rows_count, per_view = (sizes[0], sizes[9])
    groups = rows_count // 8

    def tile_of(tile, owner):
        return table[0][tile // per_view, tile % per_view, 0, owner]

    def block_of(tile, owner):
        return footprints[table[1][tile // per_view, tile % per_view, 0, owner]]

    def project(tile, pick):
        def one(group):
            owners = [group * 8 + o for o in range(8)]
            left = jnp.concatenate([pick(tile, o) for o in owners], axis=1)
            right = jnp.concatenate([block_of(tile, o) for o in owners], axis=0)
            return dot(left, right)

        if groups == 1:
            return one(0)
        return lax.fori_loop(0, groups, lambda g, a: a + one(g), jnp.zeros((16, TILE), F32))

    return tile_of, block_of, project


def dual_reader(scalars, proj, dual, meas):
    batch = 4

    def mixed_of(m, parts):
        return scalars[0][0, m] * parts[0] + scalars[0][1, m] * parts[1] + scalars[0][2, m] * parts[2]

    def stack_of(chunk):
        span = pl.ds(chunk * batch, batch)
        return span, (dual[span], proj[span], meas[span])

    return batch, mixed_of, stack_of


def dual_gradients(sizes, table, scalars, footprints, proj, dual, meas, grad_tiles, grad, sums):
    rows_count, chans, detectors, tiles, width = sizes[:5]
    low = (table[2][0] * chans + table[3][0]) * width
    tile_of, _, project = projector(sizes, table, footprints)
    batch, mixed_of, stack_of = dual_reader(scalars, proj, dual, meas)

    def project_grad(tile):
        def pick(t, o):
            return grad_tiles[o, (tile_of(t, o) == lax.div(low, TILE)).astype(jnp.int32)]

        grad[tile] = project(tile, pick)

    repeat(detectors, project_grad)
    sums[...] = jnp.zeros_like(sums)

    def dual_sums(chunk):
        span, parts = stack_of(chunk)
        pulled_in = grad[span]
        for m in range(HID):
            mixed = mixed_of(m, parts)
            gate = sigmoid(mixed)
            slope = gate * (1.0 + mixed * (1.0 - gate))
            pulled = pulled_in * slope * scalars[1][m]
            terms = [pulled_in * (mixed * gate)] + [pulled * part for part in parts]
            for k, term in enumerate(terms):
                sums[k, m] += jnp.sum(term.reshape(batch * 2, 8, TILE), axis=0)

    repeat(detectors // batch, dual_sums)
    lane_out = iota((HID, TILE), 1)
    small = jnp.zeros((HID, TILE), F32)
    for k in range(4):
        column = jnp.sum(jnp.sum(sums[k], axis=1), axis=1, keepdims=True)
        small = jnp.where(lane_out == k, column, small)
    filled = jnp.concatenate([small, jnp.zeros((TILE - HID, TILE), F32)], axis=0)
    return jnp.transpose(filled)[0:8]


def dual_gradients_kernel(sizes, rows_ref, blocks_ref, row_ref, chan_ref, mixing, readout,
                          footprints, proj, dual, meas, grad_tiles, out, grad, sums):
    table = (rows_ref, blocks_ref, row_ref, chan_ref)
    out[...] = dual_gradients(
        sizes, table, (mixing, readout), footprints, proj, dual, meas, grad_tiles, grad, sums
    )


def main_kernel(sizes, whole, rows_ref, blocks_ref, row_ref, chan_ref, mixing, readout, payload, footprints, middle, first, last,
                keep, send, dual_out, proj, dual, meas, grad_tiles,
                vol, cot, dual_half, dual_new, back, field, col_in, col_cot,
                act_wide, grad_wide, slope_first, slope_middle, row_tiles, sums):
    rows_count, chans, detectors, tiles, width, stride, cells, piece_slot, update_row, _ = sizes
    table = (rows_ref, blocks_ref, row_ref, chan_ref)
    scalars = (mixing, readout)
    row = row_ref[0]
    chan = chan_ref[0]
    low = (row * chans + chan) * width
    count = rows_count * stride
    lanes = count + TILE

    def place(owner):
        slots = [piece_slot(owner, part, row, chan) for part in range(2)]
        for field_index, target in ((0, vol), (1, cot)):
            for k in range(tiles // 2):
                halves = [payload[slot, field_index * (tiles // 2) + k].astype(F32) for slot in slots]
                for t in range(2):
                    whole_tile = jnp.concatenate([h[t * 8 : (t + 1) * 8] for h in halves], axis=0)
                    target[owner * tiles + 2 * k + t] = whole_tile.astype(BF16)
        for k, target in ((tiles, dual), (tiles + 1, meas)):
            for part in range(2):
                piece = payload[slots[part], k].astype(F32)
                for t in range(2):
                    target[owner * 2 + t, part * 8 : (part + 1) * 8, :] = piece[t * 8 : (t + 1) * 8]

    repeat(rows_count, place)

    tile_of, block_of, project = projector(sizes, table, footprints)

    def project_volume(tile):
        proj[tile] = project(tile, lambda t, o: vol[o * tiles + tile_of(t, o)])

    repeat(detectors, project_volume)

    batch, mixed_of, stack_of = dual_reader(scalars, proj, dual, meas)

    def dual_block(chunk):
        span, parts = stack_of(chunk)
        total = parts[0]
        for m in range(HID):
            mixed = mixed_of(m, parts)
            total = total + scalars[1][m] * (mixed * sigmoid(mixed))
        dual_new[span] = total
        dual_half[span] = total.astype(BF16)

    repeat(detectors // batch, dual_block)
    for t in range(2):
        dual_out[:, t * TILE : (t + 1) * TILE] = dual_new[
            row * 2 + t, pl.ds(pl.multiple_of(chan * 8, 8), 8), :
        ]

    window = width + 2 * REACH
    tile_low = lax.div(low - REACH + TILE, TILE) - 1
    offset = low - REACH - tile_low * TILE

    def backproject(group):
        owners = [group * 8 + o for o in range(8)]

        def add(tile, totals):
            right = jnp.concatenate([block_of(tile, o) for o in owners], axis=0)
            products = dot(dual_half[tile], right, NT)
            out = []
            for o in range(8):
                place_of = tile_of(tile, owners[o]) - tile_low
                product = products[:, o * TILE : (o + 1) * TILE]
                for side in range(2):
                    out.append(totals[2 * o + side] + jnp.where(place_of == side, product, 0.0))
            return tuple(out)

        totals = tuple(jnp.zeros((16, TILE), F32) for _ in range(16))
        if detectors <= 16:
            for tile in range(detectors):
                totals = add(tile, totals)
        else:
            totals = lax.fori_loop(0, detectors, add, totals)
        for o in range(8):
            for side in range(2):
                back[owners[o], side] = totals[2 * o + side]

    repeat(rows_count // 8, backproject)

    lane = iota((3 * 16, TILE), 1)
    clip_low = jnp.clip(tile_low, 0, tiles - 1)
    clip_high = jnp.clip(tile_low + 1, 0, tiles - 1)
    pieces = [None] * (lanes // TILE)
    for y in range(rows_count):
        sides = []
        for side, clipped in ((0, clip_low), (1, clip_high)):
            sides.append(
                jnp.concatenate(
                    [
                        vol[y * tiles + clipped].astype(F32),
                        back[y, side].astype(BF16).astype(F32),
                        cot[y * tiles + clipped].astype(F32),
                    ],
                    axis=0,
                )
            )
        merged = jnp.where(lane >= offset, sides[0], sides[1])
        shift = lax.rem(y * stride - offset + TILE * (count // TILE + 1), TILE)
        merged = pltpu.roll(merged, shift, 1)
        for t in range(y * stride // TILE, (y * stride + window - 1) // TILE + 1):
            column = lane + (t * TILE - y * stride)
            cell = column + (low - REACH)
            inside = (column >= 0) & (column < window) & (cell >= 0) & (cell < cells)
            taken = jnp.where(inside, merged, 0.0)
            pieces[t] = taken if pieces[t] is None else pieces[t] + taken
    for t in range(lanes // TILE):
        field[:, t * TILE : (t + 1) * TILE] = (
            jnp.zeros((3 * 16, TILE), F32) if pieces[t] is None else pieces[t]
        )

    def shift_of(tap):
        return stride * (tap // 3 - 1) + (tap % 3 - 1)

    def rolled(value, amount):
        amount = amount % lanes
        return value if amount == 0 else pltpu.roll(value, amount, 1)

    for tap in range(TAPS):
        for channel in range(2):
            begin = (channel * TAPS + tap) * HID
            part = rolled(field[channel * 16 : (channel + 1) * 16, :], -shift_of(tap))
            col_in[begin : begin + HID, :] = part[:, :count].astype(BF16)
        part = rolled(field[32:48, :], shift_of(tap))
        col_cot[tap * HID : (tap + 1) * HID, :] = part[:, :count].astype(BF16)

    wide = HID * HID
    place_x = iota((stride, wide), 0)
    cell_x = place_x + (low - REACH)
    valid = (cell_x >= 0) & (cell_x < cells)
    own = (place_x >= REACH) & (place_x < REACH + width)

    def masked(mask, value):
        shaped = value.reshape(rows_count, stride, wide)
        return jnp.where(mask[None], shaped, 0.0).reshape(count, wide)

    def widen(target, value, step):
        zero = jnp.zeros((stride, 3 * wide), BF16)
        target[0:stride, :] = zero
        target[stride + count :, :] = zero
        for k, amount in ((0, step), (1, 0), (2, -step)):
            moved = value if amount == 0 else pltpu.roll(value, amount % count, 0)
            target[stride : stride + count, k * wide : (k + 1) * wide] = moved.astype(BF16)

    first_pre = dot(col_in[...], first[...], TN)
    gate = sigmoid(first_pre)
    slope_first[...] = gate * (1.0 + first_pre * (1.0 - gate))
    widen(act_wide, masked(valid, first_pre * gate), 1)
    middle_pre = None
    for dy in range(3):
        for dx in range(3):
            part = dot(
                act_wide[stride * dy : stride * dy + count, dx * wide : (dx + 1) * wide],
                middle[dy, dx * wide : (dx + 1) * wide, :],
                NT,
            )
            middle_pre = part if middle_pre is None else middle_pre + part
    gate = sigmoid(middle_pre)
    slope_middle[...] = gate * (1.0 + middle_pre * (1.0 - gate))
    middle_act = masked(valid, middle_pre * gate)
    middle_half = middle_act.astype(BF16)

    def gather_taps(products, sign):
        padded = jnp.concatenate([products, jnp.zeros((TAPS * HID, TILE), F32)], axis=1)
        total = None
        for tap in range(TAPS):
            part = rolled(padded[tap * HID : (tap + 1) * HID], sign * shift_of(tap))
            total = part if total is None else total + part
        return total

    def rows_to_tiles(value, target):
        lane_one = iota((16, TILE), 1)
        for y in range(rows_count):
            begin = y * stride + REACH
            merged = None
            for t in range(begin // TILE, (begin + width - 1) // TILE + 1):
                column = lane_one + t * TILE
                inside = (column >= begin) & (column < begin + width)
                part = jnp.where(inside, value[:, t * TILE : (t + 1) * TILE], 0.0)
                merged = part if merged is None else merged + part
            shift = lax.rem(low - begin + TILE * (count // TILE + 1), TILE)
            target(y, pltpu.roll(merged, shift, 1))

    update = gather_taps(dot(last[...], middle_half, NT), -1) + field[0:16, :]

    def put_row(y, tile):
        row_tiles[y] = tile

    rows_to_tiles(update, put_row)

    middle_grad = masked(valid, dot(col_cot[...], last[...], TN) * slope_middle[...])
    grad_last = dot(col_cot[...], masked(own, middle_act).astype(BF16))
    widen(grad_wide, middle_grad, -1)
    turned = jnp.transpose(masked(own, middle_grad)).astype(BF16)
    grads_middle = [
        dot(turned, act_wide[stride * dy : stride * dy + count, :]) for dy in range(3)
    ]
    first_sum = None
    for dy in range(3):
        part = dot(grad_wide[stride * (2 - dy) : stride * (2 - dy) + count, :], middle[dy])
        first_sum = part if first_sum is None else first_sum + part
    first_grad = masked(valid, first_sum * slope_first[...])
    first_half = first_grad.astype(BF16)
    turned = jnp.transpose(masked(own, first_grad)).astype(BF16)
    grad_first = dot(turned, col_in[...], NT)
    back_grad = gather_taps(dot(first[TAPS * HID :, :], first_half, NT), 1)

    def put_grad(y, tile):
        grad_tiles[y, 0] = jnp.zeros((16, TILE), BF16)
        grad_tiles[y, 1] = tile.astype(BF16)

    rows_to_tiles(back_grad, put_grad)

    lane_z = iota((HID, wide), 1) >> 4
    lane_group = iota((HID, TILE), 1) >> 4
    out_tiles = [jnp.zeros((HID, TILE), F32) for _ in range(4)]

    def fold_lanes(value):
        value = value[:, :TILE] + value[:, TILE:]
        for amount in (64, 32, 16):
            value = value + pltpu.roll(value, amount, 1)
        return value

    def put(index, value):
        group = index // 8
        out_tiles[group] = jnp.where(lane_group == index % 8, value, out_tiles[group])

    for tap in range(TAPS):
        plane = grads_middle[tap // 3][:, (tap % 3) * wide : (tap % 3 + 1) * wide]
        for depth in range(3):
            total = jnp.zeros((HID, wide), F32)
            for z in range(HID):
                total = total + jnp.where(lane_z == z + depth - 1, plane[z * HID : (z + 1) * HID], 0.0)
            put(depth * TAPS + tap, fold_lanes(total))

    lane_in = iota((HID, 2 * TAPS * HID), 1) & (HID - 1)
    folds = []
    for depth in range(3):
        total = jnp.zeros((HID, 2 * TAPS * HID), F32)
        for z in range(HID):
            total = total + jnp.where(lane_in == z + depth - 1, grad_first[z * HID : (z + 1) * HID], 0.0)
        folds.append(total)
    source = iota((2 * TAPS * HID, TILE), 0) >> 4
    target = iota((2 * TAPS * HID, TILE), 1)
    for depth in range(3):
        channel = (source >= TAPS).astype(jnp.int32)
        fold = (target == 48 + (depth * TAPS + source - TAPS * channel) * 2 + channel).astype(F32)
        out_tiles[3] = out_tiles[3] + dot(folds[depth], fold, precision=lax.Precision.HIGHEST)

    row_z = iota((HID, wide), 0)
    lines = []
    for depth in range(3):
        keep_last = lane_z == row_z + depth - 1
        for tap in range(TAPS):
            part = jnp.where(keep_last, grad_last[tap * HID : (tap + 1) * HID], 0.0)
            lines.append(jnp.sum(part, axis=0, keepdims=True))
    lines.append(jnp.zeros((32 - 27, wide), F32))
    lines = fold_lanes(jnp.concatenate(lines, axis=0))
    row_eight = iota((8, TILE), 0)
    packed_last = jnp.zeros((8, TILE), F32)
    for r in range(4):
        picked = jnp.where(row_eight == iota((8, TILE), 1) >> 4, lines[r * 8 : (r + 1) * 8], 0.0)
        packed_last = jnp.where(
            row_eight == r, jnp.sum(picked, axis=0, keepdims=True), packed_last
        )

    if whole:
        small = dual_gradients(
            sizes, table, scalars, footprints, proj, dual, meas, grad_tiles, dual_new, sums
        )
    else:
        small = jnp.zeros((8, TILE), F32)

    for t in range(4):
        slope_first[0:HID, 0:TILE] = out_tiles[t]
        keep[t * 8 : (t + 1) * 8, :] = slope_first[pl.ds(pl.multiple_of(chan * 8, 8), 8), 0:TILE]
        send[t * 8 : (t + 1) * 8, :] = slope_first[
            pl.ds(pl.multiple_of((chans - 1 - chan) * 8, 8), 8), 0:TILE
        ]
    for target in (keep, send):
        target[32:40, :] = packed_last
        target[40:48, :] = small

    def put_update(y):
        begin = pl.multiple_of(48 + y * 16, 8)
        tile = row_tiles[update_row(y, row)]
        keep[pl.ds(begin, 16), :] = tile
        send[pl.ds(begin, 16), :] = tile

    repeat(rows_count, put_update)


def write_grads(chan, grads, middle, first, last, mixing, readout):
    for k in range(27):
        block = grads[(k // 8) * 8 : (k // 8 + 1) * 8]
        block = block if k % 8 == 0 else pltpu.roll(block, TILE - 16 * (k % 8), 1)
        middle[k] = block[:, :HID]
    filled = jnp.concatenate([grads[24:32], jnp.zeros((TILE - 8, TILE), F32)], axis=0)
    turned = jnp.transpose(filled)
    for k in range(27):
        first[k] = turned[48 + 2 * k : 50 + 2 * k, :8]
    block = pltpu.roll(grads[32:40], lax.rem(TILE - 8 * chan, TILE), 1)
    for group in range(8):
        moved = block if group == 0 else pltpu.roll(block, TILE - 16 * group, 1)
        for r in range(4):
            if r * 8 + group < 27:
                last[r * 8 + group] = moved[r : r + 1, :8]
    mixing[...] = grads[41:44, :HID]
    readout[...] = grads[40:41, :HID]


def finish_kernel(row_ref, chan_ref, own, one, two, three, far, total, volume, *rest):
    grads, slots = (rest[:-1], rest[-1])
    row = row_ref[0]
    write_grads(chan_ref[0], total[...] + far[0:48, :], *grads)
    for k, (source, begin) in enumerate(
        ((own, 48), (one, 48), (two, 48), (three, 48), (far, 48), (far, 64), (far, 80), (far, 96))
    ):
        slots[k] = source[begin : begin + 16, :]
    for tile in range(8):
        volume[:, tile, :] = slots[tile ^ row]


def finish_grads_kernel(chan_ref, total, *grads):
    write_grads(chan_ref[0], total[...], *grads)


def row_mask_pairs(devices, mask):
    return [(index, index ^ mask) for index in range(devices)]


def body(
    volume,
    dual_state,
    measured,
    cotangent,
    conv_first,
    conv_middle,
    conv_last,
    dual_mixing,
    dual_readout,
    footprints,
    tile_rows,
    tile_blocks,
):
    views, slabs, chans = (lax.axis_size(a) for a in ALL_AXES)
    rows_count = views * slabs
    devices = rows_count * chans
    cells = volume.shape[2]
    tiles = cells // TILE
    width = cells // devices
    stride = -(-(width + 2 * REACH) // 16) * 16
    detectors = tile_rows.shape[0] * tile_rows.shape[1]
    chan = lax.axis_index("chan")
    row = lax.axis_index("view") * slabs + lax.axis_index("slab")
    quick = rows_count == 8 and chans == 2

    def chan_half(value):
        shaped = jnp.swapaxes(value.reshape(2, 8, tiles, TILE), 1, 2)
        half = lax.dynamic_index_in_dim(shaped, chan, 0, keepdims=False)
        return half.reshape(tiles // 2, 16, TILE)

    def dual_piece(value):
        return jnp.swapaxes(value.reshape(8, 2, TILE), 0, 1).reshape(1, 16, TILE)

    payload = jnp.concatenate(
        [chan_half(volume), chan_half(cotangent), dual_piece(dual_state), dual_piece(measured)],
        axis=0,
    )[None]

    def swap(value, mask):
        return lax.ppermute(value, ALL_AXES, row_mask_pairs(devices, mask))

    if quick:
        payload = jnp.concatenate([payload, swap(payload, 8)], axis=0)
        payload = jnp.concatenate([payload] + [swap(payload, k) for k in (2, 4, 6)], axis=0)
        payload = jnp.concatenate([payload, swap(payload, 1)], axis=0)
    else:
        payload = lax.all_gather(payload, ALL_AXES, axis=0, tiled=True)

    def piece_slot(owner, part, row, chan):
        if not quick:
            return owner * chans + part
        mask = owner ^ row
        return (mask & 3) * 2 + (mask >> 2) + rows_count * (part ^ chan)

    def update_row(owner, row):
        return owner ^ row if quick else owner

    row_one = row.reshape(1).astype(jnp.int32)
    chan_one = chan.reshape(1).astype(jnp.int32)
    middle, first, last = build_weights(chan_one, conv_first, conv_middle, conv_last)
    table = (jnp.swapaxes(tile_rows, 2, 3), jnp.swapaxes(tile_blocks, 2, 3), row_one, chan_one)
    scalars = (dual_mixing.T, dual_readout)
    count = rows_count * stride
    wide = HID * HID
    moved = 48 + 16 * rows_count
    limit = (20 if quick else 56) * MIB
    vmem = pl.BlockSpec(memory_space=pltpu.VMEM)
    smem = pl.BlockSpec(memory_space=pltpu.SMEM)
    sizes = (rows_count, chans, detectors, tiles, width, stride, cells, piece_slot, update_row,
             tile_rows.shape[1])
    outs = [
        ((moved, TILE), F32),
        ((moved, TILE), F32),
        ((8, 2 * TILE), F32),
    ]
    shared = [
        ((detectors, 16, TILE), F32),
        ((detectors, 16, TILE), F32),
        ((detectors, 16, TILE), F32),
        ((rows_count, 2, 16, TILE), BF16),
    ]
    scratch = [
        ((rows_count * tiles, 16, TILE), BF16),
        ((rows_count * tiles, 16, TILE), BF16),
        ((detectors, 16, TILE), BF16),
        ((detectors, 16, TILE), F32),
        ((rows_count, 2, 16, TILE), F32),
        ((48, count + TILE), F32),
        ((2 * TAPS * HID, count), BF16),
        ((TAPS * HID, count), BF16),
        ((count + 2 * stride, 3 * wide), BF16),
        ((count + 2 * stride, 3 * wide), BF16),
        ((count, wide), F32),
        ((count, wide), F32),
        ((rows_count, 16, TILE), F32),
        ((4, HID, 8, TILE), F32),
    ]
    if quick:
        scratch = shared + scratch
    else:
        outs = outs + shared
    keep, send, new_dual, *rest = pl.pallas_call(
        functools.partial(main_kernel, sizes, quick),
        out_shape=[jax.ShapeDtypeStruct(*spec) for spec in outs],
        in_specs=[smem] * 6 + [vmem] * 5,
        out_specs=[vmem] * len(outs),
        scratch_shapes=[pltpu.VMEM(*spec) for spec in scratch],
        compiler_params=pltpu.CompilerParams(vmem_limit_bytes=limit),
        cost_estimate=pl.CostEstimate(
            flops=5 * 10**9, bytes_accessed=5 * 10**6, transcendentals=2 * 10**6
        ),
        name="primal_dual",
    )(*table, *scalars, payload, footprints, middle, first, last)

    mine = keep + swap(send, 1)
    grad_shapes = [
        jax.ShapeDtypeStruct(shape, F32)
        for shape in ((27, 8, HID), (27, 2, 8), (27, 1, 8), (3, HID), (1, HID))
    ]
    if quick:

        def piece(value, index):
            return value[48 + 16 * index : 64 + 16 * index]

        parts = [
            swap(jnp.concatenate([mine[:48], piece(mine, k), piece(mine, k ^ 4)], axis=0), 2 * k)
            for k in (1, 2, 3)
        ]
        total = mine[:48] + parts[0][:48] + parts[1][:48] + parts[2][:48]
        far = swap(
            jnp.concatenate([total, piece(mine, 4)] + [piece(part, 1) for part in parts], axis=0), 8
        )
        new_volume, *grads = pl.pallas_call(
            finish_kernel,
            out_shape=[jax.ShapeDtypeStruct((16, 8, TILE), F32)] + grad_shapes,
            in_specs=[smem, smem] + [vmem] * 6,
            out_specs=[vmem] * 6,
            scratch_shapes=[pltpu.VMEM((8, 16, TILE), F32)],
            compiler_params=pltpu.CompilerParams(vmem_limit_bytes=8 * MIB),
            name="finish",
        )(row_one, chan_one, mine, *parts, far, total)
    else:
        small = pl.pallas_call(
            functools.partial(dual_gradients_kernel, sizes),
            out_shape=jax.ShapeDtypeStruct((8, TILE), F32),
            in_specs=[smem] * 6 + [vmem] * 5,
            out_specs=vmem,
            scratch_shapes=[
                pltpu.VMEM((detectors, 16, TILE), F32),
                pltpu.VMEM((4, HID, 8, TILE), F32),
            ],
            compiler_params=pltpu.CompilerParams(vmem_limit_bytes=limit),
            name="dual_gradients",
        )(*table, *scalars, footprints, *rest)
        total = jnp.concatenate(
            [lax.psum(mine[:40], ROW_AXES), lax.psum(small, ALL_AXES)], axis=0
        )
        grads = pl.pallas_call(
            finish_grads_kernel,
            out_shape=grad_shapes,
            in_specs=[smem, vmem],
            out_specs=[vmem] * 5,
            name="finish_grads",
        )(chan_one, total)
        pieces = lax.all_to_all(
            mine[48:].reshape(rows_count, 16, TILE), ROW_AXES, 0, 0, tiled=True
        )
        pieces = pieces.reshape(tiles, rows_count // tiles, 16, TILE).sum(axis=1)
        new_volume = jnp.swapaxes(pieces, 0, 1)

    grad_middle, grad_first, grad_last, grad_mixing, grad_readout = grads
    return (
        new_volume.reshape(volume.shape),
        new_dual.reshape(dual_state.shape),
        grad_first.reshape(3, 3, 3, 2, 8).transpose(4, 3, 0, 1, 2),
        grad_middle.reshape(3, 3, 3, 8, HID).transpose(3, 4, 0, 1, 2),
        grad_last.reshape(3, 3, 3, 1, 8).transpose(3, 4, 0, 1, 2),
        grad_mixing.T,
        grad_readout.reshape(HID),
    )


def solution(mesh):
    placed = (
        P("grp", ("view", "slab"), None),
        P(("grp", "view"), "chan", "slab"),
        P(("grp", "view"), "chan", "slab"),
        P("grp", ("view", "slab"), None),
        P("chan", None, None, None, None),
        P("chan", None, None, None, None),
        P(None, "chan", None, None, None),
        P(),
        P(),
        P(),
        P(),
        P(),
    )
    return jax.shard_map(
        body,
        mesh=mesh,
        in_specs=placed,
        out_specs=(
            P("grp", ("view", "slab"), None),
            P(("grp", "view"), "chan", "slab"),
            P(("grp", "chan"), None, None, None, None),
            P(("grp", "chan"), None, None, None, None),
            P("grp", "chan", None, None, None),
            P("grp", None),
            P("grp"),
        ),
        check_vma=False,
    )
```

```python
import functools

import jax
import jax.numpy as jnp
from jax import lax
from jax.experimental import pallas as pl
from jax.experimental.pallas import tpu as pltpu
from jax.sharding import PartitionSpec as P

F32 = jnp.float32
BF16 = jnp.bfloat16
ALL_AXES = ("view", "slab", "chan")
ROW_AXES = ("view", "slab")
HID = 16
TILE = 128
REACH = 4
TAPS = 9
NN = (((1,), (0,)), ((), ()))
NT = (((1,), (1,)), ((), ()))
TN = (((0,), (0,)), ((), ()))
MIB = 1024 * 1024


def dot(left, right, dims=NN, precision=None):
    return lax.dot_general(left, right, dims, precision=precision, preferred_element_type=F32)


def iota(shape, dim):
    return lax.broadcasted_iota(jnp.int32, shape, dim)


def repeat(count, step, limit=16):
    if count <= limit:
        for index in range(count):
            step(index)
    else:

        @pl.loop(0, count)
        def unused(index):
            step(index)


def in_hbm(value):
    return pltpu.with_memory_space_constraint(value, pltpu.HBM)


def fetch(sources, targets, arrivals):
    copies = [
        pltpu.make_async_copy(source, target, arrivals.at[k])
        for k, (source, target) in enumerate(zip(sources, targets))
    ]
    for copy in copies:
        copy.start()
    return copies


def weights_kernel(chan_ref, middle_from, first_from, last_from,
                   middle_other, first_other, last_other,
                   middle, first, last, middle_own, first_own, last_own, arrivals):
    wide = HID * HID
    for copy in fetch(
        (middle_from, first_from, last_from), (middle_own, first_own, last_own), arrivals
    ):
        copy.wait()
    chan = chan_ref[0]
    lane_z = iota((HID, wide), 1) >> 4
    row_z = iota((HID, wide), 0)

    spread = ((iota((HID, wide), 1) & (HID - 1)) == iota((HID, wide), 0)).astype(BF16)

    def spread_middle(source):
        rows = jnp.concatenate([source[k].astype(F32) for k in range(27)], axis=0)
        return dot(rows.astype(BF16), spread)

    mine, theirs = (spread_middle(middle_own), spread_middle(middle_other))
    lower = jnp.where(chan == 0, mine, theirs)
    upper = jnp.where(chan == 0, theirs, mine)
    for tap in range(TAPS):
        parts = []
        for depth in range(3):
            begin = (depth * TAPS + tap) * 8
            parts.append(
                jnp.concatenate([lower[begin : begin + 8], upper[begin : begin + 8]], axis=0)
            )
        for z in range(HID):
            block = jnp.where(
                lane_z == z - 1,
                parts[0],
                jnp.where(lane_z == z, parts[1], jnp.where(lane_z == z + 1, parts[2], 0.0)),
            )
            begin = (tap % 3) * wide + z * HID
            middle[tap // 3, begin : begin + HID, :] = block.astype(BF16)

    channel = iota((8, wide), 1) & (HID - 1)
    spread_own = (channel == iota((8, wide), 0) + 8 * chan).astype(BF16)
    spread_other = (channel == iota((8, wide), 0) + 8 * (1 - chan)).astype(BF16)

    def lines(own, other):
        return dot(own, spread_own) + dot(other, spread_other)

    def banded(rows, step):
        out = jnp.zeros((HID, wide), F32)
        for depth, line in enumerate(rows):
            line = jnp.broadcast_to(line, (HID, wide))
            out = jnp.where(row_z - lane_z == step * (depth - 1), line, out)
        return out.astype(BF16)

    first_lines = [lines(first_own[k], first_other[k]) for k in range(27)]
    last_lines = [lines(last_own[k // 3, k % 3], last_other[k // 3, k % 3]) for k in range(9)]
    for tap in range(TAPS):
        for c in range(2):
            begin = (c * TAPS + tap) * HID
            rows = [first_lines[depth * TAPS + tap][c : c + 1] for depth in range(3)]
            first[begin : begin + HID, :] = banded(rows, 1)
        dy, dx = (tap // 3, tap % 3)
        rows = [last_lines[depth * 3 + dy][dx : dx + 1] for depth in range(3)]
        last[tap * HID : (tap + 1) * HID, :] = banded(rows, -1)


def own_weights(conv_first, conv_middle, conv_last):
    return (
        conv_middle.transpose(2, 3, 4, 0, 1).reshape(27, 8, HID),
        conv_first.transpose(2, 3, 4, 1, 0).reshape(27, 2, 8),
        conv_last.transpose(0, 2, 3, 4, 1).reshape(3, 3, 3, 8),
    )


def build_weights(chan, own, other):
    wide = HID * HID
    hbm = pl.BlockSpec(memory_space=pltpu.HBM)
    smem = pl.BlockSpec(memory_space=pltpu.SMEM)
    vmem = pl.BlockSpec(memory_space=pltpu.VMEM)
    return pl.pallas_call(
        weights_kernel,
        out_shape=(
            jax.ShapeDtypeStruct((3, 3 * wide, wide), BF16),
            jax.ShapeDtypeStruct((2 * TAPS * HID, wide), BF16),
            jax.ShapeDtypeStruct((TAPS * HID, wide), BF16),
        ),
        in_specs=[smem] + [hbm] * 3 + [vmem] * 3,
        out_specs=(vmem, vmem, vmem),
        scratch_shapes=[pltpu.VMEM(value.shape, value.dtype) for value in own]
        + [pltpu.SemaphoreType.DMA((3,))],
        compiler_params=pltpu.CompilerParams(vmem_limit_bytes=16 * MIB),
        cost_estimate=pl.CostEstimate(flops=10**8, bytes_accessed=2 * 10**6, transcendentals=0),
        name="band_weights",
    )(chan, *(in_hbm(value) for value in own), *other)


def sigmoid(value):
    return jax.nn.sigmoid(value)


def projector(sizes, table, footprints):
    rows_count, per_view = (sizes[0], sizes[-1])
    groups = rows_count // 8

    def tile_of(tile, owner):
        return table[0][tile // per_view, tile % per_view, 0, owner]

    def block_of(tile, owner):
        return footprints[table[1][tile // per_view, tile % per_view, 0, owner]]

    def project(tile, pick):
        def one(group):
            owners = [group * 8 + o for o in range(8)]
            left = jnp.concatenate([pick(tile, o) for o in owners], axis=1)
            right = jnp.concatenate([block_of(tile, o) for o in owners], axis=0)
            return dot(left, right)

        if groups == 1:
            return one(0)
        return lax.fori_loop(0, groups, lambda g, a: a + one(g), jnp.zeros((16, TILE), F32))

    return tile_of, block_of, project


def dual_reader(scalars, proj, dual, meas):
    batch = 4

    def mixed_of(m, parts):
        return scalars[0][0, m] * parts[0] + scalars[0][1, m] * parts[1] + scalars[0][2, m] * parts[2]

    def stack_of(chunk):
        span = pl.ds(chunk * batch, batch)
        return span, (dual[span], proj[span], meas[span])

    return batch, mixed_of, stack_of


def dual_gradients(sizes, table, scalars, footprints, proj, dual, meas, grad_tiles, grad, sums):
    detectors, width = (sizes[2], sizes[4])
    own_tile = lax.div(sizes[7][2](table[2][0], table[3][0]) * width, TILE)
    tile_of, _, project = projector(sizes, table, footprints)
    batch, mixed_of, stack_of = dual_reader(scalars, proj, dual, meas)

    def project_grad(tile):
        def pick(t, o):
            return grad_tiles[o, (tile_of(t, o) == own_tile).astype(jnp.int32)]

        grad[tile] = project(tile, pick)

    repeat(detectors, project_grad)
    sums[...] = jnp.zeros_like(sums)

    def dual_sums(chunk):
        span, parts = stack_of(chunk)
        pulled_in = grad[span]
        for m in range(HID):
            mixed = mixed_of(m, parts)
            gate = sigmoid(mixed)
            slope = gate * (1.0 + mixed * (1.0 - gate))
            pulled = pulled_in * slope * scalars[1][m]
            terms = [pulled_in * (mixed * gate)] + [pulled * part for part in parts]
            for k, term in enumerate(terms):
                sums[k, m] += jnp.sum(term.reshape(batch * 2, 8, TILE), axis=0)

    repeat(detectors // batch, dual_sums)
    lane_out = iota((HID, TILE), 1)
    small = jnp.zeros((HID, TILE), F32)
    for k in range(4):
        column = jnp.sum(jnp.sum(sums[k], axis=1), axis=1, keepdims=True)
        small = jnp.where(lane_out == k, column, small)
    filled = jnp.concatenate([small, jnp.zeros((TILE - HID, TILE), F32)], axis=0)
    return jnp.transpose(filled)[0:8]


def dual_gradients_kernel(sizes, rows_ref, blocks_ref, mixing, readout, row_ref, chan_ref,
                          footprints, proj, dual, meas, grad_tiles, out, grad, sums):
    table = (rows_ref, blocks_ref, row_ref, chan_ref)
    out[...] = dual_gradients(
        sizes, table, (mixing, readout), footprints, proj, dual, meas, grad_tiles, grad, sums
    )


def pack_kernel(chan_ref, volume_from, cotangent_from, dual_from, measured_from, out,
                volume, cotangent, dual, measured, arrivals):
    copies = fetch(
        (volume_from, cotangent_from, dual_from, measured_from),
        (volume, cotangent, dual, measured),
        arrivals,
    )
    chan = chan_ref[0]
    blocks = volume.shape[1] // (2 * TILE)

    def block(rows, k):
        begin = 2 * k * TILE
        pair = [rows[:, begin : begin + TILE], rows[:, begin + TILE : begin + 2 * TILE]]
        return jnp.concatenate(pair, axis=0).astype(BF16)

    for copy in copies:
        copy.wait()
    for index, source in enumerate((volume, cotangent)):
        value = source[...].astype(F32)
        half = jnp.where(chan == 0, value[:8], value[8:])
        for k in range(blocks):
            out[0, index * blocks + k] = block(half, k)
    out[0, 2 * blocks] = block(dual[...].astype(F32), 0)
    out[0, 2 * blocks + 1] = block(measured[...].astype(F32), 0)


def main_kernel(sizes, whole, rows_from, blocks_from, mixing_from, readout_from,
                footprints_from, row_ref, chan_ref, payload, payload_other, middle, first, last,
                keep, send, dual_out, proj, dual, meas, grad_tiles,
                vol, dual_half, dual_new, back, field, col_in, col_cot,
                act_wide, grad_wide, slope_first, slope_middle, row_tiles, sums,
                rows_ref, blocks_ref, mixing, readout, footprints, arrivals):
    rows_count, chans, detectors, tiles, width, stride, cells, places, updates, _ = sizes
    piece_slot, update_row, chunk_of, flip_of = places
    copies = fetch(
        (rows_from, blocks_from, mixing_from, readout_from, footprints_from),
        (rows_ref, blocks_ref, mixing, readout, footprints),
        arrivals,
    )
    table = (rows_ref, blocks_ref, row_ref, chan_ref)
    scalars = (mixing, readout)
    row = row_ref[0]
    chan = chan_ref[0]
    low = chunk_of(row, chan) * width
    count = rows_count * stride
    pad = -(-(stride + 1) // TILE) * TILE
    lanes = count + pad

    flip = flip_of(chan)

    def halves_of(owner, k):
        slot = piece_slot(owner, row)
        mine = payload[slot, k].astype(F32)
        theirs = payload_other[slot, k].astype(F32)
        return jnp.where(flip == 0, mine, theirs), jnp.where(flip == 0, theirs, mine)

    def place(owner):
        for k in range(tiles // 2):
            halves = halves_of(owner, k)
            for t in range(2):
                whole_tile = jnp.concatenate([h[t * 8 : (t + 1) * 8] for h in halves], axis=0)
                vol[owner * tiles + 2 * k + t] = whole_tile.astype(BF16)
        for k, target in ((tiles, dual), (tiles + 1, meas)):
            halves = halves_of(owner, k)
            for t in range(2):
                for part in range(2):
                    target[owner * 2 + t, part * 8 : (part + 1) * 8, :] = halves[part][
                        t * 8 : (t + 1) * 8
                    ]

    repeat(rows_count, place)

    for copy in copies:
        copy.wait()
    tile_of, block_of, project = projector(sizes, table, footprints)

    def project_volume(tile):
        proj[tile] = project(tile, lambda t, o: vol[o * tiles + tile_of(t, o)])

    repeat(detectors, project_volume)

    batch, mixed_of, stack_of = dual_reader(scalars, proj, dual, meas)

    def dual_block(chunk):
        span, parts = stack_of(chunk)
        total = parts[0]
        for m in range(HID):
            mixed = mixed_of(m, parts)
            total = total + scalars[1][m] * (mixed * sigmoid(mixed))
        dual_new[span] = total
        dual_half[span] = total.astype(BF16)

    repeat(detectors // batch, dual_block)
    for t in range(2):
        dual_out[:, t * TILE : (t + 1) * TILE] = dual_new[
            row * 2 + t, pl.ds(pl.multiple_of(chan * 8, 8), 8), :
        ]

    window = width + 2 * REACH
    tile_low = lax.div(low - REACH + TILE, TILE) - 1
    aligned = width % TILE == 0
    offset = TILE - REACH if aligned else low - REACH - tile_low * TILE
    sides = 3 if aligned else 2

    def backproject(group):
        owners = [group * 8 + o for o in range(8)]

        def add(tile, totals):
            right = jnp.concatenate([block_of(tile, o) for o in owners], axis=0)
            products = dot(dual_half[tile], right, NT)
            out = []
            for o in range(8):
                place_of = tile_of(tile, owners[o]) - tile_low
                product = products[:, o * TILE : (o + 1) * TILE]
                for side in range(sides):
                    out.append(totals[sides * o + side] + jnp.where(place_of == side, product, 0.0))
            return tuple(out)

        totals = tuple(jnp.zeros((16, TILE), F32) for _ in range(8 * sides))
        if detectors <= 16:
            for tile in range(detectors):
                totals = add(tile, totals)
        else:
            totals = lax.fori_loop(0, detectors, add, totals)
        for o in range(8):
            for side in range(sides):
                back[owners[o], side] = totals[sides * o + side]

    repeat(rows_count // 8, backproject)

    lane = iota((3 * 16, TILE), 1)
    clipped = [jnp.clip(tile_low + side, 0, tiles - 1) for side in range(sides)]
    pieces = [None] * (lanes // TILE)
    for y in range(rows_count):
        moved = []
        for side in range(sides):
            halves = halves_of(y, tiles // 2 + (clipped[side] >> 1))
            odd = (clipped[side] & 1) == 1
            merged = jnp.concatenate(
                [
                    vol[y * tiles + clipped[side]].astype(F32),
                    back[y, side].astype(BF16).astype(F32),
                    jnp.where(odd, halves[0][8:], halves[0][:8]),
                    jnp.where(odd, halves[1][8:], halves[1][:8]),
                ],
                axis=0,
            )
            if aligned:
                shift = (y * stride - offset) % TILE
            else:
                shift = lax.rem(y * stride - offset + TILE * (count // TILE + 1), TILE)
            moved.append(pltpu.roll(merged, shift, 1))
        for t in range(y * stride // TILE, (y * stride + window - 1) // TILE + 1):
            column = lane + (t * TILE - y * stride)
            cell = column + (low - REACH)
            inside = (column >= 0) & (column < window) & (cell >= 0) & (cell < cells)
            for side in range(sides):
                least = t * TILE - y * stride + offset
                if aligned and (least + TILE <= side * TILE or least >= (side + 1) * TILE):
                    continue
                taken = jnp.where(inside & ((column + offset) >> 7 == side), moved[side], 0.0)
                pieces[t] = taken if pieces[t] is None else pieces[t] + taken
    for t in range(lanes // TILE):
        field[:, t * TILE : (t + 1) * TILE] = (
            jnp.zeros((3 * 16, TILE), F32) if pieces[t] is None else pieces[t]
        )

    def shift_of(tap):
        return stride * (tap // 3 - 1) + (tap % 3 - 1)

    def rolled(value, amount):
        amount = amount % lanes
        return value if amount == 0 else pltpu.roll(value, amount, 1)

    for tap in range(TAPS):
        for channel in range(2):
            begin = (channel * TAPS + tap) * HID
            part = rolled(field[channel * 16 : (channel + 1) * 16, :], -shift_of(tap))
            col_in[begin : begin + HID, :] = part[:, :count].astype(BF16)
        part = rolled(field[32:48, :], shift_of(tap))
        col_cot[tap * HID : (tap + 1) * HID, :] = part[:, :count].astype(BF16)

    wide = HID * HID
    place_x = iota((stride, wide), 0)
    cell_x = place_x + (low - REACH)
    valid = (cell_x >= 0) & (cell_x < cells)
    own = (place_x >= REACH) & (place_x < REACH + width)

    def masked(mask, value):
        shaped = value.reshape(rows_count, stride, wide)
        return jnp.where(mask[None], shaped, 0.0).reshape(count, wide)

    def widen(target, value, step):
        zero = jnp.zeros((stride, 3 * wide), BF16)
        target[0:stride, :] = zero
        target[stride + count :, :] = zero
        for k, amount in ((0, step), (1, 0), (2, -step)):
            moved = value if amount == 0 else pltpu.roll(value, amount % count, 0)
            target[stride : stride + count, k * wide : (k + 1) * wide] = moved.astype(BF16)

    first_pre = dot(col_in[...], first[...], TN)
    gate = sigmoid(first_pre)
    slope_first[...] = gate * (1.0 + first_pre * (1.0 - gate))
    widen(act_wide, masked(valid, first_pre * gate), 1)
    middle_pre = None
    for dy in range(3):
        for dx in range(3):
            part = dot(
                act_wide[stride * dy : stride * dy + count, dx * wide : (dx + 1) * wide],
                middle[dy, dx * wide : (dx + 1) * wide, :],
                NT,
            )
            middle_pre = part if middle_pre is None else middle_pre + part
    gate = sigmoid(middle_pre)
    slope_middle[...] = gate * (1.0 + middle_pre * (1.0 - gate))
    middle_act = masked(valid, middle_pre * gate)
    middle_half = middle_act.astype(BF16)

    def gather_taps(products, sign):
        padded = jnp.concatenate([products, jnp.zeros((TAPS * HID, pad), F32)], axis=1)
        total = None
        for tap in range(TAPS):
            part = rolled(padded[tap * HID : (tap + 1) * HID], sign * shift_of(tap))
            total = part if total is None else total + part
        return total

    def rows_to_tiles(value, target):
        lane_one = iota((16, TILE), 1)
        for y in range(rows_count):
            begin = y * stride + REACH
            merged = None
            for t in range(begin // TILE, (begin + width - 1) // TILE + 1):
                column = lane_one + t * TILE
                inside = (column >= begin) & (column < begin + width)
                part = jnp.where(inside, value[:, t * TILE : (t + 1) * TILE], 0.0)
                merged = part if merged is None else merged + part
            if aligned:
                shift = -begin % TILE
            else:
                shift = lax.rem(low - begin + TILE * (count // TILE + 1), TILE)
            target(y, pltpu.roll(merged, shift, 1))

    update = gather_taps(dot(last[...], middle_half, NT), -1) + field[0:16, :]

    def put_row(y, tile):
        row_tiles[y] = tile

    rows_to_tiles(update, put_row)

    middle_grad = masked(valid, dot(col_cot[...], last[...], TN) * slope_middle[...])
    grad_last = dot(col_cot[...], masked(own, middle_act).astype(BF16))
    widen(grad_wide, middle_grad, -1)
    turned = jnp.transpose(masked(own, middle_grad)).astype(BF16)
    grads_middle = [
        dot(turned, act_wide[stride * dy : stride * dy + count, :]) for dy in range(3)
    ]
    first_sum = None
    for dy in range(3):
        part = dot(grad_wide[stride * (2 - dy) : stride * (2 - dy) + count, :], middle[dy])
        first_sum = part if first_sum is None else first_sum + part
    first_grad = masked(valid, first_sum * slope_first[...])
    first_half = first_grad.astype(BF16)
    turned = jnp.transpose(masked(own, first_grad)).astype(BF16)
    grad_first = dot(turned, col_in[...], NT)
    back_grad = gather_taps(dot(first[TAPS * HID :, :], first_half, NT), 1)

    def put_grad(y, tile):
        grad_tiles[y, 0] = jnp.zeros((16, TILE), BF16)
        grad_tiles[y, 1] = tile.astype(BF16)

    rows_to_tiles(back_grad, put_grad)

    lane_z = iota((HID, wide), 1) >> 4
    lane_group = iota((HID, TILE), 1) >> 4
    out_tiles = [jnp.zeros((HID, TILE), F32) for _ in range(4)]

    def fold_lanes(value):
        value = value[:, :TILE] + value[:, TILE:]
        for amount in (64, 32, 16):
            value = value + pltpu.roll(value, amount, 1)
        return value

    def put(index, value):
        group = index // 8
        out_tiles[group] = jnp.where(lane_group == index % 8, value, out_tiles[group])

    for tap in range(TAPS):
        plane = grads_middle[tap // 3][:, (tap % 3) * wide : (tap % 3 + 1) * wide]
        for depth in range(3):
            total = jnp.zeros((HID, wide), F32)
            for z in range(HID):
                total = total + jnp.where(lane_z == z + depth - 1, plane[z * HID : (z + 1) * HID], 0.0)
            put(depth * TAPS + tap, fold_lanes(total))

    lane_in = iota((HID, 2 * TAPS * HID), 1) & (HID - 1)
    folds = []
    for depth in range(3):
        total = jnp.zeros((HID, 2 * TAPS * HID), F32)
        for z in range(HID):
            total = total + jnp.where(lane_in == z + depth - 1, grad_first[z * HID : (z + 1) * HID], 0.0)
        folds.append(total)
    source = iota((2 * TAPS * HID, TILE), 0) >> 4
    target = iota((2 * TAPS * HID, TILE), 1)
    for depth in range(3):
        channel = (source >= TAPS).astype(jnp.int32)
        fold = (target == 48 + (depth * TAPS + source - TAPS * channel) * 2 + channel).astype(F32)
        out_tiles[3] = out_tiles[3] + dot(folds[depth], fold, precision=lax.Precision.HIGHEST)

    row_z = iota((HID, wide), 0)
    lines = []
    for depth in range(3):
        keep_last = lane_z == row_z + depth - 1
        for tap in range(TAPS):
            part = jnp.where(keep_last, grad_last[tap * HID : (tap + 1) * HID], 0.0)
            lines.append(jnp.sum(part, axis=0, keepdims=True))
    lines.append(jnp.zeros((32 - 27, wide), F32))
    lines = fold_lanes(jnp.concatenate(lines, axis=0))
    row_eight = iota((8, TILE), 0)
    packed_last = jnp.zeros((8, TILE), F32)
    for r in range(4):
        picked = jnp.where(row_eight == iota((8, TILE), 1) >> 4, lines[r * 8 : (r + 1) * 8], 0.0)
        packed_last = jnp.where(
            row_eight == r, jnp.sum(picked, axis=0, keepdims=True), packed_last
        )

    if whole:
        small = dual_gradients(
            sizes, table, scalars, footprints, proj, dual, meas, grad_tiles, dual_new, sums
        )
    else:
        small = jnp.zeros((8, TILE), F32)

    for t in range(4):
        slope_first[0:HID, 0:TILE] = out_tiles[t]
        keep[t * 8 : (t + 1) * 8, :] = slope_first[pl.ds(pl.multiple_of(chan * 8, 8), 8), 0:TILE]
        send[t * 8 : (t + 1) * 8, :] = slope_first[
            pl.ds(pl.multiple_of((chans - 1 - chan) * 8, 8), 8), 0:TILE
        ]
    for target in (keep, send):
        target[32:40, :] = packed_last
        target[40:48, :] = small

    def put_update(y):
        begin = pl.multiple_of(48 + y * 16, 8)
        tile = row_tiles[update_row(y, row)]
        keep[pl.ds(begin, 16), :] = tile
        send[pl.ds(begin, 16), :] = tile

    repeat(updates, put_update)


def write_grads(chan, grads, middle, first, last, mixing, readout):
    for k in range(27):
        block = grads[(k // 8) * 8 : (k // 8 + 1) * 8]
        block = block if k % 8 == 0 else pltpu.roll(block, TILE - 16 * (k % 8), 1)
        middle[k] = block[:, :HID]
    filled = jnp.concatenate([grads[24:32], jnp.zeros((TILE - 8, TILE), F32)], axis=0)
    turned = jnp.transpose(filled)
    for k in range(27):
        first[k] = turned[48 + 2 * k : 50 + 2 * k, :8]
    block = pltpu.roll(grads[32:40], lax.rem(TILE - 8 * chan, TILE), 1)
    for group in range(8):
        moved = block if group == 0 else pltpu.roll(block, TILE - 16 * group, 1)
        for r in range(4):
            if r * 8 + group < 27:
                last[r * 8 + group] = moved[r : r + 1, :8]
    mixing[...] = grads[41:44, :HID]
    readout[...] = grads[40:41, :HID]


def finish_kernel(row_ref, chan_ref, keep, near, one, two, three, volume, *rest):
    grads, slots = (rest[:-1], rest[-1])
    row = row_ref[0]
    chan = chan_ref[0]
    total = keep[0:48, :] + near[0:48, :] + one[0:48, :] + two[0:48, :] + three[0:48, :]
    write_grads(chan, total, *grads)
    for k, (source, begin) in enumerate(
        ((keep, 48), (near, 48), (one, 48), (one, 64), (two, 48), (two, 64), (three, 48), (three, 64))
    ):
        slots[k] = source[begin : begin + 16, :]
    for tile in range(8):
        volume[:, tile, :] = slots[(((tile >> 1) ^ (row & 3)) << 1) + ((tile & 1) ^ chan)]


def finish_grads_kernel(chan_ref, total, *grads):
    write_grads(chan_ref[0], total[...], *grads)


def row_mask_pairs(devices, mask):
    return [(index, index ^ mask) for index in range(devices)]


def body(
    volume,
    dual_state,
    measured,
    cotangent,
    conv_first,
    conv_middle,
    conv_last,
    dual_mixing,
    dual_readout,
    footprints,
    tile_rows,
    tile_blocks,
):
    views, slabs, chans = (lax.axis_size(a) for a in ALL_AXES)
    rows_count = views * slabs
    devices = rows_count * chans
    cells = volume.shape[2]
    tiles = cells // TILE
    quick = rows_count == 8 and chans == 2 and tiles == 8
    copies = 2 if quick else 1
    width = cells * copies // devices
    stride = -(-(width + 2 * REACH) // 16) * 16
    detectors = tile_rows.shape[0] * tile_rows.shape[1]
    chan = lax.axis_index("chan")
    row = lax.axis_index("view") * slabs + lax.axis_index("slab")

    row_one = row.reshape(1).astype(jnp.int32)
    chan_one = chan.reshape(1).astype(jnp.int32)
    vmem = pl.BlockSpec(memory_space=pltpu.VMEM)
    smem = pl.BlockSpec(memory_space=pltpu.SMEM)
    hbm = pl.BlockSpec(memory_space=pltpu.HBM)
    raw = (
        volume.reshape(16, cells),
        cotangent.reshape(16, cells),
        dual_state.reshape(8, 2 * TILE),
        measured.reshape(8, 2 * TILE),
    )
    payload = pl.pallas_call(
        pack_kernel,
        out_shape=jax.ShapeDtypeStruct((1, tiles + 2, 16, TILE), BF16),
        in_specs=[smem] + [hbm] * 4,
        out_specs=vmem,
        scratch_shapes=[pltpu.VMEM(value.shape, value.dtype) for value in raw]
        + [pltpu.SemaphoreType.DMA((4,))],
        compiler_params=pltpu.CompilerParams(vmem_limit_bytes=4 * MIB),
        name="pack",
    )(chan_one, *(in_hbm(value) for value in raw))

    def swap(value, mask):
        return lax.ppermute(value, ALL_AXES, row_mask_pairs(devices, mask))

    own = own_weights(conv_first, conv_middle, conv_last)
    if quick:
        far_payload = swap(payload, 8)
        other = tuple(swap(value, 1) for value in own)
        payload = jnp.concatenate([payload, far_payload], axis=0)
        payload, other = lax.optimization_barrier((payload, other))
        pieces = [swap(payload, k) for k in (2, 4, 6)]
        weights = build_weights(chan_one, own, other)
        pieces[0], weights = lax.optimization_barrier((pieces[0], weights))
        payload = jnp.concatenate([payload] + pieces, axis=0)
        payload_other = swap(payload, 1)
    else:
        payload = lax.all_gather(payload, ALL_AXES, axis=0, tiled=True)
        payload = payload.reshape(rows_count, chans, *payload.shape[1:])
        payload, payload_other = (payload[:, 0], payload[:, 1])
        weights = build_weights(chan_one, own, tuple(swap(value, 1) for value in own))
    middle, first, last = weights

    def piece_slot(owner, row):
        if not quick:
            return owner
        mask = owner ^ row
        return (mask & 3) * 2 + (mask >> 2)

    def update_row(owner, row):
        return owner ^ row if quick else owner

    def chunk_of(row, chan):
        return ((row & 3) if quick else row) * chans + chan

    def flip_of(chan):
        return chan if quick else 0

    updates = 4 if quick else rows_count
    table = (
        jnp.swapaxes(tile_rows, 2, 3),
        jnp.swapaxes(tile_blocks, 2, 3),
        dual_mixing.T,
        dual_readout,
    )
    count = rows_count * stride
    wide = HID * HID
    moved = 48 + 16 * updates
    pad = -(-(stride + 1) // TILE) * TILE
    limit = (20 if quick else 56) * MIB
    sizes = (rows_count, chans, detectors, tiles, width, stride, cells,
             (piece_slot, update_row, chunk_of, flip_of), updates,
             tile_rows.shape[1])
    outs = [
        ((moved, TILE), F32),
        ((moved, TILE), F32),
        ((8, 2 * TILE), F32),
    ]
    shared = [
        ((detectors, 16, TILE), F32),
        ((detectors, 16, TILE), F32),
        ((detectors, 16, TILE), F32),
        ((rows_count, 2, 16, TILE), BF16),
    ]
    scratch = [
        ((rows_count * tiles, 16, TILE), BF16),
        ((detectors, 16, TILE), BF16),
        ((detectors, 16, TILE), F32),
        ((rows_count, 3, 16, TILE), F32),
        ((48, count + pad), F32),
        ((2 * TAPS * HID, count), BF16),
        ((TAPS * HID, count), BF16),
        ((count + 2 * stride, 3 * wide), BF16),
        ((count + 2 * stride, 3 * wide), BF16),
        ((count, wide), F32),
        ((count, wide), F32),
        ((rows_count, 16, TILE), F32),
        ((4, HID, 8, TILE), F32),
    ]
    if quick:
        scratch = shared + scratch
    else:
        outs = outs + shared
    keep, send, new_dual, *rest = pl.pallas_call(
        functools.partial(main_kernel, sizes, quick),
        out_shape=[jax.ShapeDtypeStruct(*spec) for spec in outs],
        in_specs=[hbm] * 5 + [smem] * 2 + [vmem] * 5,
        out_specs=[vmem] * len(outs),
        scratch_shapes=[pltpu.VMEM(*spec) for spec in scratch]
        + [pltpu.SMEM(value.shape, value.dtype) for value in table]
        + [pltpu.VMEM(footprints.shape, BF16), pltpu.SemaphoreType.DMA((5,))],
        compiler_params=pltpu.CompilerParams(vmem_limit_bytes=limit),
        cost_estimate=pl.CostEstimate(
            flops=5 * 10**9, bytes_accessed=5 * 10**6, transcendentals=2 * 10**6
        ),
        name="primal_dual",
    )(
        *(in_hbm(value) for value in (*table, footprints)),
        row_one,
        chan_one,
        payload,
        payload_other,
        middle,
        first,
        last,
    )

    near = swap(send, 1)
    grad_shapes = [
        jax.ShapeDtypeStruct(shape, F32)
        for shape in ((27, 8, HID), (27, 2, 8), (27, 1, 8), (3, HID), (1, HID))
    ]
    if quick:

        sums = keep[:48] + near[:48]

        def piece(value, index):
            return value[48 + 16 * index : 64 + 16 * index]

        parts = [
            swap(jnp.concatenate([sums, piece(keep, k), piece(near, k)], axis=0), 2 * k)
            for k in (1, 2, 3)
        ]
        new_volume, *grads = pl.pallas_call(
            finish_kernel,
            out_shape=[jax.ShapeDtypeStruct((16, 8, TILE), F32)] + grad_shapes,
            in_specs=[smem, smem] + [vmem] * 5,
            out_specs=[vmem] * 6,
            scratch_shapes=[pltpu.VMEM((8, 16, TILE), F32)],
            compiler_params=pltpu.CompilerParams(vmem_limit_bytes=8 * MIB),
            name="finish",
        )(row_one, chan_one, keep, near, *parts)
    else:
        mine = keep + near
        small = pl.pallas_call(
            functools.partial(dual_gradients_kernel, sizes),
            out_shape=jax.ShapeDtypeStruct((8, TILE), F32),
            in_specs=[smem] * 6 + [vmem] * 5,
            out_specs=vmem,
            scratch_shapes=[
                pltpu.VMEM((detectors, 16, TILE), F32),
                pltpu.VMEM((4, HID, 8, TILE), F32),
            ],
            compiler_params=pltpu.CompilerParams(vmem_limit_bytes=limit),
            name="dual_gradients",
        )(*table, row_one, chan_one, footprints, *rest)
        total = jnp.concatenate(
            [lax.psum(mine[:40], ROW_AXES), lax.psum(small, ALL_AXES)], axis=0
        )
        grads = pl.pallas_call(
            finish_grads_kernel,
            out_shape=grad_shapes,
            in_specs=[smem, vmem],
            out_specs=[vmem] * 5,
            name="finish_grads",
        )(chan_one, total)
        pieces = lax.all_to_all(
            mine[48:].reshape(rows_count, 16, TILE), ROW_AXES, 0, 0, tiled=True
        )
        pieces = pieces.reshape(tiles, rows_count // tiles, 16, TILE).sum(axis=1)
        new_volume = jnp.swapaxes(pieces, 0, 1)

    grad_middle, grad_first, grad_last, grad_mixing, grad_readout = grads
    return (
        new_volume.reshape(volume.shape),
        new_dual.reshape(dual_state.shape),
        grad_first.reshape(3, 3, 3, 2, 8).transpose(4, 3, 0, 1, 2),
        grad_middle.reshape(3, 3, 3, 8, HID).transpose(3, 4, 0, 1, 2),
        grad_last.reshape(3, 3, 3, 1, 8).transpose(3, 4, 0, 1, 2),
        grad_mixing.T,
        grad_readout.reshape(HID),
    )


def solution(mesh):
    placed = (
        P("grp", ("view", "slab"), None),
        P(("grp", "view"), "chan", "slab"),
        P(("grp", "view"), "chan", "slab"),
        P("grp", ("view", "slab"), None),
        P("chan", None, None, None, None),
        P("chan", None, None, None, None),
        P(None, "chan", None, None, None),
        P(),
        P(),
        P(),
        P(),
        P(),
    )
    return jax.shard_map(
        body,
        mesh=mesh,
        in_specs=placed,
        out_specs=(
            P("grp", ("view", "slab"), None),
            P(("grp", "view"), "chan", "slab"),
            P(("grp", "chan"), None, None, None, None),
            P(("grp", "chan"), None, None, None, None),
            P("grp", "chan", None, None, None),
            P("grp", None),
            P("grp"),
        ),
        check_vma=False,
    )
```

```python
import functools

import jax
import jax.numpy as jnp
from jax import lax
from jax.experimental import pallas as pl
from jax.experimental.pallas import tpu as pltpu
from jax.sharding import PartitionSpec as P

F32 = jnp.float32
BF16 = jnp.bfloat16
ALL_AXES = ("view", "slab", "chan")
ROW_AXES = ("view", "slab")
HID = 16
TILE = 128
REACH = 4
TAPS = 9
NN = (((1,), (0,)), ((), ()))
NT = (((1,), (1,)), ((), ()))
TN = (((0,), (0,)), ((), ()))
MIB = 1024 * 1024


def dot(left, right, dims=NN, precision=None):
    return lax.dot_general(left, right, dims, precision=precision, preferred_element_type=F32)


def exact_parts(value):
    high = value.astype(BF16)
    rest = value - high.astype(F32)
    middle = rest.astype(BF16)
    return high, middle, (rest - middle.astype(F32)).astype(BF16)


def iota(shape, dim):
    return lax.broadcasted_iota(jnp.int32, shape, dim)


def repeat(count, step, limit=16):
    if count <= limit:
        for index in range(count):
            step(index)
    else:

        @pl.loop(0, count)
        def unused(index):
            step(index)


def in_hbm(value):
    return pltpu.with_memory_space_constraint(value, pltpu.HBM)


def own_row():
    return lax.axis_index("view") * lax.axis_size("slab") + lax.axis_index("slab")


def fetch(sources, targets, arrivals):
    copies = [
        pltpu.make_async_copy(source, target, arrivals.at[k])
        for k, (source, target) in enumerate(zip(sources, targets))
    ]
    for copy in copies:
        copy.start()
    return copies


def weights_kernel(middle_from, first_from, last_from, footprints_from,
                   rows_from, blocks_from, mixing_from, readout_from,
                   middle_other, first_other, last_other,
                   middle, first, last, footprints, rows, blocks, mixing, readout,
                   middle_own, first_own, last_own, arrivals):
    wide = HID * HID
    copies = fetch(
        (middle_from, first_from, last_from, footprints_from,
         rows_from, blocks_from, mixing_from, readout_from),
        (middle_own, first_own, last_own, footprints, rows, blocks, mixing, readout),
        arrivals,
    )
    for copy in copies[:3]:
        copy.wait()
    chan = lax.axis_index("chan")
    lane_z = iota((HID, wide), 1) >> 4
    row_z = iota((HID, wide), 0)

    spread = ((iota((HID, wide), 1) & (HID - 1)) == iota((HID, wide), 0)).astype(BF16)

    def spread_middle(source):
        rows = jnp.concatenate([source[k].astype(F32) for k in range(27)], axis=0)
        return dot(rows.astype(BF16), spread)

    mine, theirs = (spread_middle(middle_own), spread_middle(middle_other))
    lower = jnp.where(chan == 0, mine, theirs)
    upper = jnp.where(chan == 0, theirs, mine)
    for tap in range(TAPS):
        parts = []
        for depth in range(3):
            begin = (depth * TAPS + tap) * 8
            parts.append(
                jnp.concatenate([lower[begin : begin + 8], upper[begin : begin + 8]], axis=0)
            )
        for z in range(HID):
            block = jnp.where(
                lane_z == z - 1,
                parts[0],
                jnp.where(lane_z == z, parts[1], jnp.where(lane_z == z + 1, parts[2], 0.0)),
            )
            begin = (tap % 3) * wide + z * HID
            middle[tap // 3, begin : begin + HID, :] = block.astype(BF16)

    channel = iota((8, wide), 1) & (HID - 1)
    spread_own = (channel == iota((8, wide), 0) + 8 * chan).astype(BF16)
    spread_other = (channel == iota((8, wide), 0) + 8 * (1 - chan)).astype(BF16)

    def lines(own, other):
        return dot(own, spread_own) + dot(other, spread_other)

    def banded(rows, step):
        out = jnp.zeros((HID, wide), F32)
        for depth, line in enumerate(rows):
            line = jnp.broadcast_to(line, (HID, wide))
            out = jnp.where(row_z - lane_z == step * (depth - 1), line, out)
        return out.astype(BF16)

    first_lines = [lines(first_own[k], first_other[k]) for k in range(27)]
    last_lines = [lines(last_own[k // 3, k % 3], last_other[k // 3, k % 3]) for k in range(9)]
    for tap in range(TAPS):
        for c in range(2):
            begin = (c * TAPS + tap) * HID
            rows = [first_lines[depth * TAPS + tap][c : c + 1] for depth in range(3)]
            first[begin : begin + HID, :] = banded(rows, 1)
        dy, dx = (tap // 3, tap % 3)
        rows = [last_lines[depth * 3 + dy][dx : dx + 1] for depth in range(3)]
        last[tap * HID : (tap + 1) * HID, :] = banded(rows, -1)
    for copy in copies[3:]:
        copy.wait()


def own_weights(conv_first, conv_middle, conv_last):
    return (
        conv_middle.transpose(2, 3, 4, 0, 1).reshape(27, 8, HID),
        conv_first.transpose(2, 3, 4, 1, 0).reshape(27, 2, 8),
        conv_last.transpose(0, 2, 3, 4, 1).reshape(3, 3, 3, 8),
    )


def build_weights(own, other, passed):
    wide = HID * HID
    hbm = pl.BlockSpec(memory_space=pltpu.HBM)
    vmem = pl.BlockSpec(memory_space=pltpu.VMEM)
    return pl.pallas_call(
        weights_kernel,
        out_shape=(
            jax.ShapeDtypeStruct((3, 3 * wide, wide), BF16),
            jax.ShapeDtypeStruct((2 * TAPS * HID, wide), BF16),
            jax.ShapeDtypeStruct((TAPS * HID, wide), BF16),
            *(jax.ShapeDtypeStruct(value.shape, value.dtype) for value in passed),
        ),
        in_specs=[hbm] * 8 + [vmem] * 3,
        out_specs=[vmem] * 8,
        scratch_shapes=[pltpu.VMEM(value.shape, value.dtype) for value in own]
        + [pltpu.SemaphoreType.DMA((8,))],
        compiler_params=pltpu.CompilerParams(vmem_limit_bytes=16 * MIB),
        cost_estimate=pl.CostEstimate(flops=10**8, bytes_accessed=2 * 10**6, transcendentals=0),
        name="band_weights",
    )(*(in_hbm(value) for value in (*own, *passed)), *other)


def sigmoid(value):
    return jax.nn.sigmoid(value)


def projector(sizes, table, footprints):
    rows_count, per_view = (sizes[0], sizes[-1])
    groups = rows_count // 8

    def tile_of(tile, owner):
        return table[0][tile // per_view, tile % per_view, 0, owner]

    def block_of(tile, owner):
        return footprints[table[1][tile // per_view, tile % per_view, 0, owner]]

    def project(tile, pick):
        def one(group):
            owners = [group * 8 + o for o in range(8)]
            left = jnp.concatenate([pick(tile, o) for o in owners], axis=1)
            right = jnp.concatenate([block_of(tile, o) for o in owners], axis=0)
            return dot(left, right)

        if groups == 1:
            return one(0)
        return lax.fori_loop(0, groups, lambda g, a: a + one(g), jnp.zeros((16, TILE), F32))

    return tile_of, block_of, project


def dual_reader(scalars, proj, dual, meas):
    batch = 4

    def mixed_of(m, parts):
        return scalars[0][0, m] * parts[0] + scalars[0][1, m] * parts[1] + scalars[0][2, m] * parts[2]

    def stack_of(chunk):
        span = pl.ds(chunk * batch, batch)
        return span, (dual[span], proj[span], meas[span])

    return batch, mixed_of, stack_of


def dual_gradients(sizes, table, scalars, footprints, proj, dual, meas, grad_tiles, grad, sums,
                   cache=()):
    detectors, width = (sizes[2], sizes[4])
    own_tile = lax.div(sizes[7][2](own_row(), lax.axis_index("chan")) * width, TILE)
    tile_of, _, project = projector(sizes, table, footprints)
    batch, mixed_of, stack_of = dual_reader(scalars, proj, dual, meas)

    def project_grad(tile):
        def pick(t, o):
            return grad_tiles[o, (tile_of(t, o) == own_tile).astype(jnp.int32)]

        grad[tile] = project(tile, pick)

    repeat(detectors, project_grad)
    sums[...] = jnp.zeros_like(sums)

    def dual_sums(chunk):
        span, parts = stack_of(chunk)
        pulled = grad[span]
        weighted = [pulled * part for part in parts]
        for m in range(HID):
            if cache:
                active, slope = (cache[0][m, span], cache[1][m, span])
            else:
                mixed = mixed_of(m, parts)
                gate = sigmoid(mixed)
                active = mixed * gate
                slope = gate * (1.0 + (mixed - active))
            terms = [pulled * active] + [value * slope for value in weighted]
            for k, term in enumerate(terms):
                sums[k, m] += jnp.sum(term.reshape(batch * 2, 8, TILE), axis=0)

    repeat(detectors // batch, dual_sums)

    eight = 4 * HID * 8
    ones = jnp.ones((TILE, TILE), BF16)
    lines = sum(dot(part, ones) for part in exact_parts(sums[...].reshape(eight, TILE)))
    lane = iota((8, TILE), 1)
    out = jnp.zeros((8, TILE), F32)
    for k in range(4 * HID):
        out = jnp.where(lane == k, lines[8 * k : 8 * k + 8], out)
    return out


def dual_gradients_kernel(sizes, rows_ref, blocks_ref, mixing, readout,
                          footprints, proj, dual, meas, grad_tiles, out, grad, sums):
    table = (rows_ref, blocks_ref)
    out[...] = dual_gradients(
        sizes, table, (mixing, readout), footprints, proj, dual, meas, grad_tiles, grad, sums
    )


def pack_kernel(routed, volume_from, cotangent_from, dual_from, measured_from,
                out, volume, cotangent, dual, measured, arrivals):
    copies = fetch(
        (volume_from, cotangent_from, dual_from, measured_from),
        (volume, cotangent, dual, measured),
        arrivals,
    )
    chan = lax.axis_index("chan")
    row = own_row()
    tiles = volume.shape[1] // TILE
    near = tiles // 2

    def pair(value):
        return jnp.concatenate([value[:, :TILE], value[:, TILE:]], axis=0).astype(BF16)

    def tile_at(source, index):
        return source[:, pl.ds(pl.multiple_of(index * TILE, TILE), TILE)]

    for copy in copies:
        copy.wait()
    for k in range(near):
        out[0, k] = tile_at(volume, chan * near + k)
    out[0, near] = pair(dual[...].astype(F32))
    out[0, near + 1] = pair(measured[...].astype(F32))
    if not routed:
        for k in range(near):
            out[0, near + 2 + k] = tile_at(cotangent, chan * near + k)
        return
    lane = iota((16, TILE), 1)
    beside = jnp.zeros((16, TILE), F32)
    for k in range(4):
        out[0, near + 2 + k] = tile_at(cotangent, (((row & 3) ^ k) << 1) + chan)
        lower = tile_at(cotangent, jnp.maximum(2 * k + chan - 1, 0)).astype(F32)
        upper = tile_at(cotangent, jnp.minimum(2 * k + chan + 1, tiles - 1)).astype(F32)
        spot = jnp.where(lane >= TILE // 2, lower, upper)
        spot = spot if k == 0 else pltpu.roll(spot, 32 * k, 1)
        first = (32 * k - REACH) % TILE
        mine = (lane >= 32 * k) & (lane < 32 * k + REACH) | (lane >= first) & (lane < first + REACH)
        beside = jnp.where(mine, spot, beside)
    out[0, near + 6] = beside.astype(BF16)


def main_kernel(sizes, whole, rows_from, blocks_from, mixing_from, readout_from,
                payload, payload_other, routed, middle, first, last, footprints,
                keep, send, dual_out, proj, dual, meas, grad_tiles,
                vol, dual_half, dual_new, back, field, col_in, col_cot,
                act_wide, grad_wide, slope_first, slope_middle, row_tiles, sums,
                rows_ref, blocks_ref, mixing, readout, arrivals, *cache):
    rows_count, chans, detectors, tiles, width, stride, cells, places, updates, _ = sizes
    piece_slot, update_row, chunk_of, flip_of = places
    copies = fetch(
        (rows_from, blocks_from, mixing_from, readout_from),
        (rows_ref, blocks_ref, mixing, readout),
        arrivals,
    )
    table = (rows_ref, blocks_ref)
    scalars = (mixing, readout)
    row = own_row()
    chan = lax.axis_index("chan")
    low = chunk_of(row, chan) * width
    count = rows_count * stride
    pad = -(-(stride + 1) // TILE) * TILE
    lanes = count + pad

    flip = flip_of(chan)

    near = tiles // 2

    def place(owner):
        slot = piece_slot(owner, row)
        for source, part in ((payload, flip), (payload_other, 1 - flip)):
            for k in range(near):
                vol[owner * tiles + part * near + k] = source[slot, k]
            span = pl.ds(pl.multiple_of(part * 8, 8), 8)
            for k, target in ((near, dual), (near + 1, meas)):
                piece = source[slot, k].astype(F32)
                for t in range(2):
                    target[owner * 2 + t, span, :] = piece[t * 8 : (t + 1) * 8]

    def cotangent_tile(owner, side, tile):
        slot = piece_slot(owner, row)
        if not whole:
            pair = [source[slot, near + 2 + (tile & (near - 1))] for source in (payload, payload_other)]
            return jnp.where(tile < near, pair[0].astype(F32), pair[1].astype(F32))
        begin = (slot >> 1) * 4 + (slot & 1)
        if side == 1:
            return routed[begin].astype(F32)
        return pltpu.roll(routed[begin + 2].astype(F32), (TILE - 32 * (row & 3)) & (TILE - 1), 1)

    repeat(rows_count, place)

    for copy in copies:
        copy.wait()
    tile_of, block_of, project = projector(sizes, table, footprints)

    def project_volume(tile):
        proj[tile] = project(tile, lambda t, o: vol[o * tiles + tile_of(t, o)])

    repeat(detectors, project_volume)

    batch, mixed_of, stack_of = dual_reader(scalars, proj, dual, meas)

    def dual_block(chunk):
        span, parts = stack_of(chunk)
        total = parts[0]
        for m in range(HID):
            mixed = mixed_of(m, parts)
            gate = sigmoid(mixed)
            active = mixed * gate
            total = total + scalars[1][m] * active
            if whole:
                cache[0][m, span] = active
                cache[1][m, span] = gate * (1.0 + (mixed - active))
        dual_new[span] = total
        dual_half[span] = total.astype(BF16)

    repeat(detectors // batch, dual_block)
    for t in range(2):
        dual_out[:, t * TILE : (t + 1) * TILE] = dual_new[
            row * 2 + t, pl.ds(pl.multiple_of(chan * 8, 8), 8), :
        ]

    window = width + 2 * REACH
    tile_low = lax.div(low - REACH + TILE, TILE) - 1
    aligned = width % TILE == 0
    offset = TILE - REACH if aligned else low - REACH - tile_low * TILE
    sides = 3 if aligned else 2

    def backproject(group):
        owners = [group * 8 + o for o in range(8)]

        def add(tile, totals):
            right = jnp.concatenate([block_of(tile, o) for o in owners], axis=0)
            products = dot(dual_half[tile], right, NT)
            out = []
            for o in range(8):
                place_of = tile_of(tile, owners[o]) - tile_low
                product = products[:, o * TILE : (o + 1) * TILE]
                for side in range(sides):
                    out.append(totals[sides * o + side] + jnp.where(place_of == side, product, 0.0))
            return tuple(out)

        totals = tuple(jnp.zeros((16, TILE), F32) for _ in range(8 * sides))
        if detectors <= 16:
            for tile in range(detectors):
                totals = add(tile, totals)
        else:
            totals = lax.fori_loop(0, detectors, add, totals)
        for o in range(8):
            for side in range(sides):
                back[owners[o], side] = totals[sides * o + side]

    repeat(rows_count // 8, backproject)

    lane = iota((3 * 16, TILE), 1)
    clipped = [jnp.clip(tile_low + side, 0, tiles - 1) for side in range(sides)]
    pieces = [None] * (lanes // TILE)
    for y in range(rows_count):
        moved = []
        for side in range(sides):
            merged = jnp.concatenate(
                [
                    vol[y * tiles + clipped[side]].astype(F32),
                    back[y, side].astype(BF16).astype(F32),
                    cotangent_tile(y, side, clipped[side]),
                ],
                axis=0,
            )
            if aligned:
                shift = (y * stride - offset) % TILE
            else:
                shift = lax.rem(y * stride - offset + TILE * (count // TILE + 1), TILE)
            moved.append(pltpu.roll(merged, shift, 1))
        for t in range(y * stride // TILE, (y * stride + window - 1) // TILE + 1):
            column = lane + (t * TILE - y * stride)
            cell = column + (low - REACH)
            inside = (column >= 0) & (column < window) & (cell >= 0) & (cell < cells)
            for side in range(sides):
                least = t * TILE - y * stride + offset
                if aligned and (least + TILE <= side * TILE or least >= (side + 1) * TILE):
                    continue
                taken = jnp.where(inside & ((column + offset) >> 7 == side), moved[side], 0.0)
                pieces[t] = taken if pieces[t] is None else pieces[t] + taken
    for t in range(lanes // TILE):
        field[:, t * TILE : (t + 1) * TILE] = (
            jnp.zeros((3 * 16, TILE), F32) if pieces[t] is None else pieces[t]
        )

    def shift_of(tap):
        return stride * (tap // 3 - 1) + (tap % 3 - 1)

    def rolled(value, amount):
        amount = amount % lanes
        return value if amount == 0 else pltpu.roll(value, amount, 1)

    for tap in range(TAPS):
        for channel in range(2):
            begin = (channel * TAPS + tap) * HID
            part = rolled(field[channel * 16 : (channel + 1) * 16, :], -shift_of(tap))
            col_in[begin : begin + HID, :] = part[:, :count].astype(BF16)
        part = rolled(field[32:48, :], shift_of(tap))
        col_cot[tap * HID : (tap + 1) * HID, :] = part[:, :count].astype(BF16)

    wide = HID * HID
    place_x = iota((stride, wide), 0)
    cell_x = place_x + (low - REACH)
    valid = (cell_x >= 0) & (cell_x < cells)
    own = (place_x >= REACH) & (place_x < REACH + width)

    def masked(mask, value):
        shaped = value.reshape(rows_count, stride, wide)
        return jnp.where(mask[None], shaped, 0.0).reshape(count, wide)

    def widen(target, value, step):
        zero = jnp.zeros((stride, 3 * wide), BF16)
        target[0:stride, :] = zero
        target[stride + count :, :] = zero
        for k, amount in ((0, step), (1, 0), (2, -step)):
            moved = value if amount == 0 else pltpu.roll(value, amount % count, 0)
            target[stride : stride + count, k * wide : (k + 1) * wide] = moved.astype(BF16)

    first_pre = dot(col_in[...], first[...], TN)
    gate = sigmoid(first_pre)
    slope_first[...] = gate * (1.0 + (first_pre - first_pre * gate))
    widen(act_wide, masked(valid, first_pre * gate), 1)
    middle_pre = None
    for dy in range(3):
        for dx in range(3):
            part = dot(
                act_wide[stride * dy : stride * dy + count, dx * wide : (dx + 1) * wide],
                middle[dy, dx * wide : (dx + 1) * wide, :],
                NT,
            )
            middle_pre = part if middle_pre is None else middle_pre + part
    gate = sigmoid(middle_pre)
    slope_middle[...] = gate * (1.0 + (middle_pre - middle_pre * gate))
    middle_act = masked(valid, middle_pre * gate)
    middle_half = middle_act.astype(BF16)

    def gather_taps(products, sign):
        padded = jnp.concatenate([products, jnp.zeros((TAPS * HID, pad), F32)], axis=1)
        total = None
        for tap in range(TAPS):
            part = rolled(padded[tap * HID : (tap + 1) * HID], sign * shift_of(tap))
            total = part if total is None else total + part
        return total

    def rows_to_tiles(value, target):
        lane_one = iota((16, TILE), 1)
        for y in range(rows_count):
            begin = y * stride + REACH
            merged = None
            for t in range(begin // TILE, (begin + width - 1) // TILE + 1):
                column = lane_one + t * TILE
                inside = (column >= begin) & (column < begin + width)
                part = jnp.where(inside, value[:, t * TILE : (t + 1) * TILE], 0.0)
                merged = part if merged is None else merged + part
            if aligned:
                shift = -begin % TILE
            else:
                shift = lax.rem(low - begin + TILE * (count // TILE + 1), TILE)
            target(y, pltpu.roll(merged, shift, 1))

    update = gather_taps(dot(last[...], middle_half, NT), -1) + field[0:16, :]

    def put_row(y, tile):
        row_tiles[y] = tile

    rows_to_tiles(update, put_row)

    middle_grad = masked(valid, dot(col_cot[...], last[...], TN) * slope_middle[...])
    grad_last = dot(col_cot[...], masked(own, middle_act).astype(BF16))
    widen(grad_wide, middle_grad, -1)
    turned = jnp.transpose(masked(own, middle_grad)).astype(BF16)
    grads_middle = [
        dot(turned, act_wide[stride * dy : stride * dy + count, :]) for dy in range(3)
    ]
    first_sum = None
    for dy in range(3):
        part = dot(grad_wide[stride * (2 - dy) : stride * (2 - dy) + count, :], middle[dy])
        first_sum = part if first_sum is None else first_sum + part
    first_grad = masked(valid, first_sum * slope_first[...])
    first_half = first_grad.astype(BF16)
    turned = jnp.transpose(masked(own, first_grad)).astype(BF16)
    grad_first = dot(turned, col_in[...], NT)
    back_grad = gather_taps(dot(first[TAPS * HID :, :], first_half, NT), 1)

    def put_grad(y, tile):
        grad_tiles[y, 0] = jnp.zeros((16, TILE), BF16)
        grad_tiles[y, 1] = tile.astype(BF16)

    rows_to_tiles(back_grad, put_grad)

    lane_z = iota((HID, wide), 1) >> 4
    lane_group = iota((HID, TILE), 1) >> 4
    out_tiles = [jnp.zeros((HID, TILE), F32) for _ in range(4)]

    def fold_groups(value):
        for amount in (64, 32, 16):
            value = value + pltpu.roll(value, amount, 1)
        return value

    def put(index, value):
        group = index // 8
        out_tiles[group] = jnp.where(lane_group == index % 8, value, out_tiles[group])

    for tap in range(TAPS):
        plane = grads_middle[tap // 3][:, (tap % 3) * wide : (tap % 3 + 1) * wide]
        for depth in range(3):
            total = jnp.zeros((HID, TILE), F32)
            for z in range(max(0, 1 - depth), min(HID, HID + 1 - depth)):
                other = z + depth - 1
                half = other // 8
                block = plane[z * HID : (z + 1) * HID, half * TILE : (half + 1) * TILE]
                total = total + jnp.where(lane_group == other % 8, block, 0.0)
            put(depth * TAPS + tap, fold_groups(total))

    lane_in = iota((HID, 2 * TAPS * HID), 1) & (HID - 1)
    folds = []
    for depth in range(3):
        total = jnp.zeros((HID, 2 * TAPS * HID), F32)
        for z in range(HID):
            total = total + jnp.where(lane_in == z + depth - 1, grad_first[z * HID : (z + 1) * HID], 0.0)
        folds.append(total)
    source = iota((2 * TAPS * HID, TILE), 0) >> 4
    channel = (source >= TAPS).astype(jnp.int32)
    fold = ((source - TAPS * channel) * 2 + channel == iota((2 * TAPS * HID, TILE), 1)).astype(BF16)
    folded = sum(dot(part, fold) for part in exact_parts(jnp.concatenate(folds, axis=0)))
    for depth in range(3):
        block = folded[depth * HID : (depth + 1) * HID]
        out_tiles[3] = out_tiles[3] + pltpu.roll(block, 48 + depth * 2 * TAPS, 1)

    lane_z = iota((HID, wide), 1) >> 4
    row_z = iota((HID, wide), 0)
    lines = []
    for depth in range(3):
        keep_last = lane_z == row_z + depth - 1
        for tap in range(TAPS):
            part = jnp.where(keep_last, grad_last[tap * HID : (tap + 1) * HID], 0.0)
            lines.append(jnp.sum(part, axis=0, keepdims=True))
    lines.append(jnp.zeros((32 - 27, wide), F32))
    lines = jnp.concatenate(lines, axis=0)
    lines = fold_groups(lines[:, :TILE] + lines[:, TILE:])
    row_eight = iota((8, TILE), 0)
    packed_last = jnp.zeros((8, TILE), F32)
    for r in range(4):
        picked = jnp.where(row_eight == iota((8, TILE), 1) >> 4, lines[r * 8 : (r + 1) * 8], 0.0)
        packed_last = jnp.where(
            row_eight == r, jnp.sum(picked, axis=0, keepdims=True), packed_last
        )

    if whole:
        small = dual_gradients(
            sizes, table, scalars, footprints, proj, dual, meas, grad_tiles, dual_new, sums, cache
        )
    else:
        small = jnp.zeros((8, TILE), F32)

    for t in range(4):
        slope_first[0:HID, 0:TILE] = out_tiles[t]
        keep[t * 8 : (t + 1) * 8, :] = slope_first[pl.ds(pl.multiple_of(chan * 8, 8), 8), 0:TILE]
        send[t * 8 : (t + 1) * 8, :] = slope_first[
            pl.ds(pl.multiple_of((chans - 1 - chan) * 8, 8), 8), 0:TILE
        ]
    for target in (keep, send):
        target[32:40, :] = packed_last
        target[40:48, :] = small

    def put_update(y):
        begin = pl.multiple_of(48 + y * 16, 8)
        tile = row_tiles[update_row(y, row)]
        keep[pl.ds(begin, 16), :] = tile
        send[pl.ds(begin, 16), :] = tile

    repeat(updates, put_update)


def write_grads(chan, grads, scale, middle, first, last, mixing, readout):
    for k in range(27):
        block = grads[(k // 8) * 8 : (k // 8 + 1) * 8]
        block = block if k % 8 == 0 else pltpu.roll(block, TILE - 16 * (k % 8), 1)
        middle[k] = block[:, :HID]
    filled = jnp.concatenate([grads[24:32], jnp.zeros((TILE - 8, TILE), F32)], axis=0)
    turned = jnp.transpose(filled)
    for k in range(27):
        first[k] = turned[48 + 2 * k : 50 + 2 * k, :8]
    block = pltpu.roll(grads[32:40], lax.rem(TILE - 8 * chan, TILE), 1)
    for group in range(8):
        moved = block if group == 0 else pltpu.roll(block, TILE - 16 * group, 1)
        for r in range(4):
            if r * 8 + group < 27:
                last[r * 8 + group] = moved[r : r + 1, :8]
    small = jnp.broadcast_to(jnp.sum(grads[40:48], axis=0, keepdims=True), (8, TILE))
    readout[...] = small[0:1, :HID]
    for k in range(3):
        moved = pltpu.roll(small, TILE - HID * (k + 1), 1)
        mixing[k : k + 1, :] = moved[0:1, :HID] * scale[0:1, :HID]


def finish_kernel(scale, keep, near, one, two, three, volume, *rest):
    grads, slots = (rest[:-1], rest[-1])
    row = own_row()
    chan = lax.axis_index("chan")
    total = keep[0:48, :] + near[0:48, :] + one[0:48, :] + two[0:48, :] + three[0:48, :]
    write_grads(chan, total, scale, *grads)
    for k, (source, begin) in enumerate(
        ((keep, 48), (near, 48), (one, 48), (one, 64), (two, 48), (two, 64), (three, 48), (three, 64))
    ):
        slots[k] = source[begin : begin + 16, :]
    for tile in range(8):
        volume[:, tile, :] = slots[(((tile >> 1) ^ (row & 3)) << 1) + ((tile & 1) ^ chan)]


def finish_grads_kernel(scale, total, *grads):
    write_grads(lax.axis_index("chan"), total[...], scale[...], *grads)


def row_mask_pairs(devices, mask):
    return [(index, index ^ mask) for index in range(devices)]


def body(
    volume,
    dual_state,
    measured,
    cotangent,
    conv_first,
    conv_middle,
    conv_last,
    dual_mixing,
    dual_readout,
    footprints,
    tile_rows,
    tile_blocks,
):
    views, slabs, chans = (lax.axis_size(a) for a in ALL_AXES)
    rows_count = views * slabs
    devices = rows_count * chans
    cells = volume.shape[2]
    tiles = cells // TILE
    quick = rows_count == 8 and chans == 2 and tiles == 8
    copies = 2 if quick else 1
    width = cells * copies // devices
    stride = -(-(width + 2 * REACH) // 16) * 16
    detectors = tile_rows.shape[0] * tile_rows.shape[1]

    vmem = pl.BlockSpec(memory_space=pltpu.VMEM)
    smem = pl.BlockSpec(memory_space=pltpu.SMEM)
    hbm = pl.BlockSpec(memory_space=pltpu.HBM)
    raw = (
        volume.reshape(16, cells),
        cotangent.reshape(16, cells),
        dual_state.reshape(8, 2 * TILE),
        measured.reshape(8, 2 * TILE),
    )
    payload = pl.pallas_call(
        functools.partial(pack_kernel, quick),
        out_shape=jax.ShapeDtypeStruct((1, tiles // 2 + 2 + (5 if quick else tiles // 2), 16, TILE), BF16),
        in_specs=[hbm] * 4,
        out_specs=vmem,
        scratch_shapes=[pltpu.VMEM(value.shape, value.dtype) for value in raw]
        + [pltpu.SemaphoreType.DMA((4,))],
        compiler_params=pltpu.CompilerParams(vmem_limit_bytes=4 * MIB),
        name="pack",
    )(*(in_hbm(value) for value in raw))

    def swap(value, mask):
        return lax.ppermute(value, ALL_AXES, row_mask_pairs(devices, mask))

    table = (
        jnp.swapaxes(tile_rows, 2, 3),
        jnp.swapaxes(tile_blocks, 2, 3),
        dual_mixing.T,
        dual_readout,
    )
    own = own_weights(conv_first, conv_middle, conv_last)
    if quick:
        far_payload = swap(payload, 8)
        other = tuple(swap(value, 1) for value in own)
        payload, far_payload, other = lax.optimization_barrier((payload, far_payload, other))

        def bound_for(k):
            sources = (payload[0], far_payload[0])
            return jnp.concatenate(
                [source[:6] for source in sources]
                + [source[6 + k : 7 + k] for source in sources]
                + [source[10:] for source in sources],
                axis=0,
            )

        pieces = [swap(bound_for(k), 2 * k) for k in (1, 2, 3)]
        weights = build_weights(own, other, (footprints, *table))
        pieces[0], weights = lax.optimization_barrier((pieces[0], weights))
        pieces = [bound_for(0)] + pieces
        payload = jnp.concatenate([piece[:12] for piece in pieces], axis=0)
        payload = payload.reshape(rows_count, 6, 16, TILE)
        routed = jnp.concatenate([piece[12:] for piece in pieces], axis=0)
        payload_other = swap(payload, 1)
    else:
        payload = lax.all_gather(payload, ALL_AXES, axis=0, tiled=True)
        payload = payload.reshape(rows_count, chans, *payload.shape[1:])
        payload, payload_other = (payload[:, 0], payload[:, 1])
        routed = payload[0, :1]
        weights = build_weights(
            own, tuple(swap(value, 1) for value in own), (footprints, *table)
        )
    middle, first, last, footprints, *table = weights

    def piece_slot(owner, row):
        if not quick:
            return owner
        mask = owner ^ row
        return (mask & 3) * 2 + (mask >> 2)

    def update_row(owner, row):
        return owner ^ row if quick else owner

    def chunk_of(row, chan):
        return ((row & 3) if quick else row) * chans + chan

    def flip_of(chan):
        return chan if quick else 0

    updates = 4 if quick else rows_count
    count = rows_count * stride
    wide = HID * HID
    moved = 48 + 16 * updates
    pad = -(-(stride + 1) // TILE) * TILE
    limit = (24 if quick else 56) * MIB
    sizes = (rows_count, chans, detectors, tiles, width, stride, cells,
             (piece_slot, update_row, chunk_of, flip_of), updates,
             tile_rows.shape[1])
    outs = [
        ((moved, TILE), F32),
        ((moved, TILE), F32),
        ((8, 2 * TILE), F32),
    ]
    shared = [
        ((detectors, 16, TILE), F32),
        ((detectors, 16, TILE), F32),
        ((detectors, 16, TILE), F32),
        ((rows_count, 2, 16, TILE), BF16),
    ]
    scratch = [
        ((rows_count * tiles, 16, TILE), BF16),
        ((detectors, 16, TILE), BF16),
        ((detectors, 16, TILE), F32),
        ((rows_count, 3, 16, TILE), F32),
        ((48, count + pad), F32),
        ((2 * TAPS * HID, count), BF16),
        ((TAPS * HID, count), BF16),
        ((count + 2 * stride, 3 * wide), BF16),
        ((count + 2 * stride, 3 * wide), BF16),
        ((count, wide), F32),
        ((count, wide), F32),
        ((rows_count, 16, TILE), F32),
        ((4, HID, 8, TILE), F32),
    ]
    if quick:
        scratch = shared + scratch
    else:
        outs = outs + shared
    keep, send, new_dual, *rest = pl.pallas_call(
        functools.partial(main_kernel, sizes, quick),
        out_shape=[jax.ShapeDtypeStruct(*spec) for spec in outs],
        in_specs=[vmem] * 11,
        out_specs=[vmem] * len(outs),
        scratch_shapes=[pltpu.VMEM(*spec) for spec in scratch]
        + [pltpu.SMEM(value.shape, value.dtype) for value in table]
        + [pltpu.SemaphoreType.DMA((4,))]
        + [pltpu.VMEM((HID, detectors, 16, TILE), F32) for _ in range(2 if quick else 0)],
        compiler_params=pltpu.CompilerParams(vmem_limit_bytes=limit),
        cost_estimate=pl.CostEstimate(
            flops=5 * 10**9, bytes_accessed=5 * 10**6, transcendentals=2 * 10**6
        ),
        name="primal_dual",
    )(
        *table,
        payload,
        payload_other,
        routed,
        middle,
        first,
        last,
        footprints,
    )

    near = swap(send, 1)
    scale = dual_readout.reshape(1, HID)
    grad_shapes = [
        jax.ShapeDtypeStruct(shape, F32)
        for shape in ((27, 8, HID), (27, 2, 8), (27, 1, 8), (3, HID), (1, HID))
    ]
    if quick:

        sums = keep[:48] + near[:48]

        def piece(value, index):
            return value[48 + 16 * index : 64 + 16 * index]

        parts = [
            swap(jnp.concatenate([sums, piece(keep, k), piece(near, k)], axis=0), 2 * k)
            for k in (1, 2, 3)
        ]
        new_volume, *grads = pl.pallas_call(
            finish_kernel,
            out_shape=[jax.ShapeDtypeStruct((16, 8, TILE), F32)] + grad_shapes,
            in_specs=[vmem] * 6,
            out_specs=[vmem] * 6,
            scratch_shapes=[pltpu.VMEM((8, 16, TILE), F32)],
            compiler_params=pltpu.CompilerParams(vmem_limit_bytes=8 * MIB),
            name="finish",
        )(scale, keep, near, *parts)
    else:
        mine = keep + near
        small = pl.pallas_call(
            functools.partial(dual_gradients_kernel, sizes),
            out_shape=jax.ShapeDtypeStruct((8, TILE), F32),
            in_specs=[smem] * 4 + [vmem] * 5,
            out_specs=vmem,
            scratch_shapes=[
                pltpu.VMEM((detectors, 16, TILE), F32),
                pltpu.VMEM((4, HID, 8, TILE), F32),
            ],
            compiler_params=pltpu.CompilerParams(vmem_limit_bytes=limit),
            name="dual_gradients",
        )(*table, footprints, *rest)
        total = jnp.concatenate(
            [lax.psum(mine[:40], ROW_AXES), lax.psum(small, ALL_AXES)], axis=0
        )
        grads = pl.pallas_call(
            finish_grads_kernel,
            out_shape=grad_shapes,
            in_specs=[vmem, vmem],
            out_specs=[vmem] * 5,
            name="finish_grads",
        )(scale, total)
        pieces = lax.all_to_all(
            mine[48:].reshape(rows_count, 16, TILE), ROW_AXES, 0, 0, tiled=True
        )
        pieces = pieces.reshape(tiles, rows_count // tiles, 16, TILE).sum(axis=1)
        new_volume = jnp.swapaxes(pieces, 0, 1)

    grad_middle, grad_first, grad_last, grad_mixing, grad_readout = grads
    return (
        new_volume.reshape(volume.shape),
        new_dual.reshape(dual_state.shape),
        grad_first.reshape(3, 3, 3, 2, 8).transpose(4, 3, 0, 1, 2),
        grad_middle.reshape(3, 3, 3, 8, HID).transpose(3, 4, 0, 1, 2),
        grad_last.reshape(3, 3, 3, 1, 8).transpose(3, 4, 0, 1, 2),
        grad_mixing.T,
        grad_readout.reshape(HID),
    )


def solution(mesh):
    placed = (
        P("grp", ("view", "slab"), None),
        P(("grp", "view"), "chan", "slab"),
        P(("grp", "view"), "chan", "slab"),
        P("grp", ("view", "slab"), None),
        P("chan", None, None, None, None),
        P("chan", None, None, None, None),
        P(None, "chan", None, None, None),
        P(),
        P(),
        P(),
        P(),
        P(),
    )
    return jax.shard_map(
        body,
        mesh=mesh,
        in_specs=placed,
        out_specs=(
            P("grp", ("view", "slab"), None),
            P(("grp", "view"), "chan", "slab"),
            P(("grp", "chan"), None, None, None, None),
            P(("grp", "chan"), None, None, None, None),
            P("grp", "chan", None, None, None),
            P("grp", None),
            P("grp"),
        ),
        check_vma=False,
    )
```

```python
import functools

import jax
import jax.numpy as jnp
from jax import lax
from jax.experimental import pallas as pl
from jax.experimental.pallas import tpu as pltpu
from jax.sharding import PartitionSpec as P

F32 = jnp.float32
BF16 = jnp.bfloat16
ALL_AXES = ("view", "slab", "chan")
ROW_AXES = ("view", "slab")
HID = 16
TILE = 128
REACH = 4
TAPS = 9
NN = (((1,), (0,)), ((), ()))
NT = (((1,), (1,)), ((), ()))
TN = (((0,), (0,)), ((), ()))
MIB = 1024 * 1024


def dot(left, right, dims=NN, precision=None):
    return lax.dot_general(left, right, dims, precision=precision, preferred_element_type=F32)


def exact_parts(value):
    high = value.astype(BF16)
    rest = value - high.astype(F32)
    middle = rest.astype(BF16)
    return high, middle, (rest - middle.astype(F32)).astype(BF16)


def iota(shape, dim):
    return lax.broadcasted_iota(jnp.int32, shape, dim)


def repeat(count, step, limit=16):
    if count <= limit:
        for index in range(count):
            step(index)
    else:

        @pl.loop(0, count)
        def unused(index):
            step(index)


def in_hbm(value):
    return pltpu.with_memory_space_constraint(value, pltpu.HBM)


def own_row():
    return lax.axis_index("view") * lax.axis_size("slab") + lax.axis_index("slab")


def fetch(sources, targets, arrivals):
    copies = [
        pltpu.make_async_copy(source, target, arrivals.at[k])
        for k, (source, target) in enumerate(zip(sources, targets))
    ]
    for copy in copies:
        copy.start()
    return copies


def weights_kernel(middle_from, first_from, last_from, footprints_from,
                   rows_from, blocks_from, mixing_from, readout_from,
                   middle_other, first_other, last_other,
                   middle, first, last, footprints, rows, blocks, mixing, readout,
                   middle_own, first_own, last_own, arrivals):
    wide = HID * HID
    copies = fetch(
        (middle_from, first_from, last_from, footprints_from,
         rows_from, blocks_from, mixing_from, readout_from),
        (middle_own, first_own, last_own, footprints, rows, blocks, mixing, readout),
        arrivals,
    )
    for copy in copies[:3]:
        copy.wait()
    chan = lax.axis_index("chan")
    lane_z = iota((HID, wide), 1) >> 4
    row_z = iota((HID, wide), 0)

    spread = ((iota((HID, wide), 1) & (HID - 1)) == iota((HID, wide), 0)).astype(BF16)

    def spread_middle(source):
        rows = jnp.concatenate([source[k].astype(F32) for k in range(27)], axis=0)
        return dot(rows.astype(BF16), spread)

    mine, theirs = (spread_middle(middle_own), spread_middle(middle_other))
    lower = jnp.where(chan == 0, mine, theirs)
    upper = jnp.where(chan == 0, theirs, mine)
    for tap in range(TAPS):
        parts = []
        for depth in range(3):
            begin = (depth * TAPS + tap) * 8
            parts.append(
                jnp.concatenate([lower[begin : begin + 8], upper[begin : begin + 8]], axis=0)
            )
        for z in range(HID):
            block = jnp.where(
                lane_z == z - 1,
                parts[0],
                jnp.where(lane_z == z, parts[1], jnp.where(lane_z == z + 1, parts[2], 0.0)),
            )
            begin = (tap % 3) * wide + z * HID
            middle[tap // 3, begin : begin + HID, :] = block.astype(BF16)

    channel = iota((8, wide), 1) & (HID - 1)
    spread_own = (channel == iota((8, wide), 0) + 8 * chan).astype(BF16)
    spread_other = (channel == iota((8, wide), 0) + 8 * (1 - chan)).astype(BF16)

    def lines(own, other):
        return dot(own, spread_own) + dot(other, spread_other)

    def banded(rows, step):
        out = jnp.zeros((HID, wide), F32)
        for depth, line in enumerate(rows):
            line = jnp.broadcast_to(line, (HID, wide))
            out = jnp.where(row_z - lane_z == step * (depth - 1), line, out)
        return out.astype(BF16)

    first_lines = [lines(first_own[k], first_other[k]) for k in range(27)]
    last_lines = [lines(last_own[k // 3, k % 3], last_other[k // 3, k % 3]) for k in range(9)]
    for tap in range(TAPS):
        for c in range(2):
            begin = (c * TAPS + tap) * HID
            rows = [first_lines[depth * TAPS + tap][c : c + 1] for depth in range(3)]
            first[begin : begin + HID, :] = banded(rows, 1)
        dy, dx = (tap // 3, tap % 3)
        rows = [last_lines[depth * 3 + dy][dx : dx + 1] for depth in range(3)]
        last[tap * HID : (tap + 1) * HID, :] = banded(rows, -1)
    for copy in copies[3:]:
        copy.wait()


def own_weights(conv_first, conv_middle, conv_last):
    return (
        conv_middle.transpose(2, 3, 4, 0, 1).reshape(27, 8, HID),
        conv_first.transpose(2, 3, 4, 1, 0).reshape(27, 2, 8),
        conv_last.transpose(0, 2, 3, 4, 1).reshape(3, 3, 3, 8),
    )


def build_weights(own, other, passed):
    wide = HID * HID
    hbm = pl.BlockSpec(memory_space=pltpu.HBM)
    vmem = pl.BlockSpec(memory_space=pltpu.VMEM)
    return pl.pallas_call(
        weights_kernel,
        out_shape=(
            jax.ShapeDtypeStruct((3, 3 * wide, wide), BF16),
            jax.ShapeDtypeStruct((2 * TAPS * HID, wide), BF16),
            jax.ShapeDtypeStruct((TAPS * HID, wide), BF16),
            *(jax.ShapeDtypeStruct(value.shape, value.dtype) for value in passed),
        ),
        in_specs=[hbm] * 8 + [vmem] * 3,
        out_specs=[vmem] * 8,
        scratch_shapes=[pltpu.VMEM(value.shape, value.dtype) for value in own]
        + [pltpu.SemaphoreType.DMA((8,))],
        compiler_params=pltpu.CompilerParams(vmem_limit_bytes=16 * MIB),
        cost_estimate=pl.CostEstimate(flops=10**8, bytes_accessed=2 * 10**6, transcendentals=0),
        name="band_weights",
    )(*(in_hbm(value) for value in (*own, *passed)), *other)


def sigmoid(value):
    return jax.nn.sigmoid(value)


def projector(sizes, table, footprints):
    rows_count, per_view = (sizes[0], sizes[-1])
    groups = rows_count // 8

    def tile_of(tile, owner):
        return table[0][tile // per_view, tile % per_view, 0, owner]

    def block_of(tile, owner):
        return footprints[table[1][tile // per_view, tile % per_view, 0, owner]]

    def project(tile, pick):
        def one(group):
            owners = [group * 8 + o for o in range(8)]
            left = jnp.concatenate([pick(tile, o) for o in owners], axis=1)
            right = jnp.concatenate([block_of(tile, o) for o in owners], axis=0)
            return dot(left, right)

        if groups == 1:
            return one(0)
        return lax.fori_loop(0, groups, lambda g, a: a + one(g), jnp.zeros((16, TILE), F32))

    return tile_of, block_of, project


def dual_reader(scalars, proj, dual, meas):
    batch = 4

    def mixed_of(m, parts):
        return scalars[0][0, m] * parts[0] + scalars[0][1, m] * parts[1] + scalars[0][2, m] * parts[2]

    def stack_of(chunk):
        span = pl.ds(chunk * batch, batch)
        return span, (dual[span], proj[span], meas[span])

    return batch, mixed_of, stack_of


def dual_gradients(sizes, table, scalars, footprints, proj, dual, meas, grad_tiles, grad, sums,
                   cache=()):
    detectors, width = (sizes[2], sizes[4])
    own_tile = lax.div(sizes[7][2](own_row(), lax.axis_index("chan")) * width, TILE)
    tile_of, _, project = projector(sizes, table, footprints)
    batch, mixed_of, stack_of = dual_reader(scalars, proj, dual, meas)

    def project_grad(tile):
        def pick(t, o):
            return grad_tiles[o, (tile_of(t, o) == own_tile).astype(jnp.int32)]

        grad[tile] = project(tile, pick)

    repeat(detectors, project_grad)
    sums[...] = jnp.zeros_like(sums)

    def dual_sums(chunk):
        span, parts = stack_of(chunk)
        pulled = grad[span]
        weighted = [pulled * part for part in parts]
        for m in range(HID):
            if cache:
                active, slope = (cache[0][m, span], cache[1][m, span])
            else:
                mixed = mixed_of(m, parts)
                gate = sigmoid(mixed)
                active = mixed * gate
                slope = gate * (1.0 + (mixed - active))
            terms = [pulled * active] + [value * slope for value in weighted]
            for k, term in enumerate(terms):
                sums[k, m] += jnp.sum(term.reshape(batch * 2, 8, TILE), axis=0)

    repeat(detectors // batch, dual_sums)

    eight = 4 * HID * 8
    ones = jnp.ones((TILE, TILE), BF16)
    lines = sum(dot(part, ones) for part in exact_parts(sums[...].reshape(eight, TILE)))
    lane = iota((8, TILE), 1)
    out = jnp.zeros((8, TILE), F32)
    for k in range(4 * HID):
        out = jnp.where(lane == k, lines[8 * k : 8 * k + 8], out)
    return out


def dual_gradients_kernel(sizes, rows_ref, blocks_ref, mixing, readout,
                          footprints, proj, dual, meas, grad_tiles, out, grad, sums):
    table = (rows_ref, blocks_ref)
    out[...] = dual_gradients(
        sizes, table, (mixing, readout), footprints, proj, dual, meas, grad_tiles, grad, sums
    )


def pack_kernel(routed, volume_from, cotangent_from, dual_from, measured_from,
                out, volume, cotangent, dual, measured, arrivals):
    copies = fetch(
        (volume_from, cotangent_from, dual_from, measured_from),
        (volume, cotangent, dual, measured),
        arrivals,
    )
    chan = lax.axis_index("chan")
    row = own_row()
    tiles = volume.shape[1] // TILE
    near = tiles // 2

    def pair(value):
        return jnp.concatenate([value[:, :TILE], value[:, TILE:]], axis=0).astype(BF16)

    def tile_at(source, index):
        return source[:, pl.ds(pl.multiple_of(index * TILE, TILE), TILE)]

    for copy in copies:
        copy.wait()
    for k in range(near):
        out[0, k] = tile_at(volume, chan * near + k)
    out[0, near] = pair(dual[...].astype(F32))
    out[0, near + 1] = pair(measured[...].astype(F32))
    if not routed:
        for k in range(near):
            out[0, near + 2 + k] = tile_at(cotangent, chan * near + k)
        return
    lane = iota((16, TILE), 1)
    beside = jnp.zeros((16, TILE), F32)
    for k in range(4):
        out[0, near + 2 + k] = tile_at(cotangent, (((row & 3) ^ k) << 1) + chan)
        lower = tile_at(cotangent, jnp.maximum(2 * k + chan - 1, 0)).astype(F32)
        upper = tile_at(cotangent, jnp.minimum(2 * k + chan + 1, tiles - 1)).astype(F32)
        spot = jnp.where(lane >= TILE // 2, lower, upper)
        spot = spot if k == 0 else pltpu.roll(spot, 32 * k, 1)
        first = (32 * k - REACH) % TILE
        mine = (lane >= 32 * k) & (lane < 32 * k + REACH) | (lane >= first) & (lane < first + REACH)
        beside = jnp.where(mine, spot, beside)
    out[0, near + 6] = beside.astype(BF16)


def main_kernel(sizes, whole, rows_from, blocks_from, mixing_from, readout_from,
                payload, payload_other, routed, middle, first, last, footprints,
                keep, send, dual_out, proj, dual, meas, grad_tiles,
                vol, dual_half, dual_new, back, field, col_in, col_cot,
                act_wide, grad_wide, slope_first, slope_middle, row_tiles, sums,
                rows_ref, blocks_ref, mixing, readout, arrivals, *cache):
    rows_count, chans, detectors, tiles, width, stride, cells, places, updates, _ = sizes
    piece_slot, update_row, chunk_of, flip_of = places
    copies = fetch(
        (rows_from, blocks_from, mixing_from, readout_from),
        (rows_ref, blocks_ref, mixing, readout),
        arrivals,
    )
    table = (rows_ref, blocks_ref)
    scalars = (mixing, readout)
    row = own_row()
    chan = lax.axis_index("chan")
    low = chunk_of(row, chan) * width
    count = rows_count * stride
    pad = -(-(stride + 1) // TILE) * TILE
    lanes = count + pad

    flip = flip_of(chan)

    near = tiles // 2

    def place(owner):
        slot = piece_slot(owner, row)
        for source, part in ((payload, flip), (payload_other, 1 - flip)):
            for k in range(near):
                vol[owner * tiles + part * near + k] = source[slot, k]
            span = pl.ds(pl.multiple_of(part * 8, 8), 8)
            for k, target in ((near, dual), (near + 1, meas)):
                piece = source[slot, k].astype(F32)
                for t in range(2):
                    target[owner * 2 + t, span, :] = piece[t * 8 : (t + 1) * 8]

    def cotangent_tile(owner, side, tile):
        slot = piece_slot(owner, row)
        if not whole:
            pair = [source[slot, near + 2 + (tile & (near - 1))] for source in (payload, payload_other)]
            return jnp.where(tile < near, pair[0].astype(F32), pair[1].astype(F32))
        begin = (slot >> 1) * 4 + (slot & 1)
        if side == 1:
            return routed[begin].astype(F32)
        return pltpu.roll(routed[begin + 2].astype(F32), (TILE - 32 * (row & 3)) & (TILE - 1), 1)

    repeat(rows_count, place)

    window = width + 2 * REACH
    tile_low = lax.div(low - REACH + TILE, TILE) - 1
    aligned = width % TILE == 0
    offset = TILE - REACH if aligned else low - REACH - tile_low * TILE
    sides = 3 if aligned else 2

    clipped = [jnp.clip(tile_low + side, 0, tiles - 1) for side in range(sides)]

    def fill(pick, begin):
        pieces = [None] * (lanes // TILE)
        for y in range(rows_count):
            moved = []
            for side in range(sides):
                if aligned:
                    shift = (y * stride - offset) % TILE
                else:
                    shift = lax.rem(y * stride - offset + TILE * (count // TILE + 1), TILE)
                moved.append(pltpu.roll(pick(y, side), shift, 1))
            lane = iota(moved[0].shape, 1)
            for t in range(y * stride // TILE, (y * stride + window - 1) // TILE + 1):
                column = lane + (t * TILE - y * stride)
                cell = column + (low - REACH)
                inside = (column >= 0) & (column < window) & (cell >= 0) & (cell < cells)
                for side in range(sides):
                    least = t * TILE - y * stride + offset
                    if aligned and (least + TILE <= side * TILE or least >= (side + 1) * TILE):
                        continue
                    taken = jnp.where(inside & ((column + offset) >> 7 == side), moved[side], 0.0)
                    pieces[t] = taken if pieces[t] is None else pieces[t] + taken
        height = next(piece.shape[0] for piece in pieces if piece is not None)
        for t in range(lanes // TILE):
            field[begin : begin + height, t * TILE : (t + 1) * TILE] = (
                jnp.zeros((height, TILE), F32) if pieces[t] is None else pieces[t]
            )

    def shift_of(tap):
        return stride * (tap // 3 - 1) + (tap % 3 - 1)

    def rolled(value, amount):
        amount = amount % lanes
        return value if amount == 0 else pltpu.roll(value, amount, 1)

    def spread(begin, target, target_begin, sign):
        for tap in range(TAPS):
            part = rolled(field[begin : begin + HID, :], sign * shift_of(tap))
            at = target_begin + tap * HID
            target[at : at + HID, :] = part[:, :count].astype(BF16)

    def volume_and_cotangent(y, side):
        return jnp.concatenate(
            [
                vol[y * tiles + clipped[side]].astype(F32),
                cotangent_tile(y, side, clipped[side]),
            ],
            axis=0,
        )

    fill(volume_and_cotangent, 0)
    spread(0, col_in, 0, -1)
    spread(16, col_cot, 0, 1)

    for copy in copies:
        copy.wait()
    tile_of, block_of, project = projector(sizes, table, footprints)

    def project_volume(tile):
        proj[tile] = project(tile, lambda t, o: vol[o * tiles + tile_of(t, o)])

    repeat(detectors, project_volume)

    batch, mixed_of, stack_of = dual_reader(scalars, proj, dual, meas)

    def dual_block(chunk):
        span, parts = stack_of(chunk)
        total = parts[0]
        for m in range(HID):
            mixed = mixed_of(m, parts)
            gate = sigmoid(mixed)
            active = mixed * gate
            total = total + scalars[1][m] * active
            if whole:
                cache[0][m, span] = active
                cache[1][m, span] = gate * (1.0 + (mixed - active))
        dual_new[span] = total
        dual_half[span] = total.astype(BF16)

    repeat(detectors // batch, dual_block)
    for t in range(2):
        dual_out[:, t * TILE : (t + 1) * TILE] = dual_new[
            row * 2 + t, pl.ds(pl.multiple_of(chan * 8, 8), 8), :
        ]

    def backproject(group):
        owners = [group * 8 + o for o in range(8)]

        def add(tile, totals):
            right = jnp.concatenate([block_of(tile, o) for o in owners], axis=0)
            products = dot(dual_half[tile], right, NT)
            out = []
            for o in range(8):
                place_of = tile_of(tile, owners[o]) - tile_low
                product = products[:, o * TILE : (o + 1) * TILE]
                for side in range(sides):
                    out.append(totals[sides * o + side] + jnp.where(place_of == side, product, 0.0))
            return tuple(out)

        totals = tuple(jnp.zeros((16, TILE), F32) for _ in range(8 * sides))
        if detectors <= 16:
            for tile in range(detectors):
                totals = add(tile, totals)
        else:
            totals = lax.fori_loop(0, detectors, add, totals)
        for o in range(8):
            for side in range(sides):
                back[owners[o], side] = totals[sides * o + side]

    repeat(rows_count // 8, backproject)

    fill(lambda y, side: back[y, side].astype(BF16).astype(F32), 32)
    spread(32, col_in, TAPS * HID, -1)

    wide = HID * HID
    place_x = iota((stride, wide), 0)
    cell_x = place_x + (low - REACH)
    valid = (cell_x >= 0) & (cell_x < cells)
    own = (place_x >= REACH) & (place_x < REACH + width)

    def masked(mask, value):
        shaped = value.reshape(rows_count, stride, wide)
        return jnp.where(mask[None], shaped, 0.0).reshape(count, wide)

    def widen(target, value, step):
        zero = jnp.zeros((stride, 3 * wide), BF16)
        target[0:stride, :] = zero
        target[stride + count :, :] = zero
        for k, amount in ((0, step), (1, 0), (2, -step)):
            moved = value if amount == 0 else pltpu.roll(value, amount % count, 0)
            target[stride : stride + count, k * wide : (k + 1) * wide] = moved.astype(BF16)

    first_pre = dot(col_in[...], first[...], TN)
    gate = sigmoid(first_pre)
    slope_first[...] = gate * (1.0 + (first_pre - first_pre * gate))
    widen(act_wide, masked(valid, first_pre * gate), 1)
    middle_pre = None
    for dy in range(3):
        for dx in range(3):
            part = dot(
                act_wide[stride * dy : stride * dy + count, dx * wide : (dx + 1) * wide],
                middle[dy, dx * wide : (dx + 1) * wide, :],
                NT,
            )
            middle_pre = part if middle_pre is None else middle_pre + part
    gate = sigmoid(middle_pre)
    slope_middle[...] = gate * (1.0 + (middle_pre - middle_pre * gate))
    middle_act = masked(valid, middle_pre * gate)
    middle_half = middle_act.astype(BF16)

    def gather_taps(products, sign):
        padded = jnp.concatenate([products, jnp.zeros((TAPS * HID, pad), F32)], axis=1)
        total = None
        for tap in range(TAPS):
            part = rolled(padded[tap * HID : (tap + 1) * HID], sign * shift_of(tap))
            total = part if total is None else total + part
        return total

    def rows_to_tiles(value, target):
        lane_one = iota((16, TILE), 1)
        for y in range(rows_count):
            begin = y * stride + REACH
            merged = None
            for t in range(begin // TILE, (begin + width - 1) // TILE + 1):
                column = lane_one + t * TILE
                inside = (column >= begin) & (column < begin + width)
                part = jnp.where(inside, value[:, t * TILE : (t + 1) * TILE], 0.0)
                merged = part if merged is None else merged + part
            if aligned:
                shift = -begin % TILE
            else:
                shift = lax.rem(low - begin + TILE * (count // TILE + 1), TILE)
            target(y, pltpu.roll(merged, shift, 1))

    update = gather_taps(dot(last[...], middle_half, NT), -1) + field[0:16, :]

    def put_row(y, tile):
        row_tiles[y] = tile

    rows_to_tiles(update, put_row)

    middle_grad = masked(valid, dot(col_cot[...], last[...], TN) * slope_middle[...])
    grad_last = dot(col_cot[...], masked(own, middle_act).astype(BF16))
    widen(grad_wide, middle_grad, -1)
    turned = masked(own, middle_grad).astype(BF16)
    grads_middle = [
        dot(turned, act_wide[stride * dy : stride * dy + count, :], TN) for dy in range(3)
    ]
    first_sum = None
    for dy in range(3):
        part = dot(grad_wide[stride * (2 - dy) : stride * (2 - dy) + count, :], middle[dy])
        first_sum = part if first_sum is None else first_sum + part
    first_grad = masked(valid, first_sum * slope_first[...])
    first_half = first_grad.astype(BF16)
    grad_first = dot(col_in[...], masked(own, first_grad).astype(BF16))
    back_grad = gather_taps(dot(first[TAPS * HID :, :], first_half, NT), 1)

    def put_grad(y, tile):
        grad_tiles[y, 0] = jnp.zeros((16, TILE), BF16)
        grad_tiles[y, 1] = tile.astype(BF16)

    rows_to_tiles(back_grad, put_grad)

    lane_z = iota((HID, wide), 1) >> 4
    lane_group = iota((HID, TILE), 1) >> 4
    out_tiles = [jnp.zeros((HID, TILE), F32) for _ in range(4)]

    def fold_groups(value):
        for amount in (64, 32, 16):
            value = value + pltpu.roll(value, amount, 1)
        return value

    def put(index, value):
        group = index // 8
        out_tiles[group] = jnp.where(lane_group == index % 8, value, out_tiles[group])

    for tap in range(TAPS):
        plane = grads_middle[tap // 3][:, (tap % 3) * wide : (tap % 3 + 1) * wide]
        for depth in range(3):
            total = jnp.zeros((HID, TILE), F32)
            for z in range(max(0, 1 - depth), min(HID, HID + 1 - depth)):
                other = z + depth - 1
                half = other // 8
                block = plane[z * HID : (z + 1) * HID, half * TILE : (half + 1) * TILE]
                total = total + jnp.where(lane_group == other % 8, block, 0.0)
            put(depth * TAPS + tap, fold_groups(total))

    lane_z = iota((HID, wide), 1) >> 4
    row_z = iota((HID, wide), 0)
    lines = []

    def add_line(product, begin, apart):
        part = jnp.where(lane_z - row_z == apart, product[begin : begin + HID], 0.0)
        lines.append(jnp.sum(part[:, :TILE] + part[:, TILE:], axis=0, keepdims=True))

    for depth in range(3):
        for tap in range(TAPS):
            for channel in range(2):
                add_line(grad_first, (channel * TAPS + tap) * HID, 1 - depth)
    for depth in range(3):
        for tap in range(TAPS):
            add_line(grad_last, tap * HID, depth - 1)
    lines.append(jnp.zeros((88 - len(lines), TILE), F32))
    lines = fold_groups(jnp.concatenate(lines, axis=0))
    row_eight = iota((8, TILE), 0)
    row_packed = iota((HID, TILE), 0)
    packed = jnp.zeros((HID, TILE), F32)
    for r in range(11):
        picked = jnp.where(row_eight == iota((8, TILE), 1) >> 4, lines[r * 8 : (r + 1) * 8], 0.0)
        packed = jnp.where(row_packed == r, jnp.sum(picked, axis=0, keepdims=True), packed)

    if whole:
        small = dual_gradients(
            sizes, table, scalars, footprints, proj, dual, meas, grad_tiles, dual_new, sums, cache
        )
    else:
        small = jnp.zeros((8, TILE), F32)

    for t in range(4):
        slope_first[0:HID, 0:TILE] = out_tiles[t]
        keep[t * 8 : (t + 1) * 8, :] = slope_first[pl.ds(pl.multiple_of(chan * 8, 8), 8), 0:TILE]
        send[t * 8 : (t + 1) * 8, :] = slope_first[
            pl.ds(pl.multiple_of((chans - 1 - chan) * 8, 8), 8), 0:TILE
        ]
    for target in (keep, send):
        target[32:48, :] = packed
        target[48:56, :] = small

    def put_update(y):
        begin = pl.multiple_of(56 + y * 16, 8)
        tile = row_tiles[update_row(y, row)]
        keep[pl.ds(begin, 16), :] = tile
        send[pl.ds(begin, 16), :] = tile

    repeat(updates, put_update)


def write_grads(chan, grads, scale, middle, first, last, mixing, readout):
    for k in range(27):
        block = grads[(k // 8) * 8 : (k // 8 + 1) * 8]
        block = block if k % 8 == 0 else pltpu.roll(block, TILE - 16 * (k % 8), 1)
        middle[k] = block[:, :HID]
    block = pltpu.roll(grads[32:48], lax.rem(TILE - 8 * chan, TILE), 1)
    for group in range(8):
        moved = block if group == 0 else pltpu.roll(block, TILE - 16 * group, 1)
        for r in range(11):
            line = r * 8 + group
            if line < 54:
                first[line // 2, line % 2 : line % 2 + 1, :] = moved[r : r + 1, :8]
            elif line < 81:
                last[line - 54] = moved[r : r + 1, :8]
    small = jnp.broadcast_to(jnp.sum(grads[48:56], axis=0, keepdims=True), (8, TILE))
    readout[...] = small[0:1, :HID]
    for k in range(3):
        moved = pltpu.roll(small, TILE - HID * (k + 1), 1)
        mixing[k : k + 1, :] = moved[0:1, :HID] * scale[0:1, :HID]


def finish_kernel(scale, dual_in, keep, near, one, two, three, volume, dual, *rest):
    grads, slots = (rest[:-1], rest[-1])
    dual[...] = dual_in[...]
    row = own_row()
    chan = lax.axis_index("chan")
    total = keep[0:56, :] + near[0:56, :] + one[0:56, :] + two[0:56, :] + three[0:56, :]
    write_grads(chan, total, scale, *grads)
    for k, (source, begin) in enumerate(
        ((keep, 56), (near, 56), (one, 56), (one, 72), (two, 56), (two, 72), (three, 56), (three, 72))
    ):
        slots[k] = source[begin : begin + 16, :]
    for tile in range(8):
        volume[:, tile, :] = slots[(((tile >> 1) ^ (row & 3)) << 1) + ((tile & 1) ^ chan)]


def finish_grads_kernel(scale, total, *grads):
    write_grads(lax.axis_index("chan"), total[...], scale[...], *grads)


def row_mask_pairs(devices, mask):
    return [(index, index ^ mask) for index in range(devices)]


def body(
    volume,
    dual_state,
    measured,
    cotangent,
    conv_first,
    conv_middle,
    conv_last,
    dual_mixing,
    dual_readout,
    footprints,
    tile_rows,
    tile_blocks,
):
    views, slabs, chans = (lax.axis_size(a) for a in ALL_AXES)
    rows_count = views * slabs
    devices = rows_count * chans
    cells = volume.shape[2]
    tiles = cells // TILE
    quick = rows_count == 8 and chans == 2 and tiles == 8
    copies = 2 if quick else 1
    width = cells * copies // devices
    stride = -(-(width + 2 * REACH) // 16) * 16
    detectors = tile_rows.shape[0] * tile_rows.shape[1]

    vmem = pl.BlockSpec(memory_space=pltpu.VMEM)
    smem = pl.BlockSpec(memory_space=pltpu.SMEM)
    hbm = pl.BlockSpec(memory_space=pltpu.HBM)
    raw = (
        volume.reshape(16, cells),
        cotangent.reshape(16, cells),
        dual_state.reshape(8, 2 * TILE),
        measured.reshape(8, 2 * TILE),
    )
    payload = pl.pallas_call(
        functools.partial(pack_kernel, quick),
        out_shape=jax.ShapeDtypeStruct((1, tiles // 2 + 2 + (5 if quick else tiles // 2), 16, TILE), BF16),
        in_specs=[hbm] * 4,
        out_specs=vmem,
        scratch_shapes=[pltpu.VMEM(value.shape, value.dtype) for value in raw]
        + [pltpu.SemaphoreType.DMA((4,))],
        compiler_params=pltpu.CompilerParams(vmem_limit_bytes=4 * MIB),
        name="pack",
    )(*(in_hbm(value) for value in raw))

    def swap(value, mask):
        return lax.ppermute(value, ALL_AXES, row_mask_pairs(devices, mask))

    table = (
        jnp.swapaxes(tile_rows, 2, 3),
        jnp.swapaxes(tile_blocks, 2, 3),
        dual_mixing.T,
        dual_readout,
    )
    own = own_weights(conv_first, conv_middle, conv_last)
    if quick:
        far_payload = swap(payload, 8)
        other = tuple(swap(value, 1) for value in own)
        payload, far_payload, other = lax.optimization_barrier((payload, far_payload, other))

        def bound_for(k):
            sources = (payload[0], far_payload[0])
            return jnp.concatenate(
                [source[:6] for source in sources]
                + [source[6 + k : 7 + k] for source in sources]
                + [source[10:] for source in sources],
                axis=0,
            )

        pieces = [swap(bound_for(k), 2 * k) for k in (1, 2, 3)]
        weights = build_weights(own, other, (footprints, *table))
        pieces[0], weights = lax.optimization_barrier((pieces[0], weights))
        pieces = [bound_for(0)] + pieces
        payload = jnp.concatenate([piece[:12] for piece in pieces], axis=0)
        payload = payload.reshape(rows_count, 6, 16, TILE)
        routed = jnp.concatenate([piece[12:] for piece in pieces], axis=0)
        payload_other = swap(payload, 1)
    else:
        payload = lax.all_gather(payload, ALL_AXES, axis=0, tiled=True)
        payload = payload.reshape(rows_count, chans, *payload.shape[1:])
        payload, payload_other = (payload[:, 0], payload[:, 1])
        routed = payload[0, :1]
        weights = build_weights(
            own, tuple(swap(value, 1) for value in own), (footprints, *table)
        )
    middle, first, last, footprints, *table = weights

    def piece_slot(owner, row):
        if not quick:
            return owner
        mask = owner ^ row
        return (mask & 3) * 2 + (mask >> 2)

    def update_row(owner, row):
        return owner ^ row if quick else owner

    def chunk_of(row, chan):
        return ((row & 3) if quick else row) * chans + chan

    def flip_of(chan):
        return chan if quick else 0

    updates = 4 if quick else rows_count
    count = rows_count * stride
    wide = HID * HID
    moved = 56 + 16 * updates
    pad = -(-(stride + 1) // TILE) * TILE
    limit = (24 if quick else 56) * MIB
    sizes = (rows_count, chans, detectors, tiles, width, stride, cells,
             (piece_slot, update_row, chunk_of, flip_of), updates,
             tile_rows.shape[1])
    outs = [
        ((moved, TILE), F32),
        ((moved, TILE), F32),
        ((8, 2 * TILE), F32),
    ]
    shared = [
        ((detectors, 16, TILE), F32),
        ((detectors, 16, TILE), F32),
        ((detectors, 16, TILE), F32),
        ((rows_count, 2, 16, TILE), BF16),
    ]
    scratch = [
        ((rows_count * tiles, 16, TILE), BF16),
        ((detectors, 16, TILE), BF16),
        ((detectors, 16, TILE), F32),
        ((rows_count, 3, 16, TILE), F32),
        ((48, count + pad), F32),
        ((2 * TAPS * HID, count), BF16),
        ((TAPS * HID, count), BF16),
        ((count + 2 * stride, 3 * wide), BF16),
        ((count + 2 * stride, 3 * wide), BF16),
        ((count, wide), F32),
        ((count, wide), F32),
        ((rows_count, 16, TILE), F32),
        ((4, HID, 8, TILE), F32),
    ]
    if quick:
        scratch = shared + scratch
    else:
        outs = outs + shared
    keep, send, new_dual, *rest = pl.pallas_call(
        functools.partial(main_kernel, sizes, quick),
        out_shape=[jax.ShapeDtypeStruct(*spec) for spec in outs],
        in_specs=[vmem] * 11,
        out_specs=[vmem] * len(outs),
        scratch_shapes=[pltpu.VMEM(*spec) for spec in scratch]
        + [pltpu.SMEM(value.shape, value.dtype) for value in table]
        + [pltpu.SemaphoreType.DMA((4,))]
        + [pltpu.VMEM((HID, detectors, 16, TILE), F32) for _ in range(2 if quick else 0)],
        compiler_params=pltpu.CompilerParams(vmem_limit_bytes=limit),
        cost_estimate=pl.CostEstimate(
            flops=5 * 10**9, bytes_accessed=5 * 10**6, transcendentals=2 * 10**6
        ),
        name="primal_dual",
    )(
        *table,
        payload,
        payload_other,
        routed,
        middle,
        first,
        last,
        footprints,
    )

    near = swap(send, 1)
    scale = dual_readout.reshape(1, HID)
    grad_shapes = [
        jax.ShapeDtypeStruct(shape, F32)
        for shape in ((27, 8, HID), (27, 2, 8), (27, 1, 8), (3, HID), (1, HID))
    ]
    if quick:

        sums = keep[:56] + near[:56]

        def piece(value, index):
            return value[56 + 16 * index : 72 + 16 * index]

        parts = [
            swap(jnp.concatenate([sums, piece(keep, k), piece(near, k)], axis=0), 2 * k)
            for k in (1, 2, 3)
        ]
        new_volume, new_dual, *grads = pl.pallas_call(
            finish_kernel,
            out_shape=[
                jax.ShapeDtypeStruct((16, 8, TILE), F32),
                jax.ShapeDtypeStruct((8, 2 * TILE), F32),
            ]
            + grad_shapes,
            in_specs=[vmem] * 7,
            out_specs=[vmem] * 7,
            scratch_shapes=[pltpu.VMEM((8, 16, TILE), F32)],
            compiler_params=pltpu.CompilerParams(vmem_limit_bytes=8 * MIB),
            name="finish",
        )(scale, new_dual, keep, near, *parts)
    else:
        mine = keep + near
        small = pl.pallas_call(
            functools.partial(dual_gradients_kernel, sizes),
            out_shape=jax.ShapeDtypeStruct((8, TILE), F32),
            in_specs=[smem] * 4 + [vmem] * 5,
            out_specs=vmem,
            scratch_shapes=[
                pltpu.VMEM((detectors, 16, TILE), F32),
                pltpu.VMEM((4, HID, 8, TILE), F32),
            ],
            compiler_params=pltpu.CompilerParams(vmem_limit_bytes=limit),
            name="dual_gradients",
        )(*table, footprints, *rest)
        total = jnp.concatenate(
            [lax.psum(mine[:48], ROW_AXES), lax.psum(small, ALL_AXES)], axis=0
        )
        grads = pl.pallas_call(
            finish_grads_kernel,
            out_shape=grad_shapes,
            in_specs=[vmem, vmem],
            out_specs=[vmem] * 5,
            name="finish_grads",
        )(scale, total)
        pieces = lax.all_to_all(
            mine[56:].reshape(rows_count, 16, TILE), ROW_AXES, 0, 0, tiled=True
        )
        pieces = pieces.reshape(tiles, rows_count // tiles, 16, TILE).sum(axis=1)
        new_volume = jnp.swapaxes(pieces, 0, 1)

    grad_middle, grad_first, grad_last, grad_mixing, grad_readout = grads
    return (
        new_volume.reshape(volume.shape),
        new_dual.reshape(dual_state.shape),
        grad_first.reshape(3, 3, 3, 2, 8).transpose(4, 3, 0, 1, 2),
        grad_middle.reshape(3, 3, 3, 8, HID).transpose(3, 4, 0, 1, 2),
        grad_last.reshape(3, 3, 3, 1, 8).transpose(3, 4, 0, 1, 2),
        grad_mixing.T,
        grad_readout.reshape(HID),
    )


def solution(mesh):
    placed = (
        P("grp", ("view", "slab"), None),
        P(("grp", "view"), "chan", "slab"),
        P(("grp", "view"), "chan", "slab"),
        P("grp", ("view", "slab"), None),
        P("chan", None, None, None, None),
        P("chan", None, None, None, None),
        P(None, "chan", None, None, None),
        P(),
        P(),
        P(),
        P(),
        P(),
    )
    return jax.shard_map(
        body,
        mesh=mesh,
        in_specs=placed,
        out_specs=(
            P("grp", ("view", "slab"), None),
            P(("grp", "view"), "chan", "slab"),
            P(("grp", "chan"), None, None, None, None),
            P(("grp", "chan"), None, None, None, None),
            P("grp", "chan", None, None, None),
            P("grp", None),
            P("grp"),
        ),
        check_vma=False,
    )
```

```python
import functools

import jax
import jax.numpy as jnp
from jax import lax
from jax.experimental import pallas as pl
from jax.experimental.pallas import tpu as pltpu
from jax.sharding import PartitionSpec as P

F32 = jnp.float32
BF16 = jnp.bfloat16
ALL_AXES = ("view", "slab", "chan")
ROW_AXES = ("view", "slab")
HID = 16
TILE = 128
REACH = 4
TAPS = 9
NN = (((1,), (0,)), ((), ()))
NT = (((1,), (1,)), ((), ()))
TN = (((0,), (0,)), ((), ()))
MIB = 1024 * 1024


def dot(left, right, dims=NN, precision=None):
    return lax.dot_general(left, right, dims, precision=precision, preferred_element_type=F32)


def exact_parts(value):
    high = value.astype(BF16)
    rest = value - high.astype(F32)
    middle = rest.astype(BF16)
    return high, middle, (rest - middle.astype(F32)).astype(BF16)


def iota(shape, dim):
    return lax.broadcasted_iota(jnp.int32, shape, dim)


def repeat(count, step, limit=16):
    if count <= limit:
        for index in range(count):
            step(index)
    else:

        @pl.loop(0, count)
        def unused(index):
            step(index)


def in_hbm(value):
    return pltpu.with_memory_space_constraint(value, pltpu.HBM)


def own_row():
    return lax.axis_index("view") * lax.axis_size("slab") + lax.axis_index("slab")


def fetch(sources, targets, arrivals):
    copies = [
        pltpu.make_async_copy(source, target, arrivals.at[k])
        for k, (source, target) in enumerate(zip(sources, targets))
    ]
    for copy in copies:
        copy.start()
    return copies


def weights_kernel(middle_from, first_from, last_from, footprints_from,
                   rows_from, blocks_from, mixing_from, readout_from,
                   middle_other, first_other, last_other,
                   middle, first, last, footprints, rows, blocks, mixing, readout,
                   middle_own, first_own, last_own, arrivals):
    wide = HID * HID
    copies = fetch(
        (middle_from, first_from, last_from, footprints_from,
         rows_from, blocks_from, mixing_from, readout_from),
        (middle_own, first_own, last_own, footprints, rows, blocks, mixing, readout),
        arrivals,
    )
    for copy in copies[:3]:
        copy.wait()
    chan = lax.axis_index("chan")
    lane_z = iota((HID, wide), 1) >> 4
    row_z = iota((HID, wide), 0)

    spread = ((iota((HID, wide), 1) & (HID - 1)) == iota((HID, wide), 0)).astype(BF16)

    def spread_middle(source):
        rows = jnp.concatenate([source[k].astype(F32) for k in range(27)], axis=0)
        return dot(rows.astype(BF16), spread)

    mine, theirs = (spread_middle(middle_own), spread_middle(middle_other))
    lower = jnp.where(chan == 0, mine, theirs)
    upper = jnp.where(chan == 0, theirs, mine)
    for tap in range(TAPS):
        parts = []
        for depth in range(3):
            begin = (depth * TAPS + tap) * 8
            parts.append(
                jnp.concatenate([lower[begin : begin + 8], upper[begin : begin + 8]], axis=0)
            )
        for z in range(HID):
            block = jnp.where(
                lane_z == z - 1,
                parts[0],
                jnp.where(lane_z == z, parts[1], jnp.where(lane_z == z + 1, parts[2], 0.0)),
            )
            begin = (tap % 3) * wide + z * HID
            middle[tap // 3, begin : begin + HID, :] = block.astype(BF16)

    channel = iota((8, wide), 1) & (HID - 1)
    spread_own = (channel == iota((8, wide), 0) + 8 * chan).astype(BF16)
    spread_other = (channel == iota((8, wide), 0) + 8 * (1 - chan)).astype(BF16)

    def lines(own, other):
        return dot(own, spread_own) + dot(other, spread_other)

    def banded(rows, step):
        out = jnp.zeros((HID, wide), F32)
        for depth, line in enumerate(rows):
            line = jnp.broadcast_to(line, (HID, wide))
            out = jnp.where(row_z - lane_z == step * (depth - 1), line, out)
        return out.astype(BF16)

    first_lines = [lines(first_own[k], first_other[k]) for k in range(27)]
    last_lines = [lines(last_own[k // 3, k % 3], last_other[k // 3, k % 3]) for k in range(9)]
    for tap in range(TAPS):
        for c in range(2):
            begin = (c * TAPS + tap) * HID
            rows = [first_lines[depth * TAPS + tap][c : c + 1] for depth in range(3)]
            first[begin : begin + HID, :] = banded(rows, 1)
        dy, dx = (tap // 3, tap % 3)
        rows = [last_lines[depth * 3 + dy][dx : dx + 1] for depth in range(3)]
        last[tap * HID : (tap + 1) * HID, :] = banded(rows, -1)
    for copy in copies[3:]:
        copy.wait()


def own_weights(conv_first, conv_middle, conv_last):
    return (
        conv_middle.transpose(2, 3, 4, 0, 1).reshape(27, 8, HID),
        conv_first.transpose(2, 3, 4, 1, 0).reshape(27, 2, 8),
        conv_last.transpose(0, 2, 3, 4, 1).reshape(3, 3, 3, 8),
    )


def build_weights(own, other, passed):
    wide = HID * HID
    hbm = pl.BlockSpec(memory_space=pltpu.HBM)
    vmem = pl.BlockSpec(memory_space=pltpu.VMEM)
    return pl.pallas_call(
        weights_kernel,
        out_shape=(
            jax.ShapeDtypeStruct((3, 3 * wide, wide), BF16),
            jax.ShapeDtypeStruct((2 * TAPS * HID, wide), BF16),
            jax.ShapeDtypeStruct((TAPS * HID, wide), BF16),
            *(jax.ShapeDtypeStruct(value.shape, value.dtype) for value in passed),
        ),
        in_specs=[hbm] * 8 + [vmem] * 3,
        out_specs=[vmem] * 8,
        scratch_shapes=[pltpu.VMEM(value.shape, value.dtype) for value in own]
        + [pltpu.SemaphoreType.DMA((8,))],
        compiler_params=pltpu.CompilerParams(vmem_limit_bytes=16 * MIB),
        cost_estimate=pl.CostEstimate(flops=10**8, bytes_accessed=2 * 10**6, transcendentals=0),
        name="band_weights",
    )(*(in_hbm(value) for value in (*own, *passed)), *other)


def sigmoid(value):
    return jax.nn.sigmoid(value)


def projector(sizes, table, footprints):
    rows_count, per_view = (sizes[0], sizes[-1])
    groups = rows_count // 8

    def tile_of(tile, owner):
        return table[0][tile // per_view, tile % per_view, 0, owner]

    def block_of(tile, owner):
        return footprints[table[1][tile // per_view, tile % per_view, 0, owner]]

    def project(tile, pick):
        def one(group):
            owners = [group * 8 + o for o in range(8)]
            left = jnp.concatenate([pick(tile, o) for o in owners], axis=1)
            right = jnp.concatenate([block_of(tile, o) for o in owners], axis=0)
            return dot(left, right)

        if groups == 1:
            return one(0)
        return lax.fori_loop(0, groups, lambda g, a: a + one(g), jnp.zeros((16, TILE), F32))

    return tile_of, block_of, project


def dual_reader(scalars, proj, dual, meas):
    batch = 4

    def mixed_of(m, parts):
        return scalars[0][0, m] * parts[0] + scalars[0][1, m] * parts[1] + scalars[0][2, m] * parts[2]

    def stack_of(chunk):
        span = pl.ds(chunk * batch, batch)
        return span, (dual[span], proj[span], meas[span])

    return batch, mixed_of, stack_of


def dual_gradients(sizes, table, scalars, footprints, proj, dual, meas, grad_tiles, grad, sums,
                   cache=()):
    detectors, width = (sizes[2], sizes[4])
    own_tile = lax.div(sizes[7][2](own_row(), lax.axis_index("chan")) * width, TILE)
    tile_of, _, project = projector(sizes, table, footprints)
    batch, mixed_of, stack_of = dual_reader(scalars, proj, dual, meas)

    def project_grad(tile):
        def pick(t, o):
            return grad_tiles[o, (tile_of(t, o) == own_tile).astype(jnp.int32)]

        grad[tile] = project(tile, pick)

    repeat(detectors, project_grad)
    sums[...] = jnp.zeros_like(sums)

    def dual_sums(chunk):
        span, parts = stack_of(chunk)
        pulled = grad[span]
        weighted = [pulled * part for part in parts]
        for m in range(HID):
            if cache:
                active, slope = (cache[0][m, span], cache[1][m, span])
            else:
                mixed = mixed_of(m, parts)
                gate = sigmoid(mixed)
                active = mixed * gate
                slope = gate * (1.0 + (mixed - active))
            terms = [pulled * active] + [value * slope for value in weighted]
            for k, term in enumerate(terms):
                sums[k, m] += jnp.sum(term.reshape(batch * 2, 8, TILE), axis=0)

    repeat(detectors // batch, dual_sums)

    eight = 4 * HID * 8
    ones = jnp.ones((TILE, TILE), BF16)
    lines = sum(dot(part, ones) for part in exact_parts(sums[...].reshape(eight, TILE)))
    lane = iota((8, TILE), 1)
    out = jnp.zeros((8, TILE), F32)
    for k in range(4 * HID):
        out = jnp.where(lane == k, lines[8 * k : 8 * k + 8], out)
    return out


def dual_gradients_kernel(sizes, rows_ref, blocks_ref, mixing, readout,
                          footprints, proj, dual, meas, grad_tiles, out, grad, sums):
    table = (rows_ref, blocks_ref)
    out[...] = dual_gradients(
        sizes, table, (mixing, readout), footprints, proj, dual, meas, grad_tiles, grad, sums
    )


def pack_kernel(routed, volume_from, cotangent_from, dual_from, measured_from,
                out, volume, cotangent, dual, measured, arrivals):
    copies = fetch(
        (volume_from, cotangent_from, dual_from, measured_from),
        (volume, cotangent, dual, measured),
        arrivals,
    )
    chan = lax.axis_index("chan")
    row = own_row()
    tiles = volume.shape[1] // TILE
    near = tiles // 2

    def pair(value):
        return jnp.concatenate([value[:, :TILE], value[:, TILE:]], axis=0).astype(BF16)

    def tile_at(source, index):
        return source[:, pl.ds(pl.multiple_of(index * TILE, TILE), TILE)]

    for copy in copies:
        copy.wait()
    for k in range(near):
        out[0, k] = tile_at(volume, chan * near + k)
    out[0, near] = pair(dual[...].astype(F32))
    out[0, near + 1] = pair(measured[...].astype(F32))
    if not routed:
        for k in range(near):
            out[0, near + 2 + k] = tile_at(cotangent, chan * near + k)
        return
    lane = iota((16, TILE), 1)
    beside = jnp.zeros((16, TILE), F32)
    for k in range(4):
        out[0, near + 2 + k] = tile_at(cotangent, (((row & 3) ^ k) << 1) + chan)
        lower = tile_at(cotangent, jnp.maximum(2 * k + chan - 1, 0)).astype(F32)
        upper = tile_at(cotangent, jnp.minimum(2 * k + chan + 1, tiles - 1)).astype(F32)
        spot = jnp.where(lane >= TILE // 2, lower, upper)
        spot = spot if k == 0 else pltpu.roll(spot, 32 * k, 1)
        first = (32 * k - REACH) % TILE
        mine = (lane >= 32 * k) & (lane < 32 * k + REACH) | (lane >= first) & (lane < first + REACH)
        beside = jnp.where(mine, spot, beside)
    out[0, near + 6] = beside.astype(BF16)


def main_kernel(sizes, whole, rows_from, blocks_from, mixing_from, readout_from,
                payload, payload_other, payload_late, routed,
                middle, first, last, footprints,
                keep, send, dual_out, proj, dual, meas, grad_tiles,
                vol, dual_half, dual_new, back, field, col_in, col_cot,
                act_wide, grad_wide, slope_first, slope_middle, row_tiles, sums,
                rows_ref, blocks_ref, mixing, readout, arrivals, *cache):
    rows_count, chans, detectors, tiles, width, stride, cells, places, updates, _ = sizes
    piece_slot, update_row, chunk_of, flip_of = places
    copies = fetch(
        (rows_from, blocks_from, mixing_from, readout_from),
        (rows_ref, blocks_ref, mixing, readout),
        arrivals,
    )
    table = (rows_ref, blocks_ref)
    scalars = (mixing, readout)
    row = own_row()
    chan = lax.axis_index("chan")
    low = chunk_of(row, chan) * width
    count = rows_count * stride
    pad = -(-(stride + 1) // TILE) * TILE
    lanes = count + pad

    flip = flip_of(chan)

    near = tiles // 2

    def place(slot):
        owner = row ^ ((slot >> 1) + ((slot & 1) << 2)) if whole else slot
        late = whole and slot >= 2
        received = payload_late if late else payload_other
        for source, part, at in ((payload, flip, slot), (received, 1 - flip, slot - 2 * late)):
            for k in range(near):
                vol[owner * tiles + part * near + k] = source[at, k]
            span = pl.ds(pl.multiple_of(part * 8, 8), 8)
            for k, target in ((near, dual), (near + 1, meas)):
                piece = source[at, k].astype(F32)
                for t in range(2):
                    target[owner * 2 + t, span, :] = piece[t * 8 : (t + 1) * 8]

    def cotangent_tile(owner, side, tile):
        slot = piece_slot(owner, row)
        if not whole:
            pair = [source[slot, near + 2 + (tile & (near - 1))] for source in (payload, payload_other)]
            return jnp.where(tile < near, pair[0].astype(F32), pair[1].astype(F32))
        begin = (slot >> 1) * 4 + (slot & 1)
        if side == 1:
            return routed[begin].astype(F32)
        return pltpu.roll(routed[begin + 2].astype(F32), (TILE - 32 * (row & 3)) & (TILE - 1), 1)

    repeat(rows_count, place)

    window = width + 2 * REACH
    tile_low = lax.div(low - REACH + TILE, TILE) - 1
    aligned = width % TILE == 0
    offset = TILE - REACH if aligned else low - REACH - tile_low * TILE
    sides = 3 if aligned else 2

    clipped = [jnp.clip(tile_low + side, 0, tiles - 1) for side in range(sides)]

    def fill(pick, begin):
        pieces = [None] * (lanes // TILE)
        for y in range(rows_count):
            moved = []
            for side in range(sides):
                if aligned:
                    shift = (y * stride - offset) % TILE
                else:
                    shift = lax.rem(y * stride - offset + TILE * (count // TILE + 1), TILE)
                moved.append(pltpu.roll(pick(y, side), shift, 1))
            lane = iota(moved[0].shape, 1)
            for t in range(y * stride // TILE, (y * stride + window - 1) // TILE + 1):
                column = lane + (t * TILE - y * stride)
                cell = column + (low - REACH)
                inside = (column >= 0) & (column < window) & (cell >= 0) & (cell < cells)
                for side in range(sides):
                    least = t * TILE - y * stride + offset
                    if aligned and (least + TILE <= side * TILE or least >= (side + 1) * TILE):
                        continue
                    taken = jnp.where(inside & ((column + offset) >> 7 == side), moved[side], 0.0)
                    pieces[t] = taken if pieces[t] is None else pieces[t] + taken
        height = next(piece.shape[0] for piece in pieces if piece is not None)
        for t in range(lanes // TILE):
            field[begin : begin + height, t * TILE : (t + 1) * TILE] = (
                jnp.zeros((height, TILE), F32) if pieces[t] is None else pieces[t]
            )

    def shift_of(tap):
        return stride * (tap // 3 - 1) + (tap % 3 - 1)

    def rolled(value, amount):
        amount = amount % lanes
        return value if amount == 0 else pltpu.roll(value, amount, 1)

    def spread(begin, target, target_begin, sign):
        for tap in range(TAPS):
            part = rolled(field[begin : begin + HID, :], sign * shift_of(tap))
            at = target_begin + tap * HID
            target[at : at + HID, :] = part[:, :count].astype(BF16)

    def volume_and_cotangent(y, side):
        return jnp.concatenate(
            [
                vol[y * tiles + clipped[side]].astype(F32),
                cotangent_tile(y, side, clipped[side]),
            ],
            axis=0,
        )

    fill(volume_and_cotangent, 0)
    spread(0, col_in, 0, -1)
    spread(16, col_cot, 0, 1)

    for copy in copies:
        copy.wait()
    tile_of, block_of, project = projector(sizes, table, footprints)

    def project_volume(tile):
        proj[tile] = project(tile, lambda t, o: vol[o * tiles + tile_of(t, o)])

    repeat(detectors, project_volume)

    batch, mixed_of, stack_of = dual_reader(scalars, proj, dual, meas)

    def dual_block(chunk):
        span, parts = stack_of(chunk)
        total = parts[0]
        for m in range(HID):
            mixed = mixed_of(m, parts)
            gate = sigmoid(mixed)
            active = mixed * gate
            total = total + scalars[1][m] * active
            if whole:
                cache[0][m, span] = active
                cache[1][m, span] = gate * (1.0 + (mixed - active))
        dual_new[span] = total
        dual_half[span] = total.astype(BF16)

    repeat(detectors // batch, dual_block)
    for t in range(2):
        dual_out[:, t * TILE : (t + 1) * TILE] = dual_new[
            row * 2 + t, pl.ds(pl.multiple_of(chan * 8, 8), 8), :
        ]

    def backproject(group):
        owners = [group * 8 + o for o in range(8)]

        def add(tile, totals):
            right = jnp.concatenate([block_of(tile, o) for o in owners], axis=0)
            products = dot(dual_half[tile], right, NT)
            out = []
            for o in range(8):
                place_of = tile_of(tile, owners[o]) - tile_low
                product = products[:, o * TILE : (o + 1) * TILE]
                for side in range(sides):
                    out.append(totals[sides * o + side] + jnp.where(place_of == side, product, 0.0))
            return tuple(out)

        totals = tuple(jnp.zeros((16, TILE), F32) for _ in range(8 * sides))
        if detectors <= 16:
            for tile in range(detectors):
                totals = add(tile, totals)
        else:
            totals = lax.fori_loop(0, detectors, add, totals)
        for o in range(8):
            for side in range(sides):
                back[owners[o], side] = totals[sides * o + side]

    repeat(rows_count // 8, backproject)

    fill(lambda y, side: back[y, side].astype(BF16).astype(F32), 32)
    spread(32, col_in, TAPS * HID, -1)

    wide = HID * HID
    place_x = iota((stride, wide), 0)
    cell_x = place_x + (low - REACH)
    valid = (cell_x >= 0) & (cell_x < cells)
    own = (place_x >= REACH) & (place_x < REACH + width)

    def masked(mask, value):
        shaped = value.reshape(rows_count, stride, wide)
        return jnp.where(mask[None], shaped, 0.0).reshape(count, wide)

    def widen(target, value, step):
        zero = jnp.zeros((stride, 3 * wide), BF16)
        target[0:stride, :] = zero
        target[stride + count :, :] = zero
        for k, amount in ((0, step), (1, 0), (2, -step)):
            moved = value if amount == 0 else pltpu.roll(value, amount % count, 0)
            target[stride : stride + count, k * wide : (k + 1) * wide] = moved.astype(BF16)

    first_pre = dot(col_in[...], first[...], TN)
    gate = sigmoid(first_pre)
    slope_first[...] = gate * (1.0 + (first_pre - first_pre * gate))
    widen(act_wide, masked(valid, first_pre * gate), 1)
    middle_pre = None
    for dy in range(3):
        for dx in range(3):
            part = dot(
                act_wide[stride * dy : stride * dy + count, dx * wide : (dx + 1) * wide],
                middle[dy, dx * wide : (dx + 1) * wide, :],
                NT,
            )
            middle_pre = part if middle_pre is None else middle_pre + part
    gate = sigmoid(middle_pre)
    slope_middle[...] = gate * (1.0 + (middle_pre - middle_pre * gate))
    middle_act = masked(valid, middle_pre * gate)
    middle_half = middle_act.astype(BF16)

    def gather_taps(products, sign):
        padded = jnp.concatenate([products, jnp.zeros((TAPS * HID, pad), F32)], axis=1)
        total = None
        for tap in range(TAPS):
            part = rolled(padded[tap * HID : (tap + 1) * HID], sign * shift_of(tap))
            total = part if total is None else total + part
        return total

    def rows_to_tiles(value, target):
        lane_one = iota((16, TILE), 1)
        for y in range(rows_count):
            begin = y * stride + REACH
            merged = None
            for t in range(begin // TILE, (begin + width - 1) // TILE + 1):
                column = lane_one + t * TILE
                inside = (column >= begin) & (column < begin + width)
                part = jnp.where(inside, value[:, t * TILE : (t + 1) * TILE], 0.0)
                merged = part if merged is None else merged + part
            if aligned:
                shift = -begin % TILE
            else:
                shift = lax.rem(low - begin + TILE * (count // TILE + 1), TILE)
            target(y, pltpu.roll(merged, shift, 1))

    update = gather_taps(dot(last[...], middle_half, NT), -1) + field[0:16, :]

    def put_row(y, tile):
        row_tiles[y] = tile

    rows_to_tiles(update, put_row)

    middle_grad = masked(valid, dot(col_cot[...], last[...], TN) * slope_middle[...])
    grad_last = dot(col_cot[...], masked(own, middle_act).astype(BF16))
    widen(grad_wide, middle_grad, -1)
    turned = masked(own, middle_grad).astype(BF16)
    grads_middle = [
        dot(turned, act_wide[stride * dy : stride * dy + count, :], TN) for dy in range(3)
    ]
    first_sum = None
    for dy in range(3):
        part = dot(grad_wide[stride * (2 - dy) : stride * (2 - dy) + count, :], middle[dy])
        first_sum = part if first_sum is None else first_sum + part
    first_grad = masked(valid, first_sum * slope_first[...])
    first_half = first_grad.astype(BF16)
    grad_first = dot(col_in[...], masked(own, first_grad).astype(BF16))
    back_grad = gather_taps(dot(first[TAPS * HID :, :], first_half, NT), 1)

    def put_grad(y, tile):
        grad_tiles[y, 0] = jnp.zeros((16, TILE), BF16)
        grad_tiles[y, 1] = tile.astype(BF16)

    rows_to_tiles(back_grad, put_grad)

    lane_z = iota((HID, wide), 1) >> 4
    lane_group = iota((HID, TILE), 1) >> 4
    out_tiles = [jnp.zeros((HID, TILE), F32) for _ in range(4)]

    def fold_groups(value):
        for amount in (64, 32, 16):
            value = value + pltpu.roll(value, amount, 1)
        return value

    def put(index, value):
        group = index // 8
        out_tiles[group] = jnp.where(lane_group == index % 8, value, out_tiles[group])

    for tap in range(TAPS):
        plane = grads_middle[tap // 3][:, (tap % 3) * wide : (tap % 3 + 1) * wide]
        for depth in range(3):
            total = jnp.zeros((HID, TILE), F32)
            for z in range(max(0, 1 - depth), min(HID, HID + 1 - depth)):
                other = z + depth - 1
                half = other // 8
                block = plane[z * HID : (z + 1) * HID, half * TILE : (half + 1) * TILE]
                total = total + jnp.where(lane_group == other % 8, block, 0.0)
            put(depth * TAPS + tap, fold_groups(total))

    lane_z = iota((HID, wide), 1) >> 4
    row_z = iota((HID, wide), 0)
    lines = []

    def add_line(product, begin, apart):
        part = jnp.where(lane_z - row_z == apart, product[begin : begin + HID], 0.0)
        lines.append(jnp.sum(part[:, :TILE] + part[:, TILE:], axis=0, keepdims=True))

    for depth in range(3):
        for tap in range(TAPS):
            for channel in range(2):
                add_line(grad_first, (channel * TAPS + tap) * HID, 1 - depth)
    for depth in range(3):
        for tap in range(TAPS):
            add_line(grad_last, tap * HID, depth - 1)
    lines.append(jnp.zeros((88 - len(lines), TILE), F32))
    lines = fold_groups(jnp.concatenate(lines, axis=0))
    row_eight = iota((8, TILE), 0)
    row_packed = iota((HID, TILE), 0)
    packed = jnp.zeros((HID, TILE), F32)
    for r in range(11):
        picked = jnp.where(row_eight == iota((8, TILE), 1) >> 4, lines[r * 8 : (r + 1) * 8], 0.0)
        packed = jnp.where(row_packed == r, jnp.sum(picked, axis=0, keepdims=True), packed)

    if whole:
        small = dual_gradients(
            sizes, table, scalars, footprints, proj, dual, meas, grad_tiles, dual_new, sums, cache
        )
    else:
        small = jnp.zeros((8, TILE), F32)

    for t in range(4):
        slope_first[0:HID, 0:TILE] = out_tiles[t]
        keep[t * 8 : (t + 1) * 8, :] = slope_first[pl.ds(pl.multiple_of(chan * 8, 8), 8), 0:TILE]
        send[t * 8 : (t + 1) * 8, :] = slope_first[
            pl.ds(pl.multiple_of((chans - 1 - chan) * 8, 8), 8), 0:TILE
        ]
    for target in (keep, send):
        target[32:48, :] = packed
        target[48:56, :] = small

    def put_update(y):
        begin = pl.multiple_of(56 + y * 16, 8)
        tile = row_tiles[update_row(y, row)]
        keep[pl.ds(begin, 16), :] = tile
        send[pl.ds(begin, 16), :] = tile

    repeat(updates, put_update)


def write_grads(chan, grads, scale, middle, first, last, mixing, readout):
    for k in range(27):
        block = grads[(k // 8) * 8 : (k // 8 + 1) * 8]
        block = block if k % 8 == 0 else pltpu.roll(block, TILE - 16 * (k % 8), 1)
        middle[k] = block[:, :HID]
    block = pltpu.roll(grads[32:48], lax.rem(TILE - 8 * chan, TILE), 1)
    for group in range(8):
        moved = block if group == 0 else pltpu.roll(block, TILE - 16 * group, 1)
        for r in range(11):
            line = r * 8 + group
            if line < 54:
                first[line // 2, line % 2 : line % 2 + 1, :] = moved[r : r + 1, :8]
            elif line < 81:
                last[line - 54] = moved[r : r + 1, :8]
    small = jnp.broadcast_to(jnp.sum(grads[48:56], axis=0, keepdims=True), (8, TILE))
    readout[...] = small[0:1, :HID]
    for k in range(3):
        moved = pltpu.roll(small, TILE - HID * (k + 1), 1)
        mixing[k : k + 1, :] = moved[0:1, :HID] * scale[0:1, :HID]


def finish_kernel(scale, dual_in, keep, near, one, two, three, volume, dual, *rest):
    grads, slots = (rest[:-1], rest[-1])
    dual[...] = dual_in[...]
    row = own_row()
    chan = lax.axis_index("chan")
    total = keep[0:56, :] + near[0:56, :] + one[0:56, :] + two[0:56, :] + three[0:56, :]
    write_grads(chan, total, scale, *grads)
    for k, (source, begin) in enumerate(
        ((keep, 56), (near, 56), (one, 56), (one, 72), (two, 56), (two, 72), (three, 56), (three, 72))
    ):
        slots[k] = source[begin : begin + 16, :]
    for tile in range(8):
        volume[:, tile, :] = slots[(((tile >> 1) ^ (row & 3)) << 1) + ((tile & 1) ^ chan)]


def finish_grads_kernel(scale, total, *grads):
    write_grads(lax.axis_index("chan"), total[...], scale[...], *grads)


def row_mask_pairs(devices, mask):
    return [(index, index ^ mask) for index in range(devices)]


def body(
    volume,
    dual_state,
    measured,
    cotangent,
    conv_first,
    conv_middle,
    conv_last,
    dual_mixing,
    dual_readout,
    footprints,
    tile_rows,
    tile_blocks,
):
    views, slabs, chans = (lax.axis_size(a) for a in ALL_AXES)
    rows_count = views * slabs
    devices = rows_count * chans
    cells = volume.shape[2]
    tiles = cells // TILE
    quick = rows_count == 8 and chans == 2 and tiles == 8
    copies = 2 if quick else 1
    width = cells * copies // devices
    stride = -(-(width + 2 * REACH) // 16) * 16
    detectors = tile_rows.shape[0] * tile_rows.shape[1]

    vmem = pl.BlockSpec(memory_space=pltpu.VMEM)
    smem = pl.BlockSpec(memory_space=pltpu.SMEM)
    hbm = pl.BlockSpec(memory_space=pltpu.HBM)
    raw = (
        volume.reshape(16, cells),
        cotangent.reshape(16, cells),
        dual_state.reshape(8, 2 * TILE),
        measured.reshape(8, 2 * TILE),
    )
    payload = pl.pallas_call(
        functools.partial(pack_kernel, quick),
        out_shape=jax.ShapeDtypeStruct((1, tiles // 2 + 2 + (5 if quick else tiles // 2), 16, TILE), BF16),
        in_specs=[hbm] * 4,
        out_specs=vmem,
        scratch_shapes=[pltpu.VMEM(value.shape, value.dtype) for value in raw]
        + [pltpu.SemaphoreType.DMA((4,))],
        compiler_params=pltpu.CompilerParams(vmem_limit_bytes=4 * MIB),
        name="pack",
    )(*(in_hbm(value) for value in raw))

    def swap(value, mask):
        return lax.ppermute(value, ALL_AXES, row_mask_pairs(devices, mask))

    table = (
        jnp.swapaxes(tile_rows, 2, 3),
        jnp.swapaxes(tile_blocks, 2, 3),
        dual_mixing.T,
        dual_readout,
    )
    own = own_weights(conv_first, conv_middle, conv_last)
    if quick:
        far_payload = swap(payload, 8)
        other = tuple(swap(value, 1) for value in own)
        payload, far_payload, other = lax.optimization_barrier((payload, far_payload, other))

        def bound_for(k):
            sources = (payload[0], far_payload[0])
            return jnp.concatenate(
                [source[:6] for source in sources]
                + [source[6 + k : 7 + k] for source in sources]
                + [source[10:] for source in sources],
                axis=0,
            )

        pieces = [swap(bound_for(k), 2 * k) for k in (1, 2, 3)]
        weights = build_weights(own, other, (footprints, *table))
        mine = bound_for(0)
        early = swap(mine[:12], 1)
        pieces[0], weights, early = lax.optimization_barrier((pieces[0], weights, early))
        late = swap(jnp.concatenate([piece[:12] for piece in pieces], axis=0), 1)
        pieces = [mine] + pieces
        payload = jnp.concatenate([piece[:12] for piece in pieces], axis=0)
        payload = payload.reshape(rows_count, 6, 16, TILE)
        routed = jnp.concatenate([piece[12:] for piece in pieces], axis=0)
        payload_other = early.reshape(2, 6, 16, TILE)
        payload_late = late.reshape(6, 6, 16, TILE)
    else:
        payload = lax.all_gather(payload, ALL_AXES, axis=0, tiled=True)
        payload = payload.reshape(rows_count, chans, *payload.shape[1:])
        payload, payload_other = (payload[:, 0], payload[:, 1])
        routed = payload[0, :1]
        payload_late = routed
        weights = build_weights(
            own, tuple(swap(value, 1) for value in own), (footprints, *table)
        )
    middle, first, last, footprints, *table = weights

    def piece_slot(owner, row):
        if not quick:
            return owner
        mask = owner ^ row
        return (mask & 3) * 2 + (mask >> 2)

    def update_row(owner, row):
        return owner ^ row if quick else owner

    def chunk_of(row, chan):
        return ((row & 3) if quick else row) * chans + chan

    def flip_of(chan):
        return chan if quick else 0

    updates = 4 if quick else rows_count
    count = rows_count * stride
    wide = HID * HID
    moved = 56 + 16 * updates
    pad = -(-(stride + 1) // TILE) * TILE
    limit = (24 if quick else 56) * MIB
    sizes = (rows_count, chans, detectors, tiles, width, stride, cells,
             (piece_slot, update_row, chunk_of, flip_of), updates,
             tile_rows.shape[1])
    outs = [
        ((moved, TILE), F32),
        ((moved, TILE), F32),
        ((8, 2 * TILE), F32),
    ]
    shared = [
        ((detectors, 16, TILE), F32),
        ((detectors, 16, TILE), F32),
        ((detectors, 16, TILE), F32),
        ((rows_count, 2, 16, TILE), BF16),
    ]
    scratch = [
        ((rows_count * tiles, 16, TILE), BF16),
        ((detectors, 16, TILE), BF16),
        ((detectors, 16, TILE), F32),
        ((rows_count, 3, 16, TILE), F32),
        ((48, count + pad), F32),
        ((2 * TAPS * HID, count), BF16),
        ((TAPS * HID, count), BF16),
        ((count + 2 * stride, 3 * wide), BF16),
        ((count + 2 * stride, 3 * wide), BF16),
        ((count, wide), F32),
        ((count, wide), F32),
        ((rows_count, 16, TILE), F32),
        ((4, HID, 8, TILE), F32),
    ]
    if quick:
        scratch = shared + scratch
    else:
        outs = outs + shared
    keep, send, new_dual, *rest = pl.pallas_call(
        functools.partial(main_kernel, sizes, quick),
        out_shape=[jax.ShapeDtypeStruct(*spec) for spec in outs],
        in_specs=[vmem] * 12,
        out_specs=[vmem] * len(outs),
        scratch_shapes=[pltpu.VMEM(*spec) for spec in scratch]
        + [pltpu.SMEM(value.shape, value.dtype) for value in table]
        + [pltpu.SemaphoreType.DMA((4,))]
        + [pltpu.VMEM((HID, detectors, 16, TILE), F32) for _ in range(2 if quick else 0)],
        compiler_params=pltpu.CompilerParams(vmem_limit_bytes=limit),
        cost_estimate=pl.CostEstimate(
            flops=5 * 10**9, bytes_accessed=5 * 10**6, transcendentals=2 * 10**6
        ),
        name="primal_dual",
    )(
        *table,
        payload,
        payload_other,
        payload_late,
        routed,
        middle,
        first,
        last,
        footprints,
    )

    near = swap(send, 1)
    scale = dual_readout.reshape(1, HID)
    grad_shapes = [
        jax.ShapeDtypeStruct(shape, F32)
        for shape in ((27, 8, HID), (27, 2, 8), (27, 1, 8), (3, HID), (1, HID))
    ]
    if quick:

        sums = keep[:56] + near[:56]

        def piece(value, index):
            return value[56 + 16 * index : 72 + 16 * index]

        parts = [
            swap(jnp.concatenate([sums, piece(keep, k), piece(near, k)], axis=0), 2 * k)
            for k in (1, 2, 3)
        ]
        new_volume, new_dual, *grads = pl.pallas_call(
            finish_kernel,
            out_shape=[
                jax.ShapeDtypeStruct((16, 8, TILE), F32),
                jax.ShapeDtypeStruct((8, 2 * TILE), F32),
            ]
            + grad_shapes,
            in_specs=[vmem] * 7,
            out_specs=[vmem] * 7,
            scratch_shapes=[pltpu.VMEM((8, 16, TILE), F32)],
            compiler_params=pltpu.CompilerParams(vmem_limit_bytes=8 * MIB),
            name="finish",
        )(scale, new_dual, keep, near, *parts)
    else:
        mine = keep + near
        small = pl.pallas_call(
            functools.partial(dual_gradients_kernel, sizes),
            out_shape=jax.ShapeDtypeStruct((8, TILE), F32),
            in_specs=[smem] * 4 + [vmem] * 5,
            out_specs=vmem,
            scratch_shapes=[
                pltpu.VMEM((detectors, 16, TILE), F32),
                pltpu.VMEM((4, HID, 8, TILE), F32),
            ],
            compiler_params=pltpu.CompilerParams(vmem_limit_bytes=limit),
            name="dual_gradients",
        )(*table, footprints, *rest)
        total = jnp.concatenate(
            [lax.psum(mine[:48], ROW_AXES), lax.psum(small, ALL_AXES)], axis=0
        )
        grads = pl.pallas_call(
            finish_grads_kernel,
            out_shape=grad_shapes,
            in_specs=[vmem, vmem],
            out_specs=[vmem] * 5,
            name="finish_grads",
        )(scale, total)
        pieces = lax.all_to_all(
            mine[56:].reshape(rows_count, 16, TILE), ROW_AXES, 0, 0, tiled=True
        )
        pieces = pieces.reshape(tiles, rows_count // tiles, 16, TILE).sum(axis=1)
        new_volume = jnp.swapaxes(pieces, 0, 1)

    grad_middle, grad_first, grad_last, grad_mixing, grad_readout = grads
    return (
        new_volume.reshape(volume.shape),
        new_dual.reshape(dual_state.shape),
        grad_first.reshape(3, 3, 3, 2, 8).transpose(4, 3, 0, 1, 2),
        grad_middle.reshape(3, 3, 3, 8, HID).transpose(3, 4, 0, 1, 2),
        grad_last.reshape(3, 3, 3, 1, 8).transpose(3, 4, 0, 1, 2),
        grad_mixing.T,
        grad_readout.reshape(HID),
    )


def solution(mesh):
    placed = (
        P("grp", ("view", "slab"), None),
        P(("grp", "view"), "chan", "slab"),
        P(("grp", "view"), "chan", "slab"),
        P("grp", ("view", "slab"), None),
        P("chan", None, None, None, None),
        P("chan", None, None, None, None),
        P(None, "chan", None, None, None),
        P(),
        P(),
        P(),
        P(),
        P(),
    )
    return jax.shard_map(
        body,
        mesh=mesh,
        in_specs=placed,
        out_specs=(
            P("grp", ("view", "slab"), None),
            P(("grp", "view"), "chan", "slab"),
            P(("grp", "chan"), None, None, None, None),
            P(("grp", "chan"), None, None, None, None),
            P("grp", "chan", None, None, None),
            P("grp", None),
            P("grp"),
        ),
        check_vma=False,
    )
```
